256 devices in a mesh: row: 8 (over x_hi, y), col: 32 (over z, x_lo, core).
Axes of the slice: x: 4 (x_hi: 2, x_lo: 2; x = x_hi * 2 + x_lo), y: 4, z: 8, core: 2. Of those that a mesh axis runs over, the one named last changes fastest.
Arguments:
- object_field: float32 [2, 2048, 16384], P(None, 'row', 'col'), may hold values from -6 to 6
- probe: float32 [2, 256, 256], replicated, may hold values from -6 to 6
- measured: float32 [8, 32, 4, 256, 256], P('row', 'col'), may hold values from 0.5 to 4
- positions: int32 [8, 32, 4, 2], P('row', 'col'), may hold values from -128 to 16256, as said below
- counts: int32 [8, 32], P('row', 'col'), may hold values from 2 to 4, as said below
Outputs:
- object_new: float32 [2, 2048, 16384], P(None, 'row', 'col')
- probe_new: float32 [2, 256, 256], replicated
The draws below stay inside these ranges and needn't reach their ends.
Inputs may be any that keep to these rules, and one draw needn't show every extreme that they name: `positions`: for the tile (r, c) every slot's patch starts at row r * 256 - 128 + a and column c * 512 - 128 + b with 0 <= a <= 256 and 0 <= b <= 512, also for slots that are not live. Slots from index counts[r, c] on hold no live pattern; some tile is full.
All inputs are finite; a program needn't handle non-finite values.
Results may differ from the reference program's by a relative error of at most 0.00088.
The reference program's roundings to bfloat16 on the way count: a program that leaves them out, or rounds other values in their place, can miss the bound.
Values sent between devices are 32-bit elements; how exact they have to be, the bound alone decides.
A program may use at most 128 MiB of HBM per device.

```python
import math
import jax
import jax.numpy as jnp
from jax import lax

N = 256
HALF = 128
TH = 256
TW = 512
PAT_DEV = 4
OH = 2048
OW = 16384
N_ROW = 8
N_COL = 32


def draw_positions(key, part):
    key = jax.random.fold_in(key, 7)
    rows_n = OH // TH
    cols_n = OW // TW
    first_key, second_key = jax.random.split(key)
    row_offset = jax.random.randint(first_key, (rows_n, cols_n, PAT_DEV), 0, TH + 1)
    col_offset = jax.random.randint(second_key, (rows_n, cols_n, PAT_DEV), 0, TW + 1)
    row_offset = row_offset.at[0, 0, 0].set(0).at[rows_n - 1, cols_n - 1, 0].set(TH)
    col_offset = col_offset.at[0, 0, 0].set(0).at[rows_n - 1, cols_n - 1, 0].set(TW)
    row_offset = row_offset + (jnp.arange(rows_n, dtype=jnp.int32) * TH - HALF)[:, None, None]
    col_offset = col_offset + (jnp.arange(cols_n, dtype=jnp.int32) * TW - HALF)[None, :, None]
    return jnp.stack([row_offset, col_offset], axis=-1).astype(jnp.int32)


def draw_counts(key, part):
    key = jax.random.fold_in(key, 9)
    rows_n = OH // TH
    cols_n = OW // TW
    drawn = jax.random.randint(key, (rows_n, cols_n), (PAT_DEV + 1) // 2, PAT_DEV + 1)
    return drawn.at[0, 0].set(PAT_DEV).astype(jnp.int32)


def block_levels(key, shape, cuts, low, top_value):
    def one(axis_at, shards_of):
        draws = jax.random.uniform(jax.random.fold_in(jax.random.fold_in(key, 6), axis_at), (shards_of,), jnp.float32, low / len(cuts), top_value / len(cuts))
        return jnp.repeat(jnp.exp(draws), shape[axis_at] // shards_of).reshape((-1,) + (1,) * (len(shape) - axis_at - 1))

    gain = one(*cuts[0])
    for cut in cuts[1:]:
        gain = gain * one(*cut)
    return gain


def gaussian(key, shape, width, most, cuts=(), kind=jnp.bfloat16):
    factor_of = block_levels(key, shape, cuts, -0.22, 0.18) if cuts else 1.0
    entries = jax.random.normal(key, shape, jnp.float32) * width * factor_of
    return jnp.minimum(jnp.maximum(entries, -most), most).astype(kind)


def setup_inputs(seed: int = 0) -> dict:
    key_of = jax.random.split(jax.random.key(seed), 6)
    return {
        "object_field": gaussian(key_of[0], (2, OH, OW), 1.0, 6.0, ((1, 8), (2, 32)), jnp.float32),
        "probe": gaussian(key_of[1], (2, N, N), 1.0, 6.0, (), jnp.float32),
        "measured": jnp.clip(jnp.exp(math.log(4.0) - 2.0794415 * jax.random.uniform(key_of[2], (N_ROW, N_COL, PAT_DEV, N, N), jnp.float32) ** block_levels(key_of[2], (N_ROW, N_COL, PAT_DEV, N, N), ((0, 8), (1, 32)), -0.2, 0.2)), 0.5, 4.0),
        "positions": draw_positions(jax.random.fold_in(key_of[5], 71), 0),
        "counts": draw_counts(jax.random.fold_in(key_of[5], 71), 0),
    }


def tables(extent):
    indices = jnp.arange(extent, dtype=jnp.int32)
    products = indices[:, None] * indices[None, :] % extent
    angles = 2.0 * jnp.pi / extent * products.astype(jnp.float32)
    cosine = jnp.cos(angles) / jnp.sqrt(jnp.float32(extent))
    sine_part = jnp.sin(angles) / jnp.sqrt(jnp.float32(extent))
    forward = jnp.block([[cosine, -sine_part], [sine_part, cosine]]).astype(jnp.bfloat16)
    inverse = jnp.block([[cosine, sine_part], [-sine_part, cosine]]).astype(jnp.bfloat16)
    return (forward, inverse)

def product(blocks, table):
    batch_n, side_n, wide_n = blocks.shape
    flattened = blocks.reshape(batch_n * side_n, wide_n)
    return jnp.dot(flattened, table, preferred_element_type=jnp.float32).reshape(batch_n, side_n, wide_n)

def turn_planes(blocks, extent):
    batch_n = blocks.shape[0]
    return blocks.reshape(batch_n, extent, 2, extent).transpose(0, 3, 2, 1).reshape(batch_n, extent, 2 * extent)

def diffract(patches, probe, amplitudes, live_mask):
    extent = probe.shape[1]
    probe_re, probe_im = (probe[0], probe[1])
    patch_re, patch_im = (patches[:, 0], patches[:, 1])
    exit_wave = jnp.concatenate([probe_re * patch_re - probe_im * patch_im, probe_re * patch_im + probe_im * patch_re], axis=-1).astype(jnp.bfloat16)
    forward, inverse = tables(extent)
    half_done = turn_planes(product(exit_wave, forward).astype(jnp.bfloat16), extent)
    spectrum = product(half_done, forward)
    spec_re, spec_im = (spectrum[..., :extent], spectrum[..., extent:])
    magnitude = jnp.sqrt(spec_re * spec_re + spec_im * spec_im + 0.25)
    factor = live_mask[:, None, None] * (1.0 - amplitudes / magnitude)
    residue = jnp.concatenate([factor * spec_re, factor * spec_im], axis=-1).astype(jnp.bfloat16)
    back_half = turn_planes(product(residue, inverse).astype(jnp.bfloat16), extent)
    update = product(back_half, inverse)
    update_re, update_im = (update[..., :extent], update[..., extent:])
    obj_terms = jnp.stack([probe_re * update_re + probe_im * update_im, probe_re * update_im - probe_im * update_re], axis=1)
    probe_terms = jnp.stack([lax.optimization_barrier(jnp.sum(patch_re * update_re + patch_im * update_im, axis=0)), lax.optimization_barrier(jnp.sum(patch_re * update_im - patch_im * update_re, axis=0)), lax.optimization_barrier(jnp.sum(live_mask[:, None, None] * (patch_re * patch_re + patch_im * patch_im), axis=0))])
    return (obj_terms, probe_terms)

def place_terms(canvas, term_set, corners):
    zero_index = jnp.zeros((), jnp.int32)

    def add_one(number, current):
        corner_at = (zero_index, corners[number, 0].astype(jnp.int32), corners[number, 1].astype(jnp.int32))
        section = lax.dynamic_slice(current, corner_at, term_set.shape[1:]) + term_set[number]
        return lax.dynamic_update_slice(current, section, corner_at)
    return lax.fori_loop(0, term_set.shape[0], add_one, canvas)

def reference(object_field, probe, measured, positions, counts):
    extent = N
    half_w = extent // 2
    zero_index = jnp.zeros((), jnp.int32)
    padded = jnp.pad(object_field, ((0, 0), (half_w, half_w), (half_w, half_w)))
    spot_lists = (positions.reshape(-1, PAT_DEV, 2) + half_w).astype(jnp.int32)
    measures = measured.reshape(-1, PAT_DEV, extent, extent)
    live_counts = counts.reshape(-1)
    probe_power = probe[0] * probe[0] + probe[1] * probe[1]

    def visit(carry, inputs):
        canvas, probe_total = carry
        spot_list, amplitudes, live_count = inputs
        live_mask = (jnp.arange(PAT_DEV, dtype=jnp.int32) < live_count).astype(jnp.float32)
        patches = jax.vmap(lambda corner: lax.dynamic_slice(padded, (zero_index, corner[0], corner[1]), (2, extent, extent)))(spot_list)
        obj_terms, probe_terms = diffract(patches, probe, amplitudes, live_mask)
        lit = (live_mask[:, None, None] * probe_power[None])[:, None]
        term_set = jnp.concatenate([obj_terms, lit], axis=1)
        canvas = place_terms(canvas, term_set, spot_list)
        return ((canvas, probe_total + probe_terms), None)
    canvas_start = jnp.zeros((3, OH + 2 * half_w, OW + 2 * half_w), jnp.float32)
    total_start = jnp.zeros((3, extent, extent), jnp.float32)
    (canvas, probe_total), _ = lax.scan(visit, (canvas_start, total_start), (spot_lists, measures, live_counts))
    gradients = canvas[:, half_w:half_w + OH, half_w:half_w + OW]
    illum = gradients[2]
    peak_illum = jnp.max(illum)
    object_new = object_field - gradients[:2] / (0.75 * illum + 0.25 * peak_illum)
    weight = probe_total[2]
    probe_new = probe - probe_total[:2] / (0.75 * weight + 0.25 * jnp.max(weight))
    return (object_new, probe_new)
```

```python
import functools

import jax
import jax.numpy as jnp
import ml_dtypes
import numpy as np
from jax import lax
from jax.experimental import pallas as pl
from jax.experimental.pallas import tpu as pltpu
from jax.sharding import PartitionSpec as P

N = 256
HALF = 128
TH = 256
TW = 512
PAT = 4
CORES = 2
XS = 4
ZS = 8
YS = 4
CHUNK = 24
TILE = 8
DIRS = [(-1, 0), (1, 0), (0, -1), (0, 1), (-1, -1), (-1, 1), (1, -1), (1, 1)]
MESH = pl.DeviceIdType.MESH


def tables(extent):
    indices = np.arange(extent, dtype=np.int32)
    products = indices[:, None] * indices[None, :] % extent
    angles = 2.0 * np.pi / extent * products.astype(np.float64)
    cosine = np.cos(angles) / np.sqrt(float(extent))
    sine_part = np.sin(angles) / np.sqrt(float(extent))
    forward = np.block([[cosine, -sine_part], [sine_part, cosine]])
    inverse = np.block([[cosine, sine_part], [-sine_part, cosine]])
    return (
        forward.astype(np.float32).astype(ml_dtypes.bfloat16),
        inverse.astype(np.float32).astype(ml_dtypes.bfloat16),
    )


def span(step, size, middle):
    if step == 0:
        return pl.ds(HALF if middle else 0, size)
    if middle:
        return pl.ds(0 if step < 0 else size + HALF, HALF)
    return pl.ds(0 if step < 0 else size - HALF, HALF)


def landing(step, size):
    if step == 0:
        return pl.ds(HALF, size)
    return pl.ds(0 if step > 0 else size + HALF, HALF)


def kernel(
    pos,
    cnt,
    obj,
    probe_in,
    meas_in,
    fwd_in,
    inv_in,
    obj_out,
    probe_out,
    framed,
    probe,
    meas,
    meas_t,
    fwd,
    inv,
    padded,
    canvas,
    rx_v,
    rx_h,
    rx_c,
    patches,
    wave,
    exits,
    halves,
    residues,
    backs,
    s1,
    rx1,
    s2,
    rx2,
    s3,
    rx3,
    rx4,
    gathered,
    obj_new,
    probe_new,
    local_sem,
    halo_send,
    halo_recv,
    ill_send,
    ill_recv,
    grad_send,
    grad_recv,
    red_send,
    red_recv,
    out_sem,
):
    row = lax.axis_index("row")
    col = lax.axis_index("col")
    core = lax.rem(col, CORES)
    x_at = (row // YS) * 2 + lax.rem(col // 2, 2)
    z_at = col // 4
    y_at = lax.rem(row, YS)

    def core_peer():
        return (row, col + 1 - 2 * core)

    def x_peer(i):
        return ((i // 2) * YS + y_at, z_at * 4 + lax.rem(i, 2) * 2 + core)

    def z_peer(i):
        return (row, i * 4 + lax.rem(col, 4))

    def y_peer(i):
        return ((row // YS) * YS + i, col)

    def exists(step):
        near_row, near_col = row + step[0], col + step[1]
        conds = []
        if step[0] < 0:
            conds.append(near_row >= 0)
        if step[0] > 0:
            conds.append(near_row < lax.axis_size("row"))
        if step[1] < 0:
            conds.append(near_col >= 0)
        if step[1] > 0:
            conds.append(near_col < lax.axis_size("col"))
        return functools.reduce(jnp.logical_and, conds)

    center = (slice(None), pl.ds(HALF, TH), pl.ds(HALF, TW))
    local = [
        pltpu.make_async_copy(probe_in, probe, local_sem.at[0]),
        pltpu.make_async_copy(meas_in, meas, local_sem.at[1]),
        pltpu.make_async_copy(fwd_in, fwd, local_sem.at[2]),
        pltpu.make_async_copy(inv_in, inv, local_sem.at[3]),
        pltpu.make_async_copy(obj, framed.at[center], local_sem.at[4]),
    ]

    barrier = pltpu.get_barrier_semaphore()
    greeted = jnp.int32(0)
    for step in DIRS:
        there = exists(step)

        @pl.when(there)
        def _():
            pl.semaphore_signal(
                barrier, inc=1, device_id=(row + step[0], col + step[1]), device_id_type=MESH
            )

        greeted = greeted + there.astype(jnp.int32)
    pl.semaphore_signal(barrier, inc=1, device_id=core_peer(), device_id_type=MESH)
    for d in range(1, XS):
        pl.semaphore_signal(
            barrier, inc=1, device_id=x_peer(lax.rem(x_at + d, XS)), device_id_type=MESH
        )
    for d in range(1, ZS):
        pl.semaphore_signal(
            barrier, inc=1, device_id=z_peer(lax.rem(z_at + d, ZS)), device_id_type=MESH
        )
    for d in range(1, YS):
        pl.semaphore_signal(
            barrier, inc=1, device_id=y_peer(lax.rem(y_at + d, YS)), device_id_type=MESH
        )
    for copy in local:
        copy.start()
    pl.semaphore_wait(barrier, greeted + (CORES - 1 + XS - 1 + ZS - 1 + YS - 1))

    def halo_copy(n):
        dr, dc = DIRS[n]
        return pltpu.make_async_remote_copy(
            src_ref=obj.at[:, span(dr, TH, False), span(dc, TW, False)],
            dst_ref=framed.at[:, landing(dr, TH), landing(dc, TW)],
            send_sem=halo_send.at[n],
            recv_sem=halo_recv.at[n],
            device_id=(row + dr, col + dc),
            device_id_type=MESH,
        )

    def rx_of(n, planes):
        dr, dc = DIRS[n]
        if dc == 0:
            return rx_v.at[(dr + 1) // 2, planes]
        if dr == 0:
            return rx_h.at[(dc + 1) // 2, planes]
        return rx_c.at[(dr + 1) // 2, (dc + 1) // 2, planes]

    def term_copy(n, planes, send, recv):
        dr, dc = DIRS[n]
        return pltpu.make_async_remote_copy(
            src_ref=canvas.at[planes, span(dr, TH, True), span(dc, TW, True)],
            dst_ref=rx_of(n, planes),
            send_sem=send.at[n],
            recv_sem=recv.at[n],
            device_id=(row + dr, col + dc),
            device_id_type=MESH,
        )

    def ill_copy(n):
        return term_copy(n, pl.ds(2, 1), ill_send, ill_recv)

    def grad_copy(n):
        return term_copy(n, pl.ds(0, 2), grad_send, grad_recv)

    def for_each(make, order, act):
        for n in order:

            @pl.when(exists(DIRS[n]))
            def _():
                act(make(n))

    def opposite(n):
        return DIRS.index((-DIRS[n][0], -DIRS[n][1]))

    everywhere = range(len(DIRS))
    for_each(halo_copy, everywhere, lambda c: c.start())

    for n in everywhere:
        dr, dc = DIRS[n]
        opp = opposite(n)

        @pl.when(jnp.logical_not(exists(DIRS[n])))
        def _():
            rows, cols = landing(-dr, TH), landing(-dc, TW)
            framed[:, rows, cols] = jnp.zeros((2, rows.size, cols.size), jnp.float32)
            target = rx_of(opp, pl.ds(0, 3))
            target[...] = jnp.zeros(target.shape, jnp.float32)

    framed[:, TH + 2 * HALF :, :] = jnp.zeros((2, TILE, TW + 3 * HALF), jnp.float32)
    framed[:, : TH + 2 * HALF, TW + 2 * HALF :] = jnp.zeros(
        (2, TH + 2 * HALF, HALF), jnp.float32
    )

    def clear(i, carry):
        at = pl.ds(pl.multiple_of(i * 32, 32), 32)
        for k in range(PAT):
            for p in range(2):
                padded[k, p, at, :] = jnp.zeros((32, 640), jnp.float32)
        return carry

    lax.fori_loop(0, 24, clear, 0)

    count = cnt[0, 0]
    lives, tops, lefts, downs, overs = [], [], [], [], []
    for k in range(PAT):
        a = lax.max(lax.min(pos[k, 0] - (row * TH - HALF), TH), 0)
        b = lax.max(lax.min(pos[k, 1] - (col * TW - HALF), TW), 0)
        lives.append(jnp.where(k < count, 1.0, 0.0).astype(jnp.float32))
        tops.append(lax.div(a, TILE))
        downs.append(lax.rem(a, TILE))
        lefts.append(lax.div(b, 128))
        overs.append(lax.rem(b, 128))

    def lane_iota(shape):
        return lax.broadcasted_iota(jnp.int32, shape, len(shape) - 1)

    def sub_iota(shape):
        return lax.broadcasted_iota(jnp.int32, shape, len(shape) - 2)

    def window(p, k, first, tiles):
        s, r = downs[k], overs[k]
        rows = pl.ds((tops[k] + first) * TILE, (tiles + 1) * TILE)
        turned = []
        for j in range(3):
            cols = pl.ds((lefts[k] + j) * 128, 128)
            turned.append(pltpu.roll(framed[p, rows, cols], lax.rem(128 - r, 128), 1))
        near = lane_iota(turned[0].shape) < 128 - r
        found = []
        for j in range(2):
            both = jnp.where(near, turned[j], turned[j + 1]).reshape(tiles + 1, TILE, 128)
            both = pltpu.roll(both, lax.rem(TILE - s, TILE), 1)
            upper = sub_iota((tiles, TILE, 128)) < TILE - s
            found.append(
                jnp.where(upper, both[:tiles], both[1:]).reshape(tiles * TILE, 128)
            )
        return found

    def lay(k, p, tiles):
        s, r = downs[k], overs[k]
        moved = []
        for x in tiles:
            x = pltpu.roll(x.reshape(N // TILE, TILE, 128), s, 1)
            none = jnp.zeros((1, TILE, 128), jnp.float32)
            here = jnp.concatenate([x, none], axis=0)
            above = jnp.concatenate([none, x], axis=0)
            y = jnp.where(sub_iota(here.shape) >= s, here, above).reshape(N + TILE, 128)
            moved.append(pltpu.roll(y, r, 1))
        right = lane_iota((N + TILE, 128)) >= r
        rows = pl.ds(N, N + TILE)
        padded[k, p, rows, pl.ds(128, 128)] = jnp.where(right, moved[0], 0.0)
        padded[k, p, rows, pl.ds(256, 128)] = jnp.where(right, moved[1], moved[0])
        padded[k, p, rows, pl.ds(384, 128)] = jnp.where(right, 0.0, moved[1])

    def collect(start, stop, pairs):
        size = 8

        def one(i, carry):
            first = i * size
            rows = pl.ds(pl.multiple_of(first * TILE, size * TILE), size * TILE)
            for q, p in pairs:
                for j in range(6):
                    total = None
                    for k in range(PAT):
                        at = (first - tops[k] + N // TILE) * TILE
                        lane = lax.max(lax.min(j - lefts[k] + 1, 4), 0) * 128
                        part = padded[
                            k, p, pl.ds(at, size * TILE), pl.ds(lane, 128)
                        ]
                        total = part if total is None else total + part
                    canvas[q, rows, pl.ds(j * 128, 128)] = total
            return carry

        lax.fori_loop(start // size, stop // size, one, 0)

    local[0].wait()
    power = [
        probe[0, :, pl.ds(128 * j, 128)] * probe[0, :, pl.ds(128 * j, 128)]
        + probe[1, :, pl.ds(128 * j, 128)] * probe[1, :, pl.ds(128 * j, 128)]
        for j in range(2)
    ]
    for k in range(PAT):
        lay(k, 0, [lives[k] * x for x in power])
    collect(0, 64, [(2, 0)])
    local[1].wait()
    for k in range(PAT):
        meas_t[k] = meas[k].T
    for copy in local[2:]:
        copy.wait()

    for_each(halo_copy, everywhere, lambda c: c.wait_send())
    for n in everywhere:

        @pl.when(exists(DIRS[opposite(n)]))
        def _():
            halo_copy(n).wait_recv()

    for_each(ill_copy, everywhere, lambda c: c.start())

    def cut(i, carry):
        tiles = 4
        rows = pl.ds(pl.multiple_of(i * tiles * TILE, tiles * TILE), tiles * TILE)
        weight = [jnp.zeros((tiles * TILE, 128), jnp.float32)] * 2
        for k in range(PAT):
            real = window(0, k, i * tiles, tiles)
            imag = window(1, k, i * tiles, tiles)
            for j in range(2):
                cols = pl.ds(128 * j, 128)
                p_re, p_im = probe[0, rows, cols], probe[1, rows, cols]
                patches[k, 0, rows, cols] = real[j]
                patches[k, 1, rows, cols] = imag[j]
                exits[k, rows, cols] = (p_re * real[j] - p_im * imag[j]).astype(jnp.bfloat16)
                exits[k, rows, pl.ds(N + 128 * j, 128)] = (
                    p_re * imag[j] + p_im * real[j]
                ).astype(jnp.bfloat16)
                weight[j] = weight[j] + lives[k] * (real[j] * real[j] + imag[j] * imag[j])
        for j in range(2):
            s1[1, pl.ds(pl.multiple_of((1 + j) * N + i * tiles * TILE, 8), tiles * TILE), :] = (
                weight[j]
            )
        return carry

    lax.fori_loop(0, 8, cut, 0)

    def dot(a, b):
        return jnp.dot(a, b, preferred_element_type=jnp.float32)

    for k in range(PAT):
        half = dot(exits[k], fwd[...]).astype(jnp.bfloat16)
        halves[k, :N, :] = half[:, :N]
        halves[k, N:, :] = half[:, N:]
        spectrum = dot(inv[...], halves[k])
        re, im = spectrum[:N], spectrum[N:]
        factor = lives[k] * (1.0 - meas_t[k] * lax.rsqrt(re * re + im * im + 0.25))
        residues[k, :N, :] = (factor * re).astype(jnp.bfloat16)
        residues[k, N:, :] = (factor * im).astype(jnp.bfloat16)
        back = dot(fwd[...], residues[k]).astype(jnp.bfloat16)
        backs[k, :, :N] = back[:N]
        backs[k, :, N:] = back[N:]
        wave[k] = dot(backs[k], inv[...])

    def probe_sum(i, carry):
        size = 32
        at = pl.multiple_of(i * size, size)
        rows = pl.ds(at, size)
        for j in range(2):
            cols = pl.ds(128 * j, 128)
            real = imag = None
            for k in range(PAT):
                a, b = patches[k, 0, rows, cols], patches[k, 1, rows, cols]
                u, v = wave[k, rows, cols], wave[k, rows, pl.ds(N + 128 * j, 128)]
                one, two = a * u + b * v, a * v - b * u
                real = one if real is None else real + one
                imag = two if imag is None else imag + two
            s1[0, pl.ds(pl.multiple_of(j * N + at, 8), size), :] = real
            if j == 0:
                s1[0, pl.ds(pl.multiple_of(2 * N + at, 8), size), :] = imag
            else:
                s1[1, pl.ds(at, size), :] = imag
        return carry

    lax.fori_loop(0, N // 32, probe_sum, 0)

    for_each(ill_copy, everywhere, lambda c: c.wait_send())
    for n in everywhere:

        @pl.when(exists(DIRS[opposite(n)]))
        def _():
            ill_copy(n).wait_recv()

    def owned(p, rows, at, h, j):
        size = rows.size
        value = canvas[p, pl.ds(pl.multiple_of(HALF + h * HALF + at, 8), size), pl.ds(128 * (j + 1), 128)]
        near = pl.ds(at, size)
        value = value + rx_v[1 - h, p, near, pl.ds(128 * j, 128)]
        if j in (0, 3):
            side = 1 if j == 0 else 0
            value = value + rx_h[side, p, rows, :]
            value = value + rx_c[1 - h, side, p, near, :]
        return value

    size = 32
    peak = jnp.zeros((TILE, 128), jnp.float32)
    for h in range(2):

        def largest(i, most, h=h):
            at = pl.multiple_of(i * size, size)
            rows = pl.ds(pl.multiple_of(h * HALF + at, size), size)
            for j in range(4):
                value = owned(2, rows, at, h, j)
                canvas[2, pl.ds(pl.multiple_of(HALF + h * HALF + at, 8), size), pl.ds(128 * (j + 1), 128)] = value
                most = jnp.maximum(most, jnp.max(value.reshape(size // TILE, TILE, 128), axis=0))
            return most

        peak = lax.fori_loop(0, HALF // size, largest, peak)
    for c in range(CORES):
        s1[c, 3 * N :, :] = peak

    def send(src, dst, sem, peer):
        return pltpu.make_async_remote_copy(
            src_ref=src,
            dst_ref=dst,
            send_sem=red_send.at[sem],
            recv_sem=red_recv.at[sem],
            device_id=peer,
            device_id_type=MESH,
        )

    other = 1 - core
    first = send(s1.at[other], rx1, 0, core_peer())
    first.start()

    for k in range(PAT):
        parts = ([], [])
        for j in range(2):
            cols = pl.ds(128 * j, 128)
            u, v = wave[k, :, cols], wave[k, :, pl.ds(N + 128 * j, 128)]
            p_re, p_im = probe[0, :, cols], probe[1, :, cols]
            parts[0].append(p_re * u + p_im * v)
            parts[1].append(p_re * v - p_im * u)
        for p in range(2):
            lay(k, p, parts[p])

    both = [(0, 0), (1, 1)]
    collect(0, 16, both)
    for_each(grad_copy, [0, 4, 5], lambda c: c.start())
    collect(48, 64, both)
    for_each(grad_copy, [1, 6, 7], lambda c: c.start())
    collect(16, 48, both)
    for_each(grad_copy, [2, 3], lambda c: c.start())

    first.wait()
    part = 3 * N // XS
    for i in range(XS):
        at = pl.ds(i * part, part)
        s2[i, :part, :] = s1[core, at, :] + rx1[at, :]
    crown = jnp.maximum(s1[core, 3 * N :, :], rx1[3 * N :, :])
    for i in range(XS):
        s2[i, part:, :] = crown

    def x_copy(d):
        to = lax.rem(x_at + d, XS)
        return send(s2.at[to], rx2.at[d - 1], d, x_peer(to))

    for d in range(1, XS):
        x_copy(d).start()
    for d in range(1, XS):
        x_copy(d).wait()
    crown = s2[x_at, part:, :]
    for d in range(XS - 1):
        crown = jnp.maximum(crown, rx2[d, part:, :])
    for i in range(ZS):
        at = pl.ds(i * CHUNK, CHUNK)
        s3[i, :CHUNK, :] = (s2[x_at, at, :] + rx2[0, at, :]) + (rx2[1, at, :] + rx2[2, at, :])
        s3[i, CHUNK:, :] = crown

    def z_copy(d):
        to = lax.rem(z_at + d, ZS)
        return send(s3.at[to], rx3.at[d - 1], XS + d - 1, z_peer(to))

    for d in range(1, ZS):
        z_copy(d).start()
    for d in range(1, ZS):
        z_copy(d).wait()
    total = s3[z_at, :CHUNK, :]
    crown = s3[z_at, CHUNK:, :]
    for d in range(ZS - 1):
        total = total + rx3[d, :CHUNK, :]
        crown = jnp.maximum(crown, rx3[d, CHUNK:, :])
    rx4[y_at, :CHUNK, :] = total
    rx4[y_at, CHUNK:, :] = crown

    def y_copy(d):
        to = lax.rem(y_at + d, YS)
        return send(rx4.at[y_at], rx4.at[y_at], XS + ZS + d - 2, y_peer(to))

    for d in range(1, YS):
        y_copy(d).start()
    for d in range(1, YS):
        y_copy(d).wait()
    total = (rx4[0, :CHUNK, :] + rx4[1, :CHUNK, :]) + (rx4[2, :CHUNK, :] + rx4[3, :CHUNK, :])
    crown = jnp.maximum(
        jnp.maximum(rx4[0, CHUNK:, :], rx4[1, CHUNK:, :]),
        jnp.maximum(rx4[2, CHUNK:, :], rx4[3, CHUNK:, :]),
    )
    gathered[core, x_at, z_at] = total

    base = XS + ZS + YS - 2

    def z_back(d):
        to = lax.rem(z_at + d, ZS)
        mine = gathered.at[core, x_at, z_at]
        return send(mine, mine, base + d - 1, z_peer(to))

    def x_back(d):
        to = lax.rem(x_at + d, XS)
        mine = gathered.at[core, x_at]
        return send(mine, mine, base + ZS - 1 + d - 1, x_peer(to))

    for d in range(1, ZS):
        z_back(d).start()
    for d in range(1, ZS):
        z_back(d).wait()
    for d in range(1, XS):
        x_back(d).start()

    for_each(grad_copy, everywhere, lambda c: c.wait_send())
    for n in everywhere:

        @pl.when(exists(DIRS[opposite(n)]))
        def _():
            grad_copy(n).wait_recv()

    top = jnp.max(crown)
    for h in range(2):

        def renew(i, carry, h=h):
            at = pl.multiple_of(i * size, size)
            rows = pl.ds(pl.multiple_of(h * HALF + at, size), size)
            inner = pl.ds(pl.multiple_of(HALF + h * HALF + at, 8), size)
            for j in range(4):
                cols = pl.ds(128 * (j + 1), 128)
                share = 1.0 / (0.75 * canvas[2, inner, cols] + 0.25 * top)
                for p in range(2):
                    obj_new[p, rows, pl.ds(128 * j, 128)] = (
                        framed[p, inner, cols] - owned(p, rows, at, h, j) * share
                    )
            return carry

        lax.fori_loop(0, HALF // size, renew, 0)
    obj_store = pltpu.make_async_copy(obj_new, obj_out, out_sem.at[0])
    obj_store.start()

    for d in range(1, XS):
        x_back(d).wait()
    mine = gathered.at[core]
    last = send(mine, mine, base + ZS + XS - 2, core_peer())
    last.start()
    last.wait()

    flat = XS * ZS * CHUNK

    def sums(p, j):
        n = p * 2 + j
        steps = N // 8
        lines = []
        start = (n % 3) * N
        for c in range(start // CHUNK, -(-(start + N) // CHUNK)):
            lo = max(start, c * CHUNK) - c * CHUNK
            hi = min(start + N, (c + 1) * CHUNK) - c * CHUNK
            lines.append(gathered[n // 3, c // ZS, c % ZS, pl.ds(lo, hi - lo), :])
        return jnp.concatenate(lines, axis=0)

    weight = [sums(2, j) for j in range(2)]
    heavy = jnp.maximum(jnp.max(weight[0]), jnp.max(weight[1]))
    for j in range(2):
        cols = pl.ds(128 * j, 128)
        share = 1.0 / (0.75 * weight[j] + 0.25 * heavy)
        for p in range(2):
            probe_new[p, :, cols] = probe[p, :, cols] - sums(p, j) * share
    probe_store = pltpu.make_async_copy(probe_new, probe_out, out_sem.at[1])
    probe_store.start()
    probe_store.wait()
    obj_store.wait()


def body(object_field, probe, measured, positions, counts):
    forward, inverse = tables(N)
    any_space = pl.BlockSpec(memory_space=pl.ANY)
    smem = pl.BlockSpec(memory_space=pltpu.SMEM)
    f32 = jnp.float32
    bf16 = jnp.bfloat16
    red = 1 + (XS - 1) * 2 + (ZS - 1) * 2 + (YS - 1) + 1
    dma = pltpu.SemaphoreType.DMA
    return pl.pallas_call(
        kernel,
        out_shape=(
            jax.ShapeDtypeStruct((2, TH, TW), f32),
            jax.ShapeDtypeStruct((2, N, N), f32),
        ),
        in_specs=[smem, smem] + [any_space] * 5,
        out_specs=(any_space, any_space),
        scratch_shapes=[
            pltpu.VMEM((2, TH + 2 * HALF + TILE, TW + 3 * HALF), f32),
            pltpu.VMEM((2, N, N), f32),
            pltpu.VMEM((PAT, N, N), f32),
            pltpu.VMEM((PAT, N, N), f32),
            pltpu.VMEM((2 * N, 2 * N), bf16),
            pltpu.VMEM((2 * N, 2 * N), bf16),
            pltpu.VMEM((PAT, 2, 3 * N, 640), f32),
            pltpu.VMEM((3, TH + 2 * HALF, TW + 2 * HALF), f32),
            pltpu.VMEM((2, 3, HALF, TW), f32),
            pltpu.VMEM((2, 3, TH, HALF), f32),
            pltpu.VMEM((2, 2, 3, HALF, HALF), f32),
            pltpu.VMEM((PAT, 2, N, N), f32),
            pltpu.VMEM((PAT, N, 2 * N), f32),
            pltpu.VMEM((PAT, N, 2 * N), bf16),
            pltpu.VMEM((PAT, 2 * N, N), bf16),
            pltpu.VMEM((PAT, 2 * N, N), bf16),
            pltpu.VMEM((PAT, N, 2 * N), bf16),
            pltpu.VMEM((CORES, 3 * N + TILE, 128), f32),
            pltpu.VMEM((3 * N + TILE, 128), f32),
            pltpu.VMEM((XS, 3 * N // XS + TILE, 128), f32),
            pltpu.VMEM((XS - 1, 3 * N // XS + TILE, 128), f32),
            pltpu.VMEM((ZS, CHUNK + TILE, 128), f32),
            pltpu.VMEM((ZS - 1, CHUNK + TILE, 128), f32),
            pltpu.VMEM((YS, CHUNK + TILE, 128), f32),
            pltpu.VMEM((CORES, XS, ZS, CHUNK, 128), f32),
            pltpu.VMEM((2, TH, TW), f32),
            pltpu.VMEM((2, N, N), f32),
            dma((5,)),
            dma((8,)),
            dma((8,)),
            dma((8,)),
            dma((8,)),
            dma((8,)),
            dma((8,)),
            dma((red,)),
            dma((red,)),
            dma((2,)),
        ],
        compiler_params=pltpu.CompilerParams(
            collective_id=0, has_side_effects=True, vmem_limit_bytes=56 * 1024 * 1024
        ),
    )(
        positions.reshape(PAT, 2),
        counts,
        object_field,
        probe,
        measured.reshape(PAT, N, N),
        jnp.asarray(forward),
        jnp.asarray(inverse),
    )


def solution(mesh):
    in_specs = (
        P(None, "row", "col"),
        P(),
        P("row", "col", None, None, None),
        P("row", "col", None, None),
        P("row", "col"),
    )
    out_specs = (P(None, "row", "col"), P())
    return jax.shard_map(body, mesh=mesh, in_specs=in_specs, out_specs=out_specs, check_vma=False)
```

```python
import functools

import jax
import jax.numpy as jnp
import ml_dtypes
import numpy as np
from jax import lax
from jax.experimental import pallas as pl
from jax.experimental.pallas import tpu as pltpu
from jax.sharding import PartitionSpec as P

N = 256
HALF = 128
TH = 256
TW = 512
PAT = 4
CORES = 2
XS = 4
ZS = 8
YS = 4
GCHUNK = 16
CHUNK = 24
TILE = 8
DIRS = [(-1, 0), (1, 0), (0, -1), (0, 1), (-1, -1), (-1, 1), (1, -1), (1, 1)]
OWN = len(DIRS)
MESH = pl.DeviceIdType.MESH


def tables(extent):
    indices = np.arange(extent, dtype=np.int32)
    products = indices[:, None] * indices[None, :] % extent
    angles = 2.0 * np.pi / extent * products.astype(np.float64)
    cosine = np.cos(angles) / np.sqrt(float(extent))
    sine_part = np.sin(angles) / np.sqrt(float(extent))
    forward = np.block([[cosine, -sine_part], [sine_part, cosine]])
    inverse = np.block([[cosine, sine_part], [-sine_part, cosine]])
    return (
        forward.astype(np.float32).astype(ml_dtypes.bfloat16),
        inverse.astype(np.float32).astype(ml_dtypes.bfloat16),
    )


def edge(step, size):
    if step == 0:
        return pl.ds(0, size)
    return pl.ds(0 if step < 0 else size - HALF, HALF)


def margin(step, size):
    if step == 0:
        return pl.ds(HALF, size)
    return pl.ds(0 if step < 0 else size + HALF, HALF)


def kernel(
    pos_in,
    cnt_in,
    obj,
    probe_in,
    meas_in,
    fwd_in,
    inv_in,
    obj_new,
    probe_new,
    pos,
    cnt,
    framed,
    probe,
    power,
    ill,
    meas,
    meas_t,
    fwd,
    inv,
    padded,
    canvas,
    rx_v,
    rx_h,
    patches,
    wave,
    exits,
    halves,
    residues,
    backs,
    w1,
    rxw1,
    w2,
    rxw2,
    g1,
    rxg1,
    g2,
    rxg2,
    s3,
    rx3,
    rx4,
    gathered,
    local_sem,
    pos_send,
    pos_recv,
    cnt_send,
    cnt_recv,
    halo_send,
    halo_recv,
    grad_send,
    grad_recv,
    red_send,
    red_recv,
):
    row = lax.axis_index("row")
    col = lax.axis_index("col")
    core = lax.rem(col, CORES)
    x_at = (row // YS) * 2 + lax.rem(col // 2, 2)
    z_at = col // 4
    y_at = lax.rem(row, YS)

    def core_peer():
        return (row, col + 1 - 2 * core)

    def x_peer(i):
        return ((i // 2) * YS + y_at, z_at * 4 + lax.rem(i, 2) * 2 + core)

    def z_peer(i):
        return (row, i * 4 + lax.rem(col, 4))

    def y_peer(i):
        return ((row // YS) * YS + i, col)

    def exists(step):
        near_row, near_col = row + step[0], col + step[1]
        conds = []
        if step[0] < 0:
            conds.append(near_row >= 0)
        if step[0] > 0:
            conds.append(near_row < lax.axis_size("row"))
        if step[1] < 0:
            conds.append(near_col >= 0)
        if step[1] > 0:
            conds.append(near_col < lax.axis_size("col"))
        return functools.reduce(jnp.logical_and, conds)

    center = (slice(None), pl.ds(HALF, TH), pl.ds(HALF, TW))
    local = [
        pltpu.make_async_copy(probe_in, probe, local_sem.at[0]),
        pltpu.make_async_copy(meas_in, meas, local_sem.at[1]),
        pltpu.make_async_copy(fwd_in, fwd, local_sem.at[2]),
        pltpu.make_async_copy(inv_in, inv, local_sem.at[3]),
        pltpu.make_async_copy(obj, framed.at[center], local_sem.at[4]),
        pltpu.make_async_copy(pos_in, pos.at[OWN], local_sem.at[5]),
        pltpu.make_async_copy(cnt_in, cnt.at[OWN], local_sem.at[6]),
    ]

    def do_barrier():
        barrier = pltpu.get_barrier_semaphore()
        greeted = jnp.int32(0)
        for step in DIRS:
            there = exists(step)

            @pl.when(there)
            def _():
                pl.semaphore_signal(
                    barrier, inc=1, device_id=(row + step[0], col + step[1]), device_id_type=MESH
                )

            greeted = greeted + there.astype(jnp.int32)
        pl.semaphore_signal(barrier, inc=1, device_id=core_peer(), device_id_type=MESH)
        for d in range(1, XS):
            pl.semaphore_signal(
                barrier, inc=1, device_id=x_peer(lax.rem(x_at + d, XS)), device_id_type=MESH
            )
        for d in range(1, ZS):
            pl.semaphore_signal(
                barrier, inc=1, device_id=z_peer(lax.rem(z_at + d, ZS)), device_id_type=MESH
            )
        for d in range(1, YS):
            pl.semaphore_signal(
                barrier, inc=1, device_id=y_peer(lax.rem(y_at + d, YS)), device_id_type=MESH
            )
        for copy in local:
            copy.start()
        pl.semaphore_wait(barrier, greeted + (CORES - 1 + XS - 1 + ZS - 1 + YS - 1))

    def near(dr, dc):
        return (row + dr, col + dc)

    def remote(src, dst, send_sem, recv_sem, peer):
        return pltpu.make_async_remote_copy(
            src_ref=src,
            dst_ref=dst,
            send_sem=send_sem,
            recv_sem=recv_sem,
            device_id=peer,
            device_id_type=MESH,
        )

    def opposite(n):
        return DIRS.index((-DIRS[n][0], -DIRS[n][1]))

    def place_copy(n):
        return remote(pos_in, pos.at[opposite(n)], pos_send.at[n], pos_recv.at[n], near(*DIRS[n]))

    def count_copy(n):
        return remote(cnt_in, cnt.at[opposite(n)], cnt_send.at[n], cnt_recv.at[n], near(*DIRS[n]))

    strips = [pl.ds(0, HALF), pl.ds(TW - HALF, HALF), pl.ds(HALF, TW - 2 * HALF)]

    def shifted(cols):
        return pl.ds(cols.start + HALF, cols.size)

    def halo_v(n, part):
        dr = DIRS[n][0]
        sem = n * 3 + part
        return remote(
            obj.at[:, edge(dr, TH), strips[part]],
            framed.at[:, margin(-dr, TH), shifted(strips[part])],
            halo_send.at[sem],
            halo_recv.at[sem],
            near(dr, 0),
        )

    def halo_h(n):
        dc = DIRS[n][1]
        return remote(
            obj.at[:, :, edge(dc, TW)],
            framed.at[:, pl.ds(HALF, TH), margin(-dc, TW)],
            halo_send.at[4 + n],
            halo_recv.at[4 + n],
            near(0, dc),
        )

    def halo_c(n):
        dr, dc = DIRS[n]
        return remote(
            framed.at[:, margin(-dr, TH), shifted(edge(dc, TW))],
            framed.at[:, margin(-dr, TH), margin(-dc, TW)],
            halo_send.at[4 + n],
            halo_recv.at[4 + n],
            near(0, dc),
        )

    def grad_v(n, part):
        dr = DIRS[n][0]
        sem = n * 3 + part
        return remote(
            canvas.at[:, margin(dr, TH), shifted(strips[part])],
            rx_v.at[(dr + 1) // 2, :, :, strips[part]],
            grad_send.at[sem],
            grad_recv.at[sem],
            near(dr, 0),
        )

    def grad_h(n):
        dr, dc = DIRS[n]
        rows = margin(dr, TH)
        return remote(
            canvas.at[:, rows, margin(dc, TW)],
            rx_h.at[(dc + 1) // 2, :, rows],
            grad_send.at[4 + n],
            grad_recv.at[4 + n],
            near(0, dc),
        )

    vertical, level, diagonal = (0, 1), (2, 3), (4, 5, 6, 7)

    def start(make, order, *more):
        for n in order:

            @pl.when(exists(DIRS[n]))
            def _():
                make(n, *more).start()

    def arrive(make, order, *more):
        for n in order:

            @pl.when(exists(DIRS[n]))
            def _():
                make(n, *more).wait_send()

            @pl.when(exists(DIRS[opposite(n)]))
            def _():
                make(n, *more).wait_recv()

    def start_level(n):
        @pl.when(exists((0, DIRS[n][1])))
        def _():
            grad_h(n).start()

    def arrive_level(n):
        @pl.when(exists((0, DIRS[n][1])))
        def _():
            grad_h(n).wait_send()

        @pl.when(exists((0, -DIRS[n][1])))
        def _():
            grad_h(n).wait_recv()

    def do_place_send():
        start(place_copy, range(OWN))
        start(count_copy, range(OWN))

    def do_halo_send():
        start(halo_v, vertical, 0)
        start(halo_v, vertical, 1)
        start(halo_h, level)
        start(halo_v, vertical, 2)

    def do_halo_forward():
        arrive(halo_v, vertical, 0)
        arrive(halo_v, vertical, 1)
        for n in diagonal:
            @pl.when(exists((-DIRS[n][0], DIRS[n][1])))
            def _():
                halo_c(n).start()

    def do_halo_wait():
        arrive(halo_h, level)
        arrive(halo_v, vertical, 2)
        for n in diagonal:
            dr, dc = DIRS[n]

            @pl.when(exists((-dr, dc)))
            def _():
                halo_c(n).wait_send()

            @pl.when(exists((-dr, -dc)))
            def _():
                halo_c(n).wait_recv()

    def do_margins():
        for n in range(OWN):
            dr, dc = DIRS[n]

            @pl.when(jnp.logical_not(exists(DIRS[n])))
            def _():
                rows, cols = margin(dr, TH), margin(dc, TW)
                framed[:, rows, cols] = jnp.zeros((2, rows.size, cols.size), jnp.float32)
                cnt[n, 0, 0] = 0
                for k in range(PAT):
                    pos[n, 0, k] = 0
                    pos[n, 1, k] = 0

        for n in vertical:

            @pl.when(jnp.logical_not(exists(DIRS[n])))
            def _():
                rx_v[1 - n] = jnp.zeros((2, HALF, TW), jnp.float32)

        for n in level:

            @pl.when(jnp.logical_not(exists(DIRS[n])))
            def _():
                rx_h[3 - n] = jnp.zeros((2, TH + 2 * HALF, HALF), jnp.float32)

        framed[:, TH + 2 * HALF :, :] = jnp.zeros((2, TILE, TW + 3 * HALF), jnp.float32)
        framed[:, : TH + 2 * HALF, TW + 2 * HALF :] = jnp.zeros(
            (2, TH + 2 * HALF, HALF), jnp.float32
        )

    def clear(i, carry):
        at = pl.ds(pl.multiple_of(i * 32, 32), 32)
        for k in range(PAT):
            for p in range(2):
                padded[k, p, at, :] = jnp.zeros((32, 640), jnp.float32)
        return carry

    def do_clear():
        lax.fori_loop(0, 24, clear, 0)

    def do_probe_in():
        local[0].wait()

    def do_meas_in():
        for copy in local[1:5]:
            copy.wait()

    def do_place_in():
        for copy in local[5:]:
            copy.wait()
        arrive(place_copy, range(OWN))
        arrive(count_copy, range(OWN))

    lives, tops, lefts, downs, overs = [], [], [], [], []

    def do_places():
        for k in range(PAT):
            a = lax.max(lax.min(pos[OWN, 0, k] - (row * TH - HALF), TH), 0)
            b = lax.max(lax.min(pos[OWN, 1, k] - (col * TW - HALF), TW), 0)
            lives.append(jnp.where(k < cnt[OWN, 0, 0], 1.0, 0.0).astype(jnp.float32))
            tops.append(lax.div(a, TILE))
            downs.append(lax.rem(a, TILE))
            lefts.append(lax.div(b, 128))
            overs.append(lax.rem(b, 128))

    def lane_iota(shape):
        return lax.broadcasted_iota(jnp.int32, shape, len(shape) - 1)

    def sub_iota(shape):
        return lax.broadcasted_iota(jnp.int32, shape, len(shape) - 2)

    def window(p, k, first, tiles):
        s, r = downs[k], overs[k]
        rows = pl.ds((tops[k] + first) * TILE, (tiles + 1) * TILE)
        turned = []
        for j in range(3):
            cols = pl.ds((lefts[k] + j) * 128, 128)
            turned.append(pltpu.roll(framed[p, rows, cols], lax.rem(128 - r, 128), 1))
        near = lane_iota(turned[0].shape) < 128 - r
        found = []
        for j in range(2):
            both = jnp.where(near, turned[j], turned[j + 1]).reshape(tiles + 1, TILE, 128)
            both = pltpu.roll(both, lax.rem(TILE - s, TILE), 1)
            upper = sub_iota((tiles, TILE, 128)) < TILE - s
            found.append(
                jnp.where(upper, both[:tiles], both[1:]).reshape(tiles * TILE, 128)
            )
        return found

    def lay(k, p, tiles, s, r):
        moved = []
        for x in tiles:
            x = pltpu.roll(x.reshape(N // TILE, TILE, 128), s, 1)
            none = jnp.zeros((1, TILE, 128), jnp.float32)
            here = jnp.concatenate([x, none], axis=0)
            above = jnp.concatenate([none, x], axis=0)
            y = jnp.where(sub_iota(here.shape) >= s, here, above).reshape(N + TILE, 128)
            moved.append(pltpu.roll(y, r, 1))
        right = lane_iota((N + TILE, 128)) >= r
        rows = pl.ds(N, N + TILE)
        padded[k, p, rows, pl.ds(128, 128)] = jnp.where(right, moved[0], 0.0)
        padded[k, p, rows, pl.ds(256, 128)] = jnp.where(right, moved[1], moved[0])
        padded[k, p, rows, pl.ds(384, 128)] = jnp.where(right, 0.0, moved[1])

    def collect(start, stop, pairs):
        size = 8

        def one(i, carry):
            first = i * size
            rows = pl.ds(pl.multiple_of(first * TILE, size * TILE), size * TILE)
            for q, p in pairs:
                for j in range(6):
                    total = None
                    for k in range(PAT):
                        at = (first - tops[k] + N // TILE) * TILE
                        lane = lax.max(lax.min(j - lefts[k] + 1, 4), 0) * 128
                        part = padded[
                            k, p, pl.ds(at, size * TILE), pl.ds(lane, 128)
                        ]
                        total = part if total is None else total + part
                    canvas[q, rows, pl.ds(j * 128, 128)] = total
            return carry

        lax.fori_loop(start // size, stop // size, one, 0)

    def do_power():
        for j in range(2):
            cols = pl.ds(128 * j, 128)
            power[j] = probe[0, :, cols] * probe[0, :, cols] + probe[1, :, cols] * probe[1, :, cols]
        ill[...] = jnp.zeros((TH, TW), jnp.float32)

    def light(t, carry):
        high, left = [], []
        for k in range(PAT):
            alive = jnp.where(k < cnt[t, 0, 0], 1.0, 0.0).astype(jnp.float32)
            a = lax.max(lax.min(pos[t, 0, k] - row * TH, 384), -384) + 384
            b = lax.max(lax.min(pos[t, 1, k] - col * TW, 896), -640) + 640
            lay(k, 0, [alive * power[j] for j in range(2)], lax.rem(a, TILE), lax.rem(b, 128))
            high.append(lax.div(a, TILE) - 80)
            left.append(lax.div(b, 128) - 5)
        size = 8
        for i in range(0, TH // TILE, size):
            rows = pl.ds(i * TILE, size * TILE)
            for j in range(4):
                total = ill[rows, pl.ds(j * 128, 128)]
                for k in range(PAT):
                    at = lax.max(lax.min(i - high[k], 96 - size), 0) * TILE
                    lane = lax.max(lax.min(j - left[k] + 1, 4), 0) * 128
                    total = total + padded[k, 0, pl.ds(at, size * TILE), pl.ds(lane, 128)]
                ill[rows, pl.ds(j * 128, 128)] = total
        return carry

    def do_light():
        lax.fori_loop(0, len(DIRS) + 1, light, 0)

    def do_peak():
        def largest(i, most):
            rows = pl.ds(pl.multiple_of(i * 32, 32), 32)
            for j in range(4):
                value = ill[rows, pl.ds(128 * j, 128)]
                most = jnp.maximum(most, jnp.max(value.reshape(4, TILE, 128), axis=0))
            return most

        peak = lax.fori_loop(0, TH // 32, largest, jnp.zeros((TILE, 128), jnp.float32))
        for c in range(CORES):
            w1[c, N:, :] = peak

    def do_turn():
        for k in range(PAT):
            meas_t[k] = meas[k].T

    def cut(i, carry):
        tiles = 4
        rows = pl.ds(pl.multiple_of(i * tiles * TILE, tiles * TILE), tiles * TILE)
        weight = [jnp.zeros((tiles * TILE, 128), jnp.float32)] * 2
        for k in range(PAT):
            real = window(0, k, i * tiles, tiles)
            imag = window(1, k, i * tiles, tiles)
            for j in range(2):
                cols = pl.ds(128 * j, 128)
                p_re, p_im = probe[0, rows, cols], probe[1, rows, cols]
                patches[k, 0, rows, cols] = real[j]
                patches[k, 1, rows, cols] = imag[j]
                exits[k, rows, cols] = (p_re * real[j] - p_im * imag[j]).astype(jnp.bfloat16)
                exits[k, rows, pl.ds(N + 128 * j, 128)] = (
                    p_re * imag[j] + p_im * real[j]
                ).astype(jnp.bfloat16)
                weight[j] = weight[j] + lives[k] * (real[j] * real[j] + imag[j] * imag[j])
        for j in range(2):
            w1[j, rows, :] = weight[j]
        return carry

    def do_cut():
        lax.fori_loop(0, 8, cut, 0)

    def dot(a, b):
        return jnp.dot(a, b, preferred_element_type=jnp.float32)

    def do_transforms(first, last):
        for k in range(first, last):
            half = dot(exits[k], fwd[...]).astype(jnp.bfloat16)
            halves[k, :N, :] = half[:, :N]
            halves[k, N:, :] = half[:, N:]
            spectrum = dot(inv[...], halves[k])
            re, im = spectrum[:N], spectrum[N:]
            factor = lives[k] * (1.0 - meas_t[k] * lax.rsqrt(re * re + im * im + 0.25))
            residues[k, :N, :] = (factor * re).astype(jnp.bfloat16)
            residues[k, N:, :] = (factor * im).astype(jnp.bfloat16)
            back = dot(fwd[...], residues[k]).astype(jnp.bfloat16)
            backs[k, :, :N] = back[:N]
            backs[k, :, N:] = back[N:]
            wave[k] = dot(backs[k], inv[...])

    def probe_sum(i, carry):
        size = 32
        at = pl.multiple_of(i * size, size)
        rows = pl.ds(at, size)
        for j in range(2):
            cols = pl.ds(128 * j, 128)
            real = imag = None
            for k in range(PAT):
                a, b = patches[k, 0, rows, cols], patches[k, 1, rows, cols]
                u, v = wave[k, rows, cols], wave[k, rows, pl.ds(N + 128 * j, 128)]
                one, two = a * u + b * v, a * v - b * u
                real = one if real is None else real + one
                imag = two if imag is None else imag + two
            g1[j, rows, :] = real
            g1[j, pl.ds(pl.multiple_of(N + at, 8), size), :] = imag
        return carry

    def do_probe_sum():
        lax.fori_loop(0, N // 32, probe_sum, 0)

    def owned(p, rows, at, h, j):
        size = rows.size
        inner = pl.ds(pl.multiple_of(HALF + h * HALF + at, 8), size)
        value = canvas[p, inner, pl.ds(128 * (j + 1), 128)]
        value = value + rx_v[1 - h, p, pl.ds(at, size), pl.ds(128 * j, 128)]
        if j in (0, 3):
            value = value + rx_h[1 if j == 0 else 0, p, inner, :]
        return value

    size = 32

    def send(src, dst, sem, peer):
        return remote(src, dst, red_send.at[sem], red_recv.at[sem], peer)

    def w_core():
        return send(w1.at[1 - core], rxw1, 0, core_peer())

    def g_core():
        return send(g1.at[1 - core], rxg1, 1, core_peer())

    def w_x(d):
        to = lax.rem(x_at + d, XS)
        return send(w2.at[to], rxw2.at[d - 1], 1 + d, x_peer(to))

    def g_x(d):
        to = lax.rem(x_at + d, XS)
        return send(g2.at[to], rxg2.at[d - 1], 4 + d, x_peer(to))

    def z_copy(d):
        to = lax.rem(z_at + d, ZS)
        return send(s3.at[to], rx3.at[d - 1], 7 + d, z_peer(to))

    def y_copy(d):
        to = lax.rem(y_at + d, YS)
        return send(rx4.at[y_at], rx4.at[y_at], 14 + d, y_peer(to))

    def do_w_core_send():
        w_core().start()

    def do_w_core_sum():
        w_core().wait()
        part = N // XS
        crown = jnp.maximum(w1[core, N:, :], rxw1[N:, :])
        for i in range(XS):
            at = pl.ds(i * part, part)
            w2[i, :part, :] = w1[core, at, :] + rxw1[at, :]
            w2[i, part:, :] = crown

    def do_w_x_send():
        for d in range(1, XS):
            w_x(d).start()

    def do_w_x_sum():
        for d in range(1, XS):
            w_x(d).wait()
        part = N // XS
        crown = w2[x_at, part:, :]
        for d in range(XS - 1):
            crown = jnp.maximum(crown, rxw2[d, part:, :])
        size = CHUNK - GCHUNK
        for i in range(ZS):
            at = pl.ds(i * size, size)
            s3[i, GCHUNK:CHUNK, :] = (w2[x_at, at, :] + rxw2[0, at, :]) + (
                rxw2[1, at, :] + rxw2[2, at, :]
            )
            s3[i, CHUNK:, :] = crown

    def do_core_send():
        g_core().start()

    def do_core_sum():
        g_core().wait()
        part = 2 * N // XS
        for i in range(XS):
            at = pl.ds(i * part, part)
            g2[i] = g1[core, at, :] + rxg1[at, :]

    def do_x_send():
        for d in range(1, XS):
            g_x(d).start()

    def do_x_sum():
        for d in range(1, XS):
            g_x(d).wait()
        for i in range(ZS):
            at = pl.ds(i * GCHUNK, GCHUNK)
            s3[i, :GCHUNK, :] = (g2[x_at, at, :] + rxg2[0, at, :]) + (
                rxg2[1, at, :] + rxg2[2, at, :]
            )

    def do_z_send():
        for d in range(1, ZS):
            z_copy(d).start()

    def do_z_sum():
        for d in range(1, ZS):
            z_copy(d).wait()
        total = s3[z_at, :CHUNK, :]
        crown = s3[z_at, CHUNK:, :]
        for d in range(ZS - 1):
            total = total + rx3[d, :CHUNK, :]
            crown = jnp.maximum(crown, rx3[d, CHUNK:, :])
        rx4[y_at, :CHUNK, :] = total
        rx4[y_at, CHUNK:, :] = crown

    def do_y_send():
        for d in range(1, YS):
            y_copy(d).start()

    def do_y_sum():
        for d in range(1, YS):
            y_copy(d).wait()
        gathered[core, x_at, z_at] = (rx4[0, :CHUNK, :] + rx4[1, :CHUNK, :]) + (
            rx4[2, :CHUNK, :] + rx4[3, :CHUNK, :]
        )

    base = 18

    def z_back(d):
        to = lax.rem(z_at + d, ZS)
        mine = gathered.at[core, x_at, z_at]
        return send(mine, mine, base + d - 1, z_peer(to))

    def x_back(d):
        to = lax.rem(x_at + d, XS)
        mine = gathered.at[core, x_at]
        return send(mine, mine, base + ZS - 1 + d - 1, x_peer(to))

    def core_back():
        mine = gathered.at[core]
        return send(mine, mine, base + ZS + XS - 2, core_peer())

    def do_z_back():
        for d in range(1, ZS):
            z_back(d).start()

    def do_z_wait():
        for d in range(1, ZS):
            z_back(d).wait()

    def do_x_back():
        for d in range(1, XS):
            x_back(d).start()

    def do_x_wait():
        for d in range(1, XS):
            x_back(d).wait()

    def do_core_back():
        core_back().start()

    def do_core_wait():
        core_back().wait()

    def do_lay():
        for k in range(PAT):
            parts = ([], [])
            for j in range(2):
                cols = pl.ds(128 * j, 128)
                u, v = wave[k, :, cols], wave[k, :, pl.ds(N + 128 * j, 128)]
                p_re, p_im = probe[0, :, cols], probe[1, :, cols]
                parts[0].append(p_re * u + p_im * v)
                parts[1].append(p_re * v - p_im * u)
            for p in range(2):
                lay(k, p, parts[p], downs[k], overs[k])

    def do_collect(first, last):
        collect(first, last, [(0, 0), (1, 1)])

    def do_grad_send():
        for n in diagonal:
            start_level(n)
        start(grad_v, vertical, 2)
        for n in level:
            start_level(n)

    def do_grad_forward():
        for n in diagonal:
            arrive_level(n)
        for dr in (-1, 1):
            rows = margin(dr, TH)
            for dc in (-1, 1):
                cols = shifted(edge(dc, TW))
                canvas[:, rows, cols] = canvas[:, rows, cols] + rx_h[(1 - dc) // 2, :, rows, :]
        start(grad_v, vertical, 0)
        start(grad_v, vertical, 1)

    def do_grad_wait():
        for n in level:
            arrive_level(n)
        for part in range(3):
            arrive(grad_v, vertical, part)

    def do_object():
        crown = jnp.maximum(
            jnp.maximum(rx4[0, CHUNK:, :], rx4[1, CHUNK:, :]),
            jnp.maximum(rx4[2, CHUNK:, :], rx4[3, CHUNK:, :]),
        )
        top = jnp.max(crown)
        for h in range(2):

            def renew(i, carry, h=h):
                at = pl.multiple_of(i * size, size)
                rows = pl.ds(pl.multiple_of(h * HALF + at, size), size)
                inner = pl.ds(pl.multiple_of(HALF + h * HALF + at, 8), size)
                for j in range(4):
                    cols = pl.ds(128 * (j + 1), 128)
                    share = 1.0 / (0.75 * ill[rows, pl.ds(128 * j, 128)] + 0.25 * top)
                    for p in range(2):
                        obj_new[p, rows, pl.ds(128 * j, 128)] = (
                            framed[p, inner, cols] - owned(p, rows, at, h, j) * share
                        )
                return carry

            lax.fori_loop(0, HALF // size, renew, 0)

    def do_probe():
        weight = [gathered[j, :, :, GCHUNK:, :].reshape(N, 128) for j in range(2)]
        heavy = jnp.maximum(jnp.max(weight[0]), jnp.max(weight[1]))
        for j in range(2):
            cols = pl.ds(128 * j, 128)
            share = 1.0 / (0.75 * weight[j] + 0.25 * heavy)
            for p in range(2):
                total = gathered[j, 2 * p : 2 * p + 2, :, :GCHUNK, :].reshape(N, 128)
                probe_new[p, :, cols] = probe[p, :, cols] - total * share

    do_barrier()
    do_place_send()
    do_halo_send()
    do_margins()
    do_clear()
    do_probe_in()
    do_power()
    do_place_in()
    do_places()
    do_light()
    do_peak()
    do_halo_forward()
    do_meas_in()
    do_turn()
    do_halo_wait()
    do_cut()
    do_w_core_send()
    do_transforms(0, 2)
    do_w_core_sum()
    do_w_x_send()
    do_transforms(2, 4)
    do_probe_sum()
    do_core_send()
    do_lay()
    do_collect(0, 64)
    do_core_sum()
    do_x_send()
    do_grad_send()
    do_w_x_sum()
    do_x_sum()
    do_z_send()
    do_grad_forward()
    do_z_sum()
    do_y_send()
    do_y_sum()
    do_z_back()
    do_z_wait()
    do_x_back()
    do_grad_wait()
    do_object()
    do_x_wait()
    do_core_back()
    do_core_wait()
    do_probe()


def body(object_field, probe, measured, positions, counts):
    forward, inverse = tables(N)
    any_space = pl.BlockSpec(memory_space=pl.ANY)
    vmem = pl.BlockSpec(memory_space=pltpu.VMEM)
    f32 = jnp.float32
    bf16 = jnp.bfloat16
    red = 18 + (ZS - 1) + (XS - 1) + 1
    dma = pltpu.SemaphoreType.DMA
    return pl.pallas_call(
        kernel,
        out_shape=(pltpu.VMEM((2, TH, TW), f32), pltpu.VMEM((2, N, N), f32)),
        in_specs=[any_space] * 7,
        out_specs=(vmem, vmem),
        scratch_shapes=[
            pltpu.SMEM((OWN + 1, 2, PAT), jnp.int32),
            pltpu.SMEM((OWN + 1, 1, 1), jnp.int32),
            pltpu.VMEM((2, TH + 2 * HALF + TILE, TW + 3 * HALF), f32),
            pltpu.VMEM((2, N, N), f32),
            pltpu.VMEM((2, N, 128), f32),
            pltpu.VMEM((TH, TW), f32),
            pltpu.VMEM((PAT, N, N), f32),
            pltpu.VMEM((PAT, N, N), f32),
            pltpu.VMEM((2 * N, 2 * N), bf16),
            pltpu.VMEM((2 * N, 2 * N), bf16),
            pltpu.VMEM((PAT, 2, 3 * N, 640), f32),
            pltpu.VMEM((2, TH + 2 * HALF, TW + 2 * HALF), f32),
            pltpu.VMEM((2, 2, HALF, TW), f32),
            pltpu.VMEM((2, 2, TH + 2 * HALF, HALF), f32),
            pltpu.VMEM((PAT, 2, N, N), f32),
            pltpu.VMEM((PAT, N, 2 * N), f32),
            pltpu.VMEM((PAT, N, 2 * N), bf16),
            pltpu.VMEM((PAT, 2 * N, N), bf16),
            pltpu.VMEM((PAT, 2 * N, N), bf16),
            pltpu.VMEM((PAT, N, 2 * N), bf16),
            pltpu.VMEM((CORES, N + TILE, 128), f32),
            pltpu.VMEM((N + TILE, 128), f32),
            pltpu.VMEM((XS, N // XS + TILE, 128), f32),
            pltpu.VMEM((XS - 1, N // XS + TILE, 128), f32),
            pltpu.VMEM((CORES, 2 * N, 128), f32),
            pltpu.VMEM((2 * N, 128), f32),
            pltpu.VMEM((XS, 2 * N // XS, 128), f32),
            pltpu.VMEM((XS - 1, 2 * N // XS, 128), f32),
            pltpu.VMEM((ZS, CHUNK + TILE, 128), f32),
            pltpu.VMEM((ZS - 1, CHUNK + TILE, 128), f32),
            pltpu.VMEM((YS, CHUNK + TILE, 128), f32),
            pltpu.VMEM((CORES, XS, ZS, CHUNK, 128), f32),
            dma((7,)),
            dma((OWN,)),
            dma((OWN,)),
            dma((OWN,)),
            dma((OWN,)),
            dma((12,)),
            dma((12,)),
            dma((12,)),
            dma((12,)),
            dma((red,)),
            dma((red,)),
        ],
        compiler_params=pltpu.CompilerParams(
            collective_id=0, has_side_effects=True, vmem_limit_bytes=56 * 1024 * 1024
        ),
    )(
        positions.reshape(PAT, 2).T,
        counts,
        object_field,
        probe,
        measured.reshape(PAT, N, N),
        jnp.asarray(forward),
        jnp.asarray(inverse),
    )


def solution(mesh):
    in_specs = (
        P(None, "row", "col"),
        P(),
        P("row", "col", None, None, None),
        P("row", "col", None, None),
        P("row", "col"),
    )
    out_specs = (P(None, "row", "col"), P())
    return jax.shard_map(body, mesh=mesh, in_specs=in_specs, out_specs=out_specs, check_vma=False)
```

```python
import functools

import jax
import jax.numpy as jnp
import ml_dtypes
import numpy as np
from jax import lax
from jax.experimental import pallas as pl
from jax.experimental.pallas import tpu as pltpu
from jax.sharding import PartitionSpec as P

N = 256
HALF = 128
TH = 256
TW = 512
PAT = 4
CORES = 2
XS = 4
ZS = 8
YS = 4
GCHUNK = 16
CHUNK = 24
TILE = 8
DIRS = [(-1, 0), (1, 0), (0, -1), (0, 1), (-1, -1), (-1, 1), (1, -1), (1, 1)]
OWN = len(DIRS)
NEAR = (1, 7, 2, 6, 3, 5, 4)
FAR = NEAR[::-1] + (0,)
MESH = pl.DeviceIdType.MESH


def tables(extent):
    indices = np.arange(extent, dtype=np.int32)
    products = indices[:, None] * indices[None, :] % extent
    angles = 2.0 * np.pi / extent * products.astype(np.float64)
    cosine = np.cos(angles) / np.sqrt(float(extent))
    sine_part = np.sin(angles) / np.sqrt(float(extent))
    forward = np.block([[cosine, -sine_part], [sine_part, cosine]])
    inverse = np.block([[cosine, sine_part], [-sine_part, cosine]])
    return (
        forward.astype(np.float32).astype(ml_dtypes.bfloat16),
        inverse.astype(np.float32).astype(ml_dtypes.bfloat16),
    )


def edge(step, size):
    if step == 0:
        return pl.ds(0, size)
    return pl.ds(0 if step < 0 else size - HALF, HALF)


def margin(step, size):
    if step == 0:
        return pl.ds(HALF, size)
    return pl.ds(0 if step < 0 else size + HALF, HALF)


def kernel(
    pos_in,
    cnt_in,
    obj,
    probe_in,
    meas_in,
    fwd_in,
    inv_in,
    obj_new,
    probe_new,
    pos,
    cnt,
    framed,
    probe,
    power,
    ill,
    meas,
    meas_t,
    fwd,
    inv,
    padded,
    canvas,
    rx_v,
    rx_h,
    patches,
    wave,
    exits,
    halves,
    residues,
    backs,
    w1,
    rxw1,
    w2,
    rxw2,
    g1,
    rxg1,
    g2,
    rxg2,
    s3,
    rx3,
    rx4,
    gathered,
    local_sem,
    pos_send,
    pos_recv,
    cnt_send,
    cnt_recv,
    halo_relay,
    grad_relay,
    halo_hop,
    grad_hop,
    halo_send,
    halo_recv,
    grad_send,
    grad_recv,
    red_send,
    red_recv,
):
    row = lax.axis_index("row")
    col = lax.axis_index("col")
    core = lax.rem(col, CORES)
    x_at = (row // YS) * 2 + lax.rem(col // 2, 2)
    z_at = col // 4
    y_at = lax.rem(row, YS)

    def core_peer():
        return (row, col + 1 - 2 * core)

    def x_peer(i):
        return ((i // 2) * YS + y_at, z_at * 4 + lax.rem(i, 2) * 2 + core)

    def z_peer(i):
        return (row, i * 4 + lax.rem(col, 4))

    def y_peer(i):
        return ((row // YS) * YS + i, col)

    def exists(step):
        near_row, near_col = row + step[0], col + step[1]
        conds = []
        if step[0] < 0:
            conds.append(near_row >= 0)
        if step[0] > 0:
            conds.append(near_row < lax.axis_size("row"))
        if step[1] < 0:
            conds.append(near_col >= 0)
        if step[1] > 0:
            conds.append(near_col < lax.axis_size("col"))
        return functools.reduce(jnp.logical_and, conds)

    center = (slice(None), pl.ds(HALF, TH), pl.ds(HALF, TW))
    local = [
        pltpu.make_async_copy(probe_in, probe, local_sem.at[0]),
        pltpu.make_async_copy(meas_in, meas, local_sem.at[1]),
        pltpu.make_async_copy(fwd_in, fwd, local_sem.at[2]),
        pltpu.make_async_copy(inv_in, inv, local_sem.at[3]),
        pltpu.make_async_copy(obj, framed.at[center], local_sem.at[4]),
        pltpu.make_async_copy(pos_in, pos.at[OWN], local_sem.at[5]),
        pltpu.make_async_copy(cnt_in, cnt.at[OWN], local_sem.at[6]),
    ]

    def do_barrier():
        barrier = pltpu.get_barrier_semaphore()
        greeted = jnp.int32(0)
        for step in DIRS:
            there = exists(step)

            @pl.when(there)
            def _():
                pl.semaphore_signal(
                    barrier, inc=1, device_id=(row + step[0], col + step[1]), device_id_type=MESH
                )

            greeted = greeted + there.astype(jnp.int32)
        pl.semaphore_signal(barrier, inc=1, device_id=core_peer(), device_id_type=MESH)
        for d in range(1, XS):
            pl.semaphore_signal(
                barrier, inc=1, device_id=x_peer(lax.rem(x_at + d, XS)), device_id_type=MESH
            )
        for d in range(1, ZS):
            pl.semaphore_signal(
                barrier, inc=1, device_id=z_peer(lax.rem(z_at + d, ZS)), device_id_type=MESH
            )
        for d in range(1, YS):
            pl.semaphore_signal(
                barrier, inc=1, device_id=y_peer(lax.rem(y_at + d, YS)), device_id_type=MESH
            )
        for n in vertical:
            near_end, relay_row, far_end = route(n)

            @pl.when(row == far_end)
            def _():
                pl.semaphore_signal(
                    barrier, inc=1, device_id=across(relay_row), device_id_type=MESH
                )

            greeted = greeted + (row == relay_row).astype(jnp.int32)
        for copy in local:
            copy.start()
        pl.semaphore_wait(barrier, greeted + (CORES - 1 + XS - 1 + ZS - 1 + YS - 1))

    def near(dr, dc):
        return (row + dr, col + dc)

    def remote(src, dst, send_sem, recv_sem, peer):
        return pltpu.make_async_remote_copy(
            src_ref=src,
            dst_ref=dst,
            send_sem=send_sem,
            recv_sem=recv_sem,
            device_id=peer,
            device_id_type=MESH,
        )

    def opposite(n):
        return DIRS.index((-DIRS[n][0], -DIRS[n][1]))

    def place_copy(n):
        return remote(pos_in, pos.at[opposite(n)], pos_send.at[n], pos_recv.at[n], near(*DIRS[n]))

    def count_copy(n):
        return remote(cnt_in, cnt.at[opposite(n)], cnt_send.at[n], cnt_recv.at[n], near(*DIRS[n]))

    strips = [pl.ds(0, HALF), pl.ds(TW - HALF, HALF), pl.ds(HALF, TW - 2 * HALF)]

    def shifted(cols):
        return pl.ds(cols.start + HALF, cols.size)

    def halo_v(n, part):
        dr = DIRS[n][0]
        sem = n * 3 + part
        return remote(
            obj.at[:, edge(dr, TH), strips[part]],
            framed.at[:, margin(-dr, TH), shifted(strips[part])],
            halo_send.at[sem],
            halo_recv.at[sem],
            near(dr, 0),
        )

    def halo_h(n):
        dc = DIRS[n][1]
        return remote(
            obj.at[:, :, edge(dc, TW)],
            framed.at[:, pl.ds(HALF, TH), margin(-dc, TW)],
            halo_send.at[4 + n],
            halo_recv.at[4 + n],
            near(0, dc),
        )

    def halo_c(n):
        dr, dc = DIRS[n]
        return remote(
            framed.at[:, margin(-dr, TH), shifted(edge(dc, TW))],
            framed.at[:, margin(-dr, TH), margin(-dc, TW)],
            halo_send.at[4 + n],
            halo_recv.at[4 + n],
            near(0, dc),
        )

    def grad_v(n, part):
        dr = DIRS[n][0]
        sem = n * 3 + part
        return remote(
            canvas.at[:, margin(dr, TH), shifted(strips[part])],
            rx_v.at[(dr + 1) // 2, :, :, strips[part]],
            grad_send.at[sem],
            grad_recv.at[sem],
            near(dr, 0),
        )

    def grad_h(n):
        dr, dc = DIRS[n]
        rows = margin(dr, TH)
        return remote(
            canvas.at[:, rows, margin(dc, TW)],
            rx_h.at[(dc + 1) // 2, :, rows],
            grad_send.at[4 + n],
            grad_recv.at[4 + n],
            near(0, dc),
        )

    vertical, level, diagonal = (0, 1), (2, 3), (4, 5, 6, 7)

    def start(make, order, *more):
        for n in order:

            @pl.when(exists(DIRS[n]))
            def _():
                make(n, *more).start()

    def arrive(make, order, *more):
        for n in order:

            @pl.when(exists(DIRS[n]))
            def _():
                make(n, *more).wait_send()

            @pl.when(exists(DIRS[opposite(n)]))
            def _():
                make(n, *more).wait_recv()

    def start_level(n):
        @pl.when(exists((0, DIRS[n][1])))
        def _():
            grad_h(n).start()

    def arrive_level(n):
        @pl.when(exists((0, DIRS[n][1])))
        def _():
            grad_h(n).wait_send()

        @pl.when(exists((0, -DIRS[n][1])))
        def _():
            grad_h(n).wait_recv()

    def do_place_send():
        start(place_copy, range(OWN))
        start(count_copy, range(OWN))

    def route(n):
        return (3, 7, 4) if DIRS[n][0] > 0 else (4, 0, 3)

    def across(i):
        return (i, col + 2 - 4 * lax.rem(col // 2, 2))

    def leg_one(n, p, src, buf, sems):
        return remote(src, buf.at[p], sems.at[p], sems.at[2 + p], across(route(n)[1]))

    def leg_two(n, p, dst, buf, sems):
        return remote(buf.at[p], dst, sems.at[4 + p], sems.at[6 + p], across(route(n)[2]))

    def halo_ends(n, p):
        dr = DIRS[n][0]
        src = obj.at[p, edge(dr, TH), strips[2]]
        return src, framed.at[p, margin(-dr, TH), shifted(strips[2])], halo_relay, halo_hop

    def grad_ends(n, p):
        dr = DIRS[n][0]
        src = canvas.at[p, margin(dr, TH), shifted(strips[2])]
        return src, rx_v.at[(dr + 1) // 2, p, :, strips[2]], grad_relay, grad_hop

    def first_leg(n, p, ends):
        src, dst, buf, sems = ends(n, p)
        return leg_one(n, p, src, buf, sems)

    def second_leg(n, p, ends):
        src, dst, buf, sems = ends(n, p)
        return leg_two(n, p, dst, buf, sems)

    def start_middle(direct, ends):
        for n in vertical:

            @pl.when(row == route(n)[0])
            def _():
                for p in range(2):
                    first_leg(n, p, ends).start()

            @pl.when(exists(DIRS[n]) & (row != route(n)[0]))
            def _():
                direct(n, 2).start()

    def relay_middle(ends):
        for n in vertical:

            @pl.when(row == route(n)[1])
            def _():
                for p in range(2):
                    first_leg(n, p, ends).wait_recv()
                    second_leg(n, p, ends).start()

    def arrive_middle(direct, ends):
        for n in vertical:

            @pl.when(row == route(n)[0])
            def _():
                for p in range(2):
                    first_leg(n, p, ends).wait_send()

            @pl.when(exists(DIRS[n]) & (row != route(n)[0]))
            def _():
                direct(n, 2).wait_send()

            @pl.when(row == route(n)[1])
            def _():
                for p in range(2):
                    second_leg(n, p, ends).wait_send()

            @pl.when(row == route(n)[2])
            def _():
                for p in range(2):
                    second_leg(n, p, ends).wait_recv()

            @pl.when(exists(DIRS[opposite(n)]) & (row != route(n)[2]))
            def _():
                direct(n, 2).wait_recv()

    def do_halo_send():
        start(halo_v, vertical, 0)
        start(halo_v, vertical, 1)
        start_middle(halo_v, halo_ends)
        start(halo_h, level)

    def do_halo_forward():
        arrive(halo_v, vertical, 0)
        arrive(halo_v, vertical, 1)
        for n in diagonal:
            @pl.when(exists((-DIRS[n][0], DIRS[n][1])))
            def _():
                halo_c(n).start()

    def do_halo_relay():
        relay_middle(halo_ends)

    def do_halo_wait():
        arrive(halo_h, level)
        arrive_middle(halo_v, halo_ends)
        for n in diagonal:
            dr, dc = DIRS[n]

            @pl.when(exists((-dr, dc)))
            def _():
                halo_c(n).wait_send()

            @pl.when(exists((-dr, -dc)))
            def _():
                halo_c(n).wait_recv()

    def do_margins():
        for n in range(OWN):
            dr, dc = DIRS[n]

            @pl.when(jnp.logical_not(exists(DIRS[n])))
            def _():
                rows, cols = margin(dr, TH), margin(dc, TW)
                framed[:, rows, cols] = jnp.zeros((2, rows.size, cols.size), jnp.float32)
                cnt[n, 0, 0] = 0
                for k in range(PAT):
                    pos[n, 0, k] = 0
                    pos[n, 1, k] = 0

        for n in vertical:

            @pl.when(jnp.logical_not(exists(DIRS[n])))
            def _():
                rx_v[1 - n] = jnp.zeros((2, HALF, TW), jnp.float32)

        for n in level:

            @pl.when(jnp.logical_not(exists(DIRS[n])))
            def _():
                rx_h[3 - n] = jnp.zeros((2, TH + 2 * HALF, HALF), jnp.float32)

        framed[:, TH + 2 * HALF :, :] = jnp.zeros((2, TILE, TW + 3 * HALF), jnp.float32)
        framed[:, : TH + 2 * HALF, TW + 2 * HALF :] = jnp.zeros(
            (2, TH + 2 * HALF, HALF), jnp.float32
        )

    def clear(i, carry):
        at = pl.ds(pl.multiple_of(i * 32, 32), 32)
        for k in range(PAT):
            for p in range(2):
                padded[k, p, at, :] = jnp.zeros((32, 640), jnp.float32)
        return carry

    def do_clear():
        lax.fori_loop(0, 24, clear, 0)

    def do_probe_in():
        local[0].wait()

    def do_meas_in():
        for copy in local[1:5]:
            copy.wait()

    def do_place_in():
        for copy in local[5:]:
            copy.wait()
        arrive(place_copy, range(OWN))
        arrive(count_copy, range(OWN))

    lives, tops, lefts, downs, overs = [], [], [], [], []

    def do_places():
        for k in range(PAT):
            a = lax.max(lax.min(pos[OWN, 0, k] - (row * TH - HALF), TH), 0)
            b = lax.max(lax.min(pos[OWN, 1, k] - (col * TW - HALF), TW), 0)
            lives.append(jnp.where(k < cnt[OWN, 0, 0], 1.0, 0.0).astype(jnp.float32))
            tops.append(lax.div(a, TILE))
            downs.append(lax.rem(a, TILE))
            lefts.append(lax.div(b, 128))
            overs.append(lax.rem(b, 128))

    def lane_iota(shape):
        return lax.broadcasted_iota(jnp.int32, shape, len(shape) - 1)

    def sub_iota(shape):
        return lax.broadcasted_iota(jnp.int32, shape, len(shape) - 2)

    def window(p, k, first, tiles):
        s, r = downs[k], overs[k]
        rows = pl.ds((tops[k] + first) * TILE, (tiles + 1) * TILE)
        turned = []
        for j in range(3):
            cols = pl.ds((lefts[k] + j) * 128, 128)
            turned.append(pltpu.roll(framed[p, rows, cols], lax.rem(128 - r, 128), 1))
        near = lane_iota(turned[0].shape) < 128 - r
        found = []
        for j in range(2):
            both = jnp.where(near, turned[j], turned[j + 1]).reshape(tiles + 1, TILE, 128)
            both = pltpu.roll(both, lax.rem(TILE - s, TILE), 1)
            upper = sub_iota((tiles, TILE, 128)) < TILE - s
            found.append(
                jnp.where(upper, both[:tiles], both[1:]).reshape(tiles * TILE, 128)
            )
        return found

    def lay(k, p, tiles, s, r):
        moved = []
        for x in tiles:
            x = pltpu.roll(x.reshape(N // TILE, TILE, 128), s, 1)
            none = jnp.zeros((1, TILE, 128), jnp.float32)
            here = jnp.concatenate([x, none], axis=0)
            above = jnp.concatenate([none, x], axis=0)
            y = jnp.where(sub_iota(here.shape) >= s, here, above).reshape(N + TILE, 128)
            moved.append(pltpu.roll(y, r, 1))
        right = lane_iota((N + TILE, 128)) >= r
        rows = pl.ds(N, N + TILE)
        padded[k, p, rows, pl.ds(128, 128)] = jnp.where(right, moved[0], 0.0)
        padded[k, p, rows, pl.ds(256, 128)] = jnp.where(right, moved[1], moved[0])
        padded[k, p, rows, pl.ds(384, 128)] = jnp.where(right, 0.0, moved[1])

    def collect(start, stop, pairs):
        size = 8

        def one(i, carry):
            first = i * size
            rows = pl.ds(pl.multiple_of(first * TILE, size * TILE), size * TILE)
            for q, p in pairs:
                for j in range(6):
                    total = None
                    for k in range(PAT):
                        at = (first - tops[k] + N // TILE) * TILE
                        lane = lax.max(lax.min(j - lefts[k] + 1, 4), 0) * 128
                        part = padded[
                            k, p, pl.ds(at, size * TILE), pl.ds(lane, 128)
                        ]
                        total = part if total is None else total + part
                    canvas[q, rows, pl.ds(j * 128, 128)] = total
            return carry

        lax.fori_loop(start // size, stop // size, one, 0)

    def do_power():
        for j in range(2):
            cols = pl.ds(128 * j, 128)
            power[j] = probe[0, :, cols] * probe[0, :, cols] + probe[1, :, cols] * probe[1, :, cols]
        ill[...] = jnp.zeros((TH, TW), jnp.float32)

    def light(t, carry):
        high, left = [], []
        for k in range(PAT):
            alive = jnp.where(k < cnt[t, 0, 0], 1.0, 0.0).astype(jnp.float32)
            a = lax.max(lax.min(pos[t, 0, k] - row * TH, 384), -384) + 384
            b = lax.max(lax.min(pos[t, 1, k] - col * TW, 896), -640) + 640
            lay(k, 0, [alive * power[j] for j in range(2)], lax.rem(a, TILE), lax.rem(b, 128))
            high.append(lax.div(a, TILE) - 80)
            left.append(lax.div(b, 128) - 5)
        size = 8
        for i in range(0, TH // TILE, size):
            rows = pl.ds(i * TILE, size * TILE)
            for j in range(4):
                total = ill[rows, pl.ds(j * 128, 128)]
                for k in range(PAT):
                    at = lax.max(lax.min(i - high[k], 96 - size), 0) * TILE
                    lane = lax.max(lax.min(j - left[k] + 1, 4), 0) * 128
                    total = total + padded[k, 0, pl.ds(at, size * TILE), pl.ds(lane, 128)]
                ill[rows, pl.ds(j * 128, 128)] = total
        return carry

    def do_light():
        lax.fori_loop(0, len(DIRS) + 1, light, 0)

    def do_peak():
        def largest(i, most):
            rows = pl.ds(pl.multiple_of(i * 32, 32), 32)
            for j in range(4):
                value = ill[rows, pl.ds(128 * j, 128)]
                most = jnp.maximum(most, jnp.max(value.reshape(4, TILE, 128), axis=0))
            return most

        peak = lax.fori_loop(0, TH // 32, largest, jnp.zeros((TILE, 128), jnp.float32))
        for c in range(CORES):
            w1[c, N:, :] = peak

    def do_turn():
        for k in range(PAT):
            meas_t[k] = meas[k].T

    def cut(i, carry):
        tiles = 4
        rows = pl.ds(pl.multiple_of(i * tiles * TILE, tiles * TILE), tiles * TILE)
        weight = [jnp.zeros((tiles * TILE, 128), jnp.float32)] * 2
        for k in range(PAT):
            real = window(0, k, i * tiles, tiles)
            imag = window(1, k, i * tiles, tiles)
            for j in range(2):
                cols = pl.ds(128 * j, 128)
                p_re, p_im = probe[0, rows, cols], probe[1, rows, cols]
                patches[k, 0, rows, cols] = real[j]
                patches[k, 1, rows, cols] = imag[j]
                exits[k, rows, cols] = (p_re * real[j] - p_im * imag[j]).astype(jnp.bfloat16)
                exits[k, rows, pl.ds(N + 128 * j, 128)] = (
                    p_re * imag[j] + p_im * real[j]
                ).astype(jnp.bfloat16)
                weight[j] = weight[j] + lives[k] * (real[j] * real[j] + imag[j] * imag[j])
        for j in range(2):
            w1[j, rows, :] = weight[j]
        return carry

    def do_cut():
        lax.fori_loop(0, 8, cut, 0)

    def dot(a, b):
        return jnp.dot(a, b, preferred_element_type=jnp.float32)

    def do_transforms(first, last):
        for k in range(first, last):
            half = dot(exits[k], fwd[...]).astype(jnp.bfloat16)
            halves[k, :N, :] = half[:, :N]
            halves[k, N:, :] = half[:, N:]
            spectrum = dot(inv[...], halves[k])
            re, im = spectrum[:N], spectrum[N:]
            factor = lives[k] * (1.0 - meas_t[k] * lax.rsqrt(re * re + im * im + 0.25))
            residues[k, :N, :] = (factor * re).astype(jnp.bfloat16)
            residues[k, N:, :] = (factor * im).astype(jnp.bfloat16)
            back = dot(fwd[...], residues[k]).astype(jnp.bfloat16)
            backs[k, :, :N] = back[:N]
            backs[k, :, N:] = back[N:]
            wave[k] = dot(backs[k], inv[...])

    def do_probe_sum():
        size = 32
        for i in range(N // size):
            rows = pl.ds(i * size, size)
            for j in range(2):
                cols = pl.ds(128 * j, 128)
                real = imag = None
                for k in range(PAT):
                    a, b = patches[k, 0, rows, cols], patches[k, 1, rows, cols]
                    u, v = wave[k, rows, cols], wave[k, rows, pl.ds(N + 128 * j, 128)]
                    one, two = a * u + b * v, a * v - b * u
                    real = one if real is None else real + one
                    imag = two if imag is None else imag + two
                part = pl.ds((i % 2) * size, size)
                g1[j, i // 2, part, :] = real
                g1[j, ZS // 2 + i // 2, part, :] = imag

    def owned(p, rows, at, h, j):
        size = rows.size
        inner = pl.ds(pl.multiple_of(HALF + h * HALF + at, 8), size)
        value = canvas[p, inner, pl.ds(128 * (j + 1), 128)]
        value = value + rx_v[1 - h, p, pl.ds(at, size), pl.ds(128 * j, 128)]
        if j in (0, 3):
            value = value + rx_h[1 if j == 0 else 0, p, inner, :]
        return value

    size = 32

    def send(src, dst, sem, peer):
        return remote(src, dst, red_send.at[sem], red_recv.at[sem], peer)

    def ahead(d):
        return lax.rem(z_at + d, ZS)

    def behind(d):
        return lax.rem(z_at + ZS - d, ZS)

    def w_core():
        return send(w1.at[1 - core], rxw1, 0, core_peer())

    def w_x(e):
        to = lax.rem(x_at + e, XS)
        return send(w2.at[to], rxw2.at[e - 1], e, x_peer(to))

    def g_core(d):
        return send(g1.at[1 - core, ahead(d)], rxg1.at[ahead(d)], 4 + d, core_peer())

    def g_x(d, e):
        to = lax.rem(x_at + e, XS)
        return send(g2.at[ahead(d), to], rxg2.at[e - 1, ahead(d)], 11 + 3 * d + e, x_peer(to))

    def z_copy(d):
        return send(s3.at[ahead(d)], rx3.at[d - 1], 35 + d, z_peer(ahead(d)))

    def y_copy(d):
        to = lax.rem(y_at + d, YS)
        return send(rx4.at[y_at], rx4.at[y_at], 42 + d, y_peer(to))

    def do_w_core_send():
        w_core().start()

    def do_w_core_sum():
        w_core().wait()
        part = N // XS
        crown = jnp.maximum(w1[core, N:, :], rxw1[N:, :])
        total = (w1[core, :N, :] + rxw1[:N, :]).reshape(ZS, XS, TILE, 128)
        for i in range(XS):
            w2[i, :part, :] = total[:, i].reshape(part, 128)
            w2[i, part:, :] = crown

    def do_w_x_send():
        for d in range(1, XS):
            w_x(d).start()

    def do_w_x_sum():
        for d in range(1, XS):
            w_x(d).wait()
        part = N // XS
        crown = w2[x_at, part:, :]
        for d in range(XS - 1):
            crown = jnp.maximum(crown, rxw2[d, part:, :])
        size = CHUNK - GCHUNK
        for i in range(ZS):
            at = pl.ds(i * size, size)
            s3[i, GCHUNK:CHUNK, :] = (w2[x_at, at, :] + rxw2[0, at, :]) + (
                rxw2[1, at, :] + rxw2[2, at, :]
            )
            s3[i, CHUNK:, :] = crown

    def do_core_send():
        for d in FAR:
            g_core(d).start()

    def do_core_sum():
        for d in FAR:
            g_core(d).wait()
            at = ahead(d)
            g2[at] = (g1[core, at] + rxg1[at]).reshape(XS, GCHUNK, 128)
            for e in range(1, XS):
                g_x(d, e).start()

    def do_x_sum():
        for d in FAR:
            for e in range(1, XS):
                g_x(d, e).wait()
            at = ahead(d)
            s3[at, :GCHUNK, :] = (g2[at, x_at] + rxg2[0, at]) + (rxg2[1, at] + rxg2[2, at])
            if d:
                z_copy(d).start()

    def do_z_sum():
        total = s3[z_at, :CHUNK, :]
        crown = s3[z_at, CHUNK:, :]
        for d in NEAR:
            z_copy(d).wait()
            total = total + rx3[d - 1, :CHUNK, :]
            crown = jnp.maximum(crown, rx3[d - 1, CHUNK:, :])
        rx4[y_at, :CHUNK, :] = total
        rx4[y_at, CHUNK:, :] = crown

    def do_y_send():
        for d in range(1, YS):
            y_copy(d).start()

    def do_y_sum():
        for d in range(1, YS):
            y_copy(d).wait()
        gathered[core, z_at, x_at] = (rx4[0, :CHUNK, :] + rx4[1, :CHUNK, :]) + (
            rx4[2, :CHUNK, :] + rx4[3, :CHUNK, :]
        )

    def z_back(d):
        mine = gathered.at[core, z_at, x_at]
        return send(mine, mine, 45 + d, z_peer(ahead(d)))

    def x_back(d, e):
        mine = gathered.at[core, behind(d), x_at]
        return send(mine, mine, 52 + 3 * d + e, x_peer(lax.rem(x_at + e, XS)))

    def core_back(d):
        mine = gathered.at[core, behind(d)]
        return send(mine, mine, 77 + d, core_peer())

    def do_z_back():
        for d in NEAR[::-1]:
            z_back(d).start()
        for e in range(1, XS):
            x_back(0, e).start()

    def do_x_back():
        for d in NEAR:
            z_back(d).wait()
            for e in range(1, XS):
                x_back(d, e).start()

    def do_core_back():
        for d in (0,) + NEAR:
            for e in range(1, XS):
                x_back(d, e).wait()
            core_back(d).start()

    def do_core_wait():
        for d in (0,) + NEAR:
            core_back(d).wait()

    def do_lay():
        for k in range(PAT):
            parts = ([], [])
            for j in range(2):
                cols = pl.ds(128 * j, 128)
                u, v = wave[k, :, cols], wave[k, :, pl.ds(N + 128 * j, 128)]
                p_re, p_im = probe[0, :, cols], probe[1, :, cols]
                parts[0].append(p_re * u + p_im * v)
                parts[1].append(p_re * v - p_im * u)
            for p in range(2):
                lay(k, p, parts[p], downs[k], overs[k])

    def do_collect(first, last):
        collect(first, last, [(0, 0), (1, 1)])

    def do_grad_corner():
        for n in diagonal:
            start_level(n)

    def do_grad_middle():
        start_middle(grad_v, grad_ends)

    def do_grad_relay():
        relay_middle(grad_ends)

    def do_grad_level():
        for n in level:
            start_level(n)

    def do_grad_forward():
        for n in diagonal:
            arrive_level(n)
        for dr in (-1, 1):
            rows = margin(dr, TH)
            for dc in (-1, 1):
                cols = shifted(edge(dc, TW))
                canvas[:, rows, cols] = canvas[:, rows, cols] + rx_h[(1 - dc) // 2, :, rows, :]
        start(grad_v, vertical, 0)
        start(grad_v, vertical, 1)

    def do_grad_wait():
        for n in level:
            arrive_level(n)
        for part in range(2):
            arrive(grad_v, vertical, part)
        arrive_middle(grad_v, grad_ends)

    def do_object():
        crown = jnp.maximum(
            jnp.maximum(rx4[0, CHUNK:, :], rx4[1, CHUNK:, :]),
            jnp.maximum(rx4[2, CHUNK:, :], rx4[3, CHUNK:, :]),
        )
        top = jnp.max(crown)
        for h in range(2):

            def renew(i, carry, h=h):
                at = pl.multiple_of(i * size, size)
                rows = pl.ds(pl.multiple_of(h * HALF + at, size), size)
                inner = pl.ds(pl.multiple_of(HALF + h * HALF + at, 8), size)
                for j in range(4):
                    cols = pl.ds(128 * (j + 1), 128)
                    share = 1.0 / (0.75 * ill[rows, pl.ds(128 * j, 128)] + 0.25 * top)
                    for p in range(2):
                        obj_new[p, rows, pl.ds(128 * j, 128)] = (
                            framed[p, inner, cols] - owned(p, rows, at, h, j) * share
                        )
                return carry

            lax.fori_loop(0, HALF // size, renew, 0)

    def do_probe():
        weight = [gathered[j, :, :, GCHUNK:, :].reshape(N, 128) for j in range(2)]
        heavy = jnp.maximum(jnp.max(weight[0]), jnp.max(weight[1]))
        for j in range(2):
            cols = pl.ds(128 * j, 128)
            share = 1.0 / (0.75 * weight[j] + 0.25 * heavy)
            for p in range(2):
                half = ZS // 2
                total = gathered[j, half * p : half * (p + 1), :, :GCHUNK, :].reshape(N, 128)
                probe_new[p, :, cols] = probe[p, :, cols] - total * share

    do_barrier()
    do_place_send()
    do_halo_send()
    do_margins()
    do_clear()
    do_probe_in()
    do_power()
    do_place_in()
    do_places()
    do_light()
    do_peak()
    do_halo_forward()
    do_meas_in()
    do_turn()
    do_halo_relay()
    do_halo_wait()
    do_cut()
    do_w_core_send()
    do_transforms(0, 2)
    do_w_core_sum()
    do_w_x_send()
    do_transforms(2, 4)
    do_probe_sum()
    do_core_send()
    do_lay()
    do_w_x_sum()
    do_core_sum()
    do_collect(0, 64)
    do_grad_middle()
    do_x_sum()
    do_grad_corner()
    do_grad_level()
    do_z_sum()
    do_y_send()
    do_grad_relay()
    do_y_sum()
    do_z_back()
    do_grad_forward()
    do_x_back()
    do_core_back()
    do_grad_wait()
    do_object()
    do_core_wait()
    do_probe()


def body(object_field, probe, measured, positions, counts):
    forward, inverse = tables(N)
    any_space = pl.BlockSpec(memory_space=pl.ANY)
    vmem = pl.BlockSpec(memory_space=pltpu.VMEM)
    f32 = jnp.float32
    bf16 = jnp.bfloat16
    red = 85
    dma = pltpu.SemaphoreType.DMA
    return pl.pallas_call(
        kernel,
        out_shape=(pltpu.VMEM((2, TH, TW), f32), pltpu.VMEM((2, N, N), f32)),
        in_specs=[any_space] * 7,
        out_specs=(vmem, vmem),
        scratch_shapes=[
            pltpu.SMEM((OWN + 1, 2, PAT), jnp.int32),
            pltpu.SMEM((OWN + 1, 1, 1), jnp.int32),
            pltpu.VMEM((2, TH + 2 * HALF + TILE, TW + 3 * HALF), f32),
            pltpu.VMEM((2, N, N), f32),
            pltpu.VMEM((2, N, 128), f32),
            pltpu.VMEM((TH, TW), f32),
            pltpu.VMEM((PAT, N, N), f32),
            pltpu.VMEM((PAT, N, N), f32),
            pltpu.VMEM((2 * N, 2 * N), bf16),
            pltpu.VMEM((2 * N, 2 * N), bf16),
            pltpu.VMEM((PAT, 2, 3 * N, 640), f32),
            pltpu.VMEM((2, TH + 2 * HALF, TW + 2 * HALF), f32),
            pltpu.VMEM((2, 2, HALF, TW), f32),
            pltpu.VMEM((2, 2, TH + 2 * HALF, HALF), f32),
            pltpu.VMEM((PAT, 2, N, N), f32),
            pltpu.VMEM((PAT, N, 2 * N), f32),
            pltpu.VMEM((PAT, N, 2 * N), bf16),
            pltpu.VMEM((PAT, 2 * N, N), bf16),
            pltpu.VMEM((PAT, 2 * N, N), bf16),
            pltpu.VMEM((PAT, N, 2 * N), bf16),
            pltpu.VMEM((CORES, N + TILE, 128), f32),
            pltpu.VMEM((N + TILE, 128), f32),
            pltpu.VMEM((XS, N // XS + TILE, 128), f32),
            pltpu.VMEM((XS - 1, N // XS + TILE, 128), f32),
            pltpu.VMEM((CORES, ZS, 2 * N // ZS, 128), f32),
            pltpu.VMEM((ZS, 2 * N // ZS, 128), f32),
            pltpu.VMEM((ZS, XS, GCHUNK, 128), f32),
            pltpu.VMEM((XS - 1, ZS, GCHUNK, 128), f32),
            pltpu.VMEM((ZS, CHUNK + TILE, 128), f32),
            pltpu.VMEM((ZS - 1, CHUNK + TILE, 128), f32),
            pltpu.VMEM((YS, CHUNK + TILE, 128), f32),
            pltpu.VMEM((CORES, ZS, XS, CHUNK, 128), f32),
            dma((7,)),
            dma((OWN,)),
            dma((OWN,)),
            dma((OWN,)),
            dma((OWN,)),
            pltpu.VMEM((2, HALF, TW - 2 * HALF), f32),
            pltpu.VMEM((2, HALF, TW - 2 * HALF), f32),
            dma((8,)),
            dma((8,)),
            dma((12,)),
            dma((12,)),
            dma((12,)),
            dma((12,)),
            dma((red,)),
            dma((red,)),
        ],
        compiler_params=pltpu.CompilerParams(
            collective_id=0, has_side_effects=True, vmem_limit_bytes=56 * 1024 * 1024
        ),
    )(
        positions.reshape(PAT, 2).T,
        counts,
        object_field,
        probe,
        measured.reshape(PAT, N, N),
        jnp.asarray(forward),
        jnp.asarray(inverse),
    )


def solution(mesh):
    in_specs = (
        P(None, "row", "col"),
        P(),
        P("row", "col", None, None, None),
        P("row", "col", None, None),
        P("row", "col"),
    )
    out_specs = (P(None, "row", "col"), P())
    return jax.shard_map(body, mesh=mesh, in_specs=in_specs, out_specs=out_specs, check_vma=False)
```

```python
import functools

import jax
import jax.numpy as jnp
import ml_dtypes
import numpy as np
from jax import lax
from jax.experimental import pallas as pl
from jax.experimental.pallas import tpu as pltpu
from jax.sharding import PartitionSpec as P

N = 256
HALF = 128
TH = 256
TW = 512
PAT = 4
CORES = 2
XS = 4
ZS = 8
YS = 4
GCHUNK = 16
CHUNK = 24
TILE = 8
DIRS = [(-1, 0), (1, 0), (0, -1), (0, 1), (-1, -1), (-1, 1), (1, -1), (1, 1)]
OWN = len(DIRS)
NEAR = (1, 7, 2, 6, 3, 5, 4)
FAR = NEAR[::-1] + (0,)
MESH = pl.DeviceIdType.MESH


def tables(extent):
    indices = np.arange(extent, dtype=np.int32)
    products = indices[:, None] * indices[None, :] % extent
    angles = 2.0 * np.pi / extent * products.astype(np.float64)
    cosine = np.cos(angles) / np.sqrt(float(extent))
    sine_part = np.sin(angles) / np.sqrt(float(extent))
    forward = np.block([[cosine, -sine_part], [sine_part, cosine]])
    inverse = np.block([[cosine, sine_part], [-sine_part, cosine]])
    return (
        forward.astype(np.float32).astype(ml_dtypes.bfloat16),
        inverse.astype(np.float32).astype(ml_dtypes.bfloat16),
    )


def edge(step, size):
    if step == 0:
        return pl.ds(0, size)
    return pl.ds(0 if step < 0 else size - HALF, HALF)


def margin(step, size):
    if step == 0:
        return pl.ds(HALF, size)
    return pl.ds(0 if step < 0 else size + HALF, HALF)


def kernel(
    pos_in,
    cnt_in,
    obj,
    probe_in,
    meas_in,
    fwd_in,
    inv_in,
    obj_new,
    probe_new,
    pos,
    cnt,
    framed,
    probe,
    power,
    ill,
    meas,
    meas_t,
    fwd,
    inv,
    padded,
    canvas,
    rx_v,
    rx_h,
    patches,
    wave,
    exits,
    halves,
    residues,
    backs,
    w1,
    rxw1,
    w2,
    rxw2,
    g1,
    rxg1,
    g2,
    rxg2,
    s3,
    rx3,
    rx4,
    gathered,
    local_sem,
    pos_send,
    pos_recv,
    cnt_send,
    cnt_recv,
    halo_relay,
    grad_relay,
    halo_hop,
    grad_hop,
    halo_send,
    halo_recv,
    grad_send,
    grad_recv,
    red_send,
    red_recv,
):
    row = lax.axis_index("row")
    col = lax.axis_index("col")
    core = lax.rem(col, CORES)
    x_at = (row // YS) * 2 + lax.rem(col // 2, 2)
    z_at = col // 4
    y_at = lax.rem(row, YS)

    def core_peer():
        return (row, col + 1 - 2 * core)

    def x_peer(i):
        return ((i // 2) * YS + y_at, z_at * 4 + lax.rem(i, 2) * 2 + core)

    def z_peer(i):
        return (row, i * 4 + lax.rem(col, 4))

    def y_peer(i):
        return ((row // YS) * YS + i, col)

    def exists(step):
        near_row, near_col = row + step[0], col + step[1]
        conds = []
        if step[0] < 0:
            conds.append(near_row >= 0)
        if step[0] > 0:
            conds.append(near_row < lax.axis_size("row"))
        if step[1] < 0:
            conds.append(near_col >= 0)
        if step[1] > 0:
            conds.append(near_col < lax.axis_size("col"))
        return functools.reduce(jnp.logical_and, conds)

    center = (slice(None), pl.ds(HALF, TH), pl.ds(HALF, TW))
    local = [
        pltpu.make_async_copy(probe_in, probe, local_sem.at[0]),
        pltpu.make_async_copy(meas_in, meas, local_sem.at[1]),
        pltpu.make_async_copy(fwd_in, fwd, local_sem.at[2]),
        pltpu.make_async_copy(inv_in, inv, local_sem.at[3]),
        pltpu.make_async_copy(obj, framed.at[center], local_sem.at[4]),
        pltpu.make_async_copy(pos_in, pos.at[OWN], local_sem.at[5]),
        pltpu.make_async_copy(cnt_in, cnt.at[OWN], local_sem.at[6]),
    ]

    def do_barrier():
        barrier = pltpu.get_barrier_semaphore()
        greeted = jnp.int32(0)
        for step in DIRS:
            there = exists(step)

            @pl.when(there)
            def _():
                pl.semaphore_signal(
                    barrier, inc=1, device_id=(row + step[0], col + step[1]), device_id_type=MESH
                )

            greeted = greeted + there.astype(jnp.int32)
        pl.semaphore_signal(barrier, inc=1, device_id=core_peer(), device_id_type=MESH)
        for d in range(1, XS):
            pl.semaphore_signal(
                barrier, inc=1, device_id=x_peer(lax.rem(x_at + d, XS)), device_id_type=MESH
            )
        for d in range(1, ZS):
            pl.semaphore_signal(
                barrier, inc=1, device_id=z_peer(lax.rem(z_at + d, ZS)), device_id_type=MESH
            )
        for d in range(1, YS):
            pl.semaphore_signal(
                barrier, inc=1, device_id=y_peer(lax.rem(y_at + d, YS)), device_id_type=MESH
            )
        for n in vertical:
            near_end, relay_row, far_end = route(n)

            @pl.when(row == far_end)
            def _():
                pl.semaphore_signal(
                    barrier, inc=1, device_id=across(relay_row), device_id_type=MESH
                )

            greeted = greeted + (row == relay_row).astype(jnp.int32)
        for copy in local[:1] + local[5:]:
            copy.start()
        pl.semaphore_wait(barrier, greeted + (CORES - 1 + XS - 1 + ZS - 1 + YS - 1))

    def near(dr, dc):
        return (row + dr, col + dc)

    def remote(src, dst, send_sem, recv_sem, peer):
        return pltpu.make_async_remote_copy(
            src_ref=src,
            dst_ref=dst,
            send_sem=send_sem,
            recv_sem=recv_sem,
            device_id=peer,
            device_id_type=MESH,
        )

    def opposite(n):
        return DIRS.index((-DIRS[n][0], -DIRS[n][1]))

    def place_copy(n):
        return remote(pos_in, pos.at[opposite(n)], pos_send.at[n], pos_recv.at[n], near(*DIRS[n]))

    def count_copy(n):
        return remote(cnt_in, cnt.at[opposite(n)], cnt_send.at[n], cnt_recv.at[n], near(*DIRS[n]))

    strips = [pl.ds(0, HALF), pl.ds(TW - HALF, HALF), pl.ds(HALF, TW - 2 * HALF)]

    def shifted(cols):
        return pl.ds(cols.start + HALF, cols.size)

    def halo_v(n, part):
        dr = DIRS[n][0]
        sem = n * 3 + part
        return remote(
            obj.at[:, edge(dr, TH), strips[part]],
            framed.at[:, margin(-dr, TH), shifted(strips[part])],
            halo_send.at[sem],
            halo_recv.at[sem],
            near(dr, 0),
        )

    def halo_h(n):
        dc = DIRS[n][1]
        return remote(
            obj.at[:, :, edge(dc, TW)],
            framed.at[:, pl.ds(HALF, TH), margin(-dc, TW)],
            halo_send.at[4 + n],
            halo_recv.at[4 + n],
            near(0, dc),
        )

    def halo_c(n):
        dr, dc = DIRS[n]
        return remote(
            framed.at[:, margin(-dr, TH), shifted(edge(dc, TW))],
            framed.at[:, margin(-dr, TH), margin(-dc, TW)],
            halo_send.at[4 + n],
            halo_recv.at[4 + n],
            near(0, dc),
        )

    def grad_v(n, part):
        dr = DIRS[n][0]
        sem = n * 3 + part
        return remote(
            canvas.at[:, margin(dr, TH), shifted(strips[part])],
            rx_v.at[(dr + 1) // 2, :, :, strips[part]],
            grad_send.at[sem],
            grad_recv.at[sem],
            near(dr, 0),
        )

    def grad_h(n):
        dr, dc = DIRS[n]
        rows = margin(dr, TH)
        return remote(
            canvas.at[:, rows, margin(dc, TW)],
            rx_h.at[(dc + 1) // 2, :, rows],
            grad_send.at[4 + n],
            grad_recv.at[4 + n],
            near(0, dc),
        )

    vertical, level, diagonal = (0, 1), (2, 3), (4, 5, 6, 7)

    def start(make, order, *more):
        for n in order:

            @pl.when(exists(DIRS[n]))
            def _():
                make(n, *more).start()

    def arrive(make, order, *more):
        for n in order:

            @pl.when(exists(DIRS[n]))
            def _():
                make(n, *more).wait_send()

            @pl.when(exists(DIRS[opposite(n)]))
            def _():
                make(n, *more).wait_recv()

    def start_level(n):
        @pl.when(exists((0, DIRS[n][1])))
        def _():
            grad_h(n).start()

    def arrive_level(n):
        @pl.when(exists((0, DIRS[n][1])))
        def _():
            grad_h(n).wait_send()

        @pl.when(exists((0, -DIRS[n][1])))
        def _():
            grad_h(n).wait_recv()

    def do_place_send():
        start(place_copy, range(OWN))
        start(count_copy, range(OWN))

    def route(n):
        return (3, 7, 4) if DIRS[n][0] > 0 else (4, 0, 3)

    def across(i):
        return (i, col + 2 - 4 * lax.rem(col // 2, 2))

    def leg_one(n, p, src, buf, sems):
        return remote(src, buf.at[p], sems.at[p], sems.at[2 + p], across(route(n)[1]))

    def leg_two(n, p, dst, buf, sems):
        return remote(buf.at[p], dst, sems.at[4 + p], sems.at[6 + p], across(route(n)[2]))

    def halo_ends(n, p):
        dr = DIRS[n][0]
        src = obj.at[p, edge(dr, TH), strips[2]]
        return src, framed.at[p, margin(-dr, TH), shifted(strips[2])], halo_relay, halo_hop

    def grad_ends(n, p):
        dr = DIRS[n][0]
        src = canvas.at[p, margin(dr, TH), shifted(strips[2])]
        return src, rx_v.at[(dr + 1) // 2, p, :, strips[2]], grad_relay, grad_hop

    def first_leg(n, p, ends):
        src, dst, buf, sems = ends(n, p)
        return leg_one(n, p, src, buf, sems)

    def second_leg(n, p, ends):
        src, dst, buf, sems = ends(n, p)
        return leg_two(n, p, dst, buf, sems)

    def start_legs(ends):
        for n in vertical:

            @pl.when(row == route(n)[0])
            def _():
                for p in range(2):
                    first_leg(n, p, ends).start()

    def start_middle(direct):
        for n in vertical:

            @pl.when(exists(DIRS[n]) & (row != route(n)[0]))
            def _():
                direct(n, 2).start()

    def relay_middle(p, ends):
        for n in vertical:

            @pl.when(row == route(n)[1])
            def _():
                first_leg(n, p, ends).wait_recv()
                second_leg(n, p, ends).start()

    def arrive_middle(direct, ends):
        for n in vertical:

            @pl.when(row == route(n)[0])
            def _():
                for p in range(2):
                    first_leg(n, p, ends).wait_send()

            @pl.when(exists(DIRS[n]) & (row != route(n)[0]))
            def _():
                direct(n, 2).wait_send()

            @pl.when(row == route(n)[1])
            def _():
                for p in range(2):
                    second_leg(n, p, ends).wait_send()

            @pl.when(row == route(n)[2])
            def _():
                for p in range(2):
                    second_leg(n, p, ends).wait_recv()

            @pl.when(exists(DIRS[opposite(n)]) & (row != route(n)[2]))
            def _():
                direct(n, 2).wait_recv()

    def do_halo_send():
        start(halo_v, vertical, 0)
        start(halo_v, vertical, 1)
        for n in diagonal:

            @pl.when(direct_from(n))
            def _():
                halo_d(n).start()

        start(halo_h, level)

    def do_halo_middle():
        start_legs(halo_ends)
        start_middle(halo_v)

    def halo_d(n):
        dr, dc = DIRS[n]
        return remote(
            obj.at[:, edge(dr, TH), edge(dc, TW)],
            framed.at[:, margin(-dr, TH), margin(-dc, TW)],
            halo_send.at[8 + n],
            halo_recv.at[8 + n],
            near(dr, dc),
        )

    def leaves(dc):
        return core == (1 if dc > 0 else 0)

    def direct_from(n):
        return (row == (2 if DIRS[n][0] > 0 else 5)) & exists((0, DIRS[n][1])) & leaves(DIRS[n][1])

    def direct_to(n):
        dr, dc = DIRS[n]
        return (row == (3 if dr > 0 else 4)) & exists((0, -dc)) & leaves(-dc)

    def handed_from(n):
        dr, dc = DIRS[n]
        apart = (row == (3 if dr > 0 else 4)) & leaves(dc)
        return exists((-dr, dc)) & jnp.logical_not(apart)

    def handed_to(n):
        dr, dc = DIRS[n]
        return exists((-dr, -dc)) & jnp.logical_not(direct_to(n))

    def do_halo_forward():
        arrive(halo_v, vertical, 0)
        arrive(halo_v, vertical, 1)
        for n in diagonal:

            @pl.when(handed_from(n))
            def _():
                halo_c(n).start()

    def do_halo_relay(p):
        relay_middle(p, halo_ends)

    def do_halo_wait():
        arrive(halo_h, level)
        arrive_middle(halo_v, halo_ends)
        for n in diagonal:

            @pl.when(handed_from(n))
            def _():
                halo_c(n).wait_send()

            @pl.when(handed_to(n))
            def _():
                halo_c(n).wait_recv()

            @pl.when(direct_from(n))
            def _():
                halo_d(n).wait_send()

            @pl.when(direct_to(n))
            def _():
                halo_d(n).wait_recv()

    def do_local():
        for copy in local[1:5]:
            copy.start()

    def do_margins():
        for n in range(OWN):
            dr, dc = DIRS[n]

            @pl.when(jnp.logical_not(exists(DIRS[n])))
            def _():
                rows, cols = margin(dr, TH), margin(dc, TW)
                framed[:, rows, cols] = jnp.zeros((2, rows.size, cols.size), jnp.float32)
                cnt[n, 0, 0] = 0
                for k in range(PAT):
                    pos[n, 0, k] = 0
                    pos[n, 1, k] = 0

        for n in vertical:

            @pl.when(jnp.logical_not(exists(DIRS[n])))
            def _():
                rx_v[1 - n] = jnp.zeros((2, HALF, TW), jnp.float32)

        for n in level:

            @pl.when(jnp.logical_not(exists(DIRS[n])))
            def _():
                rx_h[3 - n] = jnp.zeros((2, TH + 2 * HALF, HALF), jnp.float32)

        framed[:, TH + 2 * HALF :, :] = jnp.zeros((2, TILE, TW + 3 * HALF), jnp.float32)
        framed[:, : TH + 2 * HALF, TW + 2 * HALF :] = jnp.zeros(
            (2, TH + 2 * HALF, HALF), jnp.float32
        )

    def clear(i, carry):
        at = pl.ds(pl.multiple_of(i * 32, 32), 32)
        for k in range(PAT):
            for p in range(2):
                padded[k, p, at, :] = jnp.zeros((32, 640), jnp.float32)
        return carry

    def do_clear():
        lax.fori_loop(0, 24, clear, 0)

    def do_probe_in():
        local[0].wait()

    def do_meas_in():
        for copy in local[1:5]:
            copy.wait()

    def do_place_in():
        for copy in local[5:]:
            copy.wait()
        arrive(place_copy, range(OWN))
        arrive(count_copy, range(OWN))

    lives, tops, lefts, downs, overs = [], [], [], [], []

    def do_places():
        for k in range(PAT):
            a = lax.max(lax.min(pos[OWN, 0, k] - (row * TH - HALF), TH), 0)
            b = lax.max(lax.min(pos[OWN, 1, k] - (col * TW - HALF), TW), 0)
            lives.append(jnp.where(k < cnt[OWN, 0, 0], 1.0, 0.0).astype(jnp.float32))
            tops.append(lax.div(a, TILE))
            downs.append(lax.rem(a, TILE))
            lefts.append(lax.div(b, 128))
            overs.append(lax.rem(b, 128))

    def lane_iota(shape):
        return lax.broadcasted_iota(jnp.int32, shape, len(shape) - 1)

    def sub_iota(shape):
        return lax.broadcasted_iota(jnp.int32, shape, len(shape) - 2)

    def window(p, k, first, tiles):
        s, r = downs[k], overs[k]
        rows = pl.ds((tops[k] + first) * TILE, (tiles + 1) * TILE)
        turned = []
        for j in range(3):
            cols = pl.ds((lefts[k] + j) * 128, 128)
            turned.append(pltpu.roll(framed[p, rows, cols], lax.rem(128 - r, 128), 1))
        near = lane_iota(turned[0].shape) < 128 - r
        found = []
        for j in range(2):
            both = jnp.where(near, turned[j], turned[j + 1]).reshape(tiles + 1, TILE, 128)
            both = pltpu.roll(both, lax.rem(TILE - s, TILE), 1)
            upper = sub_iota((tiles, TILE, 128)) < TILE - s
            found.append(
                jnp.where(upper, both[:tiles], both[1:]).reshape(tiles * TILE, 128)
            )
        return found

    def lay(k, p, tiles, s, r):
        moved = []
        for x in tiles:
            x = pltpu.roll(x.reshape(N // TILE, TILE, 128), s, 1)
            none = jnp.zeros((1, TILE, 128), jnp.float32)
            here = jnp.concatenate([x, none], axis=0)
            above = jnp.concatenate([none, x], axis=0)
            y = jnp.where(sub_iota(here.shape) >= s, here, above).reshape(N + TILE, 128)
            moved.append(pltpu.roll(y, r, 1))
        right = lane_iota((N + TILE, 128)) >= r
        rows = pl.ds(N, N + TILE)
        padded[k, p, rows, pl.ds(128, 128)] = jnp.where(right, moved[0], 0.0)
        padded[k, p, rows, pl.ds(256, 128)] = jnp.where(right, moved[1], moved[0])
        padded[k, p, rows, pl.ds(384, 128)] = jnp.where(right, 0.0, moved[1])

    def collect(start, stop, pairs):
        size = 8

        def one(i, carry):
            first = i * size
            rows = pl.ds(pl.multiple_of(first * TILE, size * TILE), size * TILE)
            for q, p in pairs:
                for j in range(6):
                    total = None
                    for k in range(PAT):
                        at = (first - tops[k] + N // TILE) * TILE
                        lane = lax.max(lax.min(j - lefts[k] + 1, 4), 0) * 128
                        part = padded[
                            k, p, pl.ds(at, size * TILE), pl.ds(lane, 128)
                        ]
                        total = part if total is None else total + part
                    canvas[q, rows, pl.ds(j * 128, 128)] = total
            return carry

        lax.fori_loop(start // size, stop // size, one, 0)

    def do_power():
        for j in range(2):
            cols = pl.ds(128 * j, 128)
            power[j] = probe[0, :, cols] * probe[0, :, cols] + probe[1, :, cols] * probe[1, :, cols]
        ill[...] = jnp.zeros((TH, TW), jnp.float32)

    def light(t, carry):
        high, left = [], []
        for k in range(PAT):
            alive = jnp.where(k < cnt[t, 0, 0], 1.0, 0.0).astype(jnp.float32)
            a = lax.max(lax.min(pos[t, 0, k] - row * TH, 384), -384) + 384
            b = lax.max(lax.min(pos[t, 1, k] - col * TW, 896), -640) + 640
            lay(k, 0, [alive * power[j] for j in range(2)], lax.rem(a, TILE), lax.rem(b, 128))
            high.append(lax.div(a, TILE) - 80)
            left.append(lax.div(b, 128) - 5)
        size = 8
        for i in range(0, TH // TILE, size):
            rows = pl.ds(i * TILE, size * TILE)
            for j in range(4):
                total = ill[rows, pl.ds(j * 128, 128)]
                for k in range(PAT):
                    at = lax.max(lax.min(i - high[k], 96 - size), 0) * TILE
                    lane = lax.max(lax.min(j - left[k] + 1, 4), 0) * 128
                    total = total + padded[k, 0, pl.ds(at, size * TILE), pl.ds(lane, 128)]
                ill[rows, pl.ds(j * 128, 128)] = total
        return carry

    def do_light():
        lax.fori_loop(0, len(DIRS) + 1, light, 0)

    def do_peak():
        def largest(i, most):
            rows = pl.ds(pl.multiple_of(i * 32, 32), 32)
            for j in range(4):
                value = ill[rows, pl.ds(128 * j, 128)]
                most = jnp.maximum(most, jnp.max(value.reshape(4, TILE, 128), axis=0))
            return most

        peak = lax.fori_loop(0, TH // 32, largest, jnp.zeros((TILE, 128), jnp.float32))
        for c in range(CORES):
            w1[c, N:, :] = peak

    def do_turn():
        for k in range(PAT):
            meas_t[k] = meas[k].T

    def cut(i, carry):
        tiles = 4
        rows = pl.ds(pl.multiple_of(i * tiles * TILE, tiles * TILE), tiles * TILE)
        weight = [jnp.zeros((tiles * TILE, 128), jnp.float32)] * 2
        for k in range(PAT):
            real = window(0, k, i * tiles, tiles)
            imag = window(1, k, i * tiles, tiles)
            for j in range(2):
                cols = pl.ds(128 * j, 128)
                p_re, p_im = probe[0, rows, cols], probe[1, rows, cols]
                patches[k, 0, rows, cols] = real[j]
                patches[k, 1, rows, cols] = imag[j]
                exits[k, rows, cols] = (p_re * real[j] - p_im * imag[j]).astype(jnp.bfloat16)
                exits[k, rows, pl.ds(N + 128 * j, 128)] = (
                    p_re * imag[j] + p_im * real[j]
                ).astype(jnp.bfloat16)
                weight[j] = weight[j] + lives[k] * (real[j] * real[j] + imag[j] * imag[j])
        for j in range(2):
            w1[j, rows, :] = weight[j]
        return carry

    def do_cut():
        lax.fori_loop(0, 8, cut, 0)

    def dot(a, b):
        return jnp.dot(a, b, preferred_element_type=jnp.float32)

    def do_transforms(first, last):
        for k in range(first, last):
            half = dot(exits[k], fwd[...]).astype(jnp.bfloat16)
            halves[k, :N, :] = half[:, :N]
            halves[k, N:, :] = half[:, N:]
            spectrum = dot(inv[...], halves[k])
            re, im = spectrum[:N], spectrum[N:]
            factor = lives[k] * (1.0 - meas_t[k] * lax.rsqrt(re * re + im * im + 0.25))
            residues[k, :N, :] = (factor * re).astype(jnp.bfloat16)
            residues[k, N:, :] = (factor * im).astype(jnp.bfloat16)
            back = dot(fwd[...], residues[k]).astype(jnp.bfloat16)
            backs[k, :, :N] = back[:N]
            backs[k, :, N:] = back[N:]
            wave[k] = dot(backs[k], inv[...])

    def do_probe_sum():
        size = 32
        for i in range(N // size):
            rows = pl.ds(i * size, size)
            for j in range(2):
                cols = pl.ds(128 * j, 128)
                real = imag = None
                for k in range(PAT):
                    a, b = patches[k, 0, rows, cols], patches[k, 1, rows, cols]
                    u, v = wave[k, rows, cols], wave[k, rows, pl.ds(N + 128 * j, 128)]
                    one, two = a * u + b * v, a * v - b * u
                    real = one if real is None else real + one
                    imag = two if imag is None else imag + two
                part = pl.ds((i % 2) * size, size)
                g1[j, i // 2, part, :] = real
                g1[j, ZS // 2 + i // 2, part, :] = imag

    def owned(p, rows, at, h, j):
        size = rows.size
        inner = pl.ds(pl.multiple_of(HALF + h * HALF + at, 8), size)
        value = canvas[p, inner, pl.ds(128 * (j + 1), 128)]
        value = value + rx_v[1 - h, p, pl.ds(at, size), pl.ds(128 * j, 128)]
        if j in (0, 3):
            value = value + rx_h[1 if j == 0 else 0, p, inner, :]
        return value

    size = 32

    def send(src, dst, sem, peer):
        return remote(src, dst, red_send.at[sem], red_recv.at[sem], peer)

    def ahead(d):
        return lax.rem(z_at + d, ZS)

    def behind(d):
        return lax.rem(z_at + ZS - d, ZS)

    def w_core():
        return send(w1.at[1 - core], rxw1, 0, core_peer())

    def w_y(e):
        to = lax.rem(y_at + e, YS)
        return send(w2.at[to], rxw2.at[e - 1], e, y_peer(to))

    def g_core(d):
        return send(g1.at[1 - core, ahead(d)], rxg1.at[ahead(d)], 4 + d, core_peer())

    def g_y(d, e):
        to = lax.rem(y_at + e, YS)
        return send(g2.at[ahead(d), to], rxg2.at[e - 1, ahead(d)], 11 + 3 * d + e, y_peer(to))

    def z_copy(d):
        return send(s3.at[ahead(d)], rx3.at[d - 1], 35 + d, z_peer(ahead(d)))

    def x_copy(d):
        to = lax.rem(x_at + d, XS)
        return send(rx4.at[x_at], rx4.at[x_at], 42 + d, x_peer(to))

    def do_w_core_send():
        w_core().start()

    def do_w_core_sum():
        w_core().wait()
        part = N // YS
        crown = jnp.maximum(w1[core, N:, :], rxw1[N:, :])
        total = (w1[core, :N, :] + rxw1[:N, :]).reshape(ZS, YS, TILE, 128)
        for i in range(YS):
            w2[i, :part, :] = total[:, i].reshape(part, 128)
            w2[i, part:, :] = crown

    def do_w_y_send():
        for d in range(1, YS):
            w_y(d).start()

    def do_w_y_sum():
        for d in range(1, YS):
            w_y(d).wait()
        part = N // YS
        crown = w2[y_at, part:, :]
        for d in range(YS - 1):
            crown = jnp.maximum(crown, rxw2[d, part:, :])
        size = CHUNK - GCHUNK
        for i in range(ZS):
            at = pl.ds(i * size, size)
            s3[i, GCHUNK:CHUNK, :] = (w2[y_at, at, :] + rxw2[0, at, :]) + (
                rxw2[1, at, :] + rxw2[2, at, :]
            )
            s3[i, CHUNK:, :] = crown

    def do_core_send():
        for d in FAR:
            g_core(d).start()

    def do_core_sum():
        for d in FAR:
            g_core(d).wait()
            at = ahead(d)
            g2[at] = (g1[core, at] + rxg1[at]).reshape(YS, GCHUNK, 128)
            for e in range(1, YS):
                g_y(d, e).start()

    def do_y_sum():
        for d in FAR:
            for e in range(1, YS):
                g_y(d, e).wait()
            at = ahead(d)
            s3[at, :GCHUNK, :] = (g2[at, y_at] + rxg2[0, at]) + (rxg2[1, at] + rxg2[2, at])
            if d:
                z_copy(d).start()

    def do_z_sum():
        total = s3[z_at, :CHUNK, :]
        crown = s3[z_at, CHUNK:, :]
        for d in NEAR:
            z_copy(d).wait()
            total = total + rx3[d - 1, :CHUNK, :]
            crown = jnp.maximum(crown, rx3[d - 1, CHUNK:, :])
        rx4[x_at, :CHUNK, :] = total
        rx4[x_at, CHUNK:, :] = crown

    def do_x_send():
        for d in range(1, XS):
            x_copy(d).start()

    def do_x_sum():
        for d in range(1, XS):
            x_copy(d).wait()
        gathered[core, z_at, y_at] = (rx4[0, :CHUNK, :] + rx4[1, :CHUNK, :]) + (
            rx4[2, :CHUNK, :] + rx4[3, :CHUNK, :]
        )

    def z_back(d):
        mine = gathered.at[core, z_at, y_at]
        return send(mine, mine, 45 + d, z_peer(ahead(d)))

    def y_back(d, e):
        mine = gathered.at[core, behind(d), y_at]
        return send(mine, mine, 52 + 3 * d + e, y_peer(lax.rem(y_at + e, YS)))

    def core_back(d):
        mine = gathered.at[core, behind(d)]
        return send(mine, mine, 77 + d, core_peer())

    def do_z_back():
        for d in NEAR[::-1]:
            z_back(d).start()
        for e in range(1, YS):
            y_back(0, e).start()

    def do_y_back():
        for d in NEAR:
            z_back(d).wait()
            for e in range(1, YS):
                y_back(d, e).start()

    def do_core_back():
        for d in (0,) + NEAR:
            for e in range(1, YS):
                y_back(d, e).wait()
            core_back(d).start()

    def do_core_wait():
        for d in (0,) + NEAR:
            core_back(d).wait()

    def do_lay():
        for k in range(PAT):
            parts = ([], [])
            for j in range(2):
                cols = pl.ds(128 * j, 128)
                u, v = wave[k, :, cols], wave[k, :, pl.ds(N + 128 * j, 128)]
                p_re, p_im = probe[0, :, cols], probe[1, :, cols]
                parts[0].append(p_re * u + p_im * v)
                parts[1].append(p_re * v - p_im * u)
            for p in range(2):
                lay(k, p, parts[p], downs[k], overs[k])

    def do_collect(first, last):
        collect(first, last, [(0, 0), (1, 1)])

    def do_grad_corner():
        for n in diagonal:
            start_level(n)

    def do_grad_middle():
        start_middle(grad_v)

    def do_grad_legs():
        start_legs(grad_ends)

    def do_grad_relay(p):
        relay_middle(p, grad_ends)

    def do_grad_level():
        for n in level:
            start_level(n)

    def do_grad_forward():
        for n in diagonal:
            arrive_level(n)
        for dr in (-1, 1):
            rows = margin(dr, TH)
            for dc in (-1, 1):
                cols = shifted(edge(dc, TW))
                canvas[:, rows, cols] = canvas[:, rows, cols] + rx_h[(1 - dc) // 2, :, rows, :]
        start(grad_v, vertical, 0)
        start(grad_v, vertical, 1)

    def do_grad_wait():
        for n in level:
            arrive_level(n)
        for part in range(2):
            arrive(grad_v, vertical, part)
        arrive_middle(grad_v, grad_ends)

    def do_object():
        crown = jnp.maximum(
            jnp.maximum(rx4[0, CHUNK:, :], rx4[1, CHUNK:, :]),
            jnp.maximum(rx4[2, CHUNK:, :], rx4[3, CHUNK:, :]),
        )
        top = jnp.max(crown)
        for h in range(2):

            def renew(i, carry, h=h):
                at = pl.multiple_of(i * size, size)
                rows = pl.ds(pl.multiple_of(h * HALF + at, size), size)
                inner = pl.ds(pl.multiple_of(HALF + h * HALF + at, 8), size)
                for j in range(4):
                    cols = pl.ds(128 * (j + 1), 128)
                    share = 1.0 / (0.75 * ill[rows, pl.ds(128 * j, 128)] + 0.25 * top)
                    for p in range(2):
                        obj_new[p, rows, pl.ds(128 * j, 128)] = (
                            framed[p, inner, cols] - owned(p, rows, at, h, j) * share
                        )
                return carry

            lax.fori_loop(0, HALF // size, renew, 0)

    def do_probe():
        weight = [gathered[j, :, :, GCHUNK:, :].reshape(N, 128) for j in range(2)]
        heavy = jnp.maximum(jnp.max(weight[0]), jnp.max(weight[1]))
        for j in range(2):
            cols = pl.ds(128 * j, 128)
            share = 1.0 / (0.75 * weight[j] + 0.25 * heavy)
            for p in range(2):
                half = ZS // 2
                total = gathered[j, half * p : half * (p + 1), :, :GCHUNK, :].reshape(N, 128)
                probe_new[p, :, cols] = probe[p, :, cols] - total * share

    do_barrier()
    do_place_send()
    do_halo_send()
    do_halo_middle()
    do_local()
    do_margins()
    do_clear()
    do_probe_in()
    do_power()
    do_place_in()
    do_places()
    do_light()
    do_halo_forward()
    do_peak()
    do_meas_in()
    do_turn()
    do_halo_relay(0)
    do_halo_relay(1)
    do_halo_wait()
    do_cut()
    do_w_core_send()
    do_transforms(0, 2)
    do_w_core_sum()
    do_w_y_send()
    do_transforms(2, 4)
    do_probe_sum()
    do_core_send()
    do_lay()
    do_w_y_sum()
    do_core_sum()
    do_collect(0, 64)
    do_grad_legs()
    do_grad_middle()
    do_grad_corner()
    do_y_sum()
    do_grad_relay(0)
    do_z_sum()
    do_x_send()
    do_grad_relay(1)
    do_grad_forward()
    do_x_sum()
    do_z_back()
    do_grad_level()
    do_y_back()
    do_core_back()
    do_grad_wait()
    do_object()
    do_core_wait()
    do_probe()


def body(object_field, probe, measured, positions, counts):
    forward, inverse = tables(N)
    any_space = pl.BlockSpec(memory_space=pl.ANY)
    vmem = pl.BlockSpec(memory_space=pltpu.VMEM)
    f32 = jnp.float32
    bf16 = jnp.bfloat16
    red = 85
    dma = pltpu.SemaphoreType.DMA
    return pl.pallas_call(
        kernel,
        out_shape=(pltpu.VMEM((2, TH, TW), f32), pltpu.VMEM((2, N, N), f32)),
        in_specs=[any_space] * 7,
        out_specs=(vmem, vmem),
        scratch_shapes=[
            pltpu.SMEM((OWN + 1, 2, PAT), jnp.int32),
            pltpu.SMEM((OWN + 1, 1, 1), jnp.int32),
            pltpu.VMEM((2, TH + 2 * HALF + TILE, TW + 3 * HALF), f32),
            pltpu.VMEM((2, N, N), f32),
            pltpu.VMEM((2, N, 128), f32),
            pltpu.VMEM((TH, TW), f32),
            pltpu.VMEM((PAT, N, N), f32),
            pltpu.VMEM((PAT, N, N), f32),
            pltpu.VMEM((2 * N, 2 * N), bf16),
            pltpu.VMEM((2 * N, 2 * N), bf16),
            pltpu.VMEM((PAT, 2, 3 * N, 640), f32),
            pltpu.VMEM((2, TH + 2 * HALF, TW + 2 * HALF), f32),
            pltpu.VMEM((2, 2, HALF, TW), f32),
            pltpu.VMEM((2, 2, TH + 2 * HALF, HALF), f32),
            pltpu.VMEM((PAT, 2, N, N), f32),
            pltpu.VMEM((PAT, N, 2 * N), f32),
            pltpu.VMEM((PAT, N, 2 * N), bf16),
            pltpu.VMEM((PAT, 2 * N, N), bf16),
            pltpu.VMEM((PAT, 2 * N, N), bf16),
            pltpu.VMEM((PAT, N, 2 * N), bf16),
            pltpu.VMEM((CORES, N + TILE, 128), f32),
            pltpu.VMEM((N + TILE, 128), f32),
            pltpu.VMEM((XS, N // XS + TILE, 128), f32),
            pltpu.VMEM((XS - 1, N // XS + TILE, 128), f32),
            pltpu.VMEM((CORES, ZS, 2 * N // ZS, 128), f32),
            pltpu.VMEM((ZS, 2 * N // ZS, 128), f32),
            pltpu.VMEM((ZS, XS, GCHUNK, 128), f32),
            pltpu.VMEM((XS - 1, ZS, GCHUNK, 128), f32),
            pltpu.VMEM((ZS, CHUNK + TILE, 128), f32),
            pltpu.VMEM((ZS - 1, CHUNK + TILE, 128), f32),
            pltpu.VMEM((YS, CHUNK + TILE, 128), f32),
            pltpu.VMEM((CORES, ZS, XS, CHUNK, 128), f32),
            dma((7,)),
            dma((OWN,)),
            dma((OWN,)),
            dma((OWN,)),
            dma((OWN,)),
            pltpu.VMEM((2, HALF, TW - 2 * HALF), f32),
            pltpu.VMEM((2, HALF, TW - 2 * HALF), f32),
            dma((8,)),
            dma((8,)),
            dma((16,)),
            dma((16,)),
            dma((12,)),
            dma((12,)),
            dma((red,)),
            dma((red,)),
        ],
        compiler_params=pltpu.CompilerParams(
            collective_id=0, has_side_effects=True, vmem_limit_bytes=56 * 1024 * 1024
        ),
    )(
        positions.reshape(PAT, 2).T,
        counts,
        object_field,
        probe,
        measured.reshape(PAT, N, N),
        jnp.asarray(forward),
        jnp.asarray(inverse),
    )


def solution(mesh):
    in_specs = (
        P(None, "row", "col"),
        P(),
        P("row", "col", None, None, None),
        P("row", "col", None, None),
        P("row", "col"),
    )
    out_specs = (P(None, "row", "col"), P())
    return jax.shard_map(body, mesh=mesh, in_specs=in_specs, out_specs=out_specs, check_vma=False)
```

```python
import functools

import jax
import jax.numpy as jnp
import ml_dtypes
import numpy as np
from jax import lax
from jax.experimental import pallas as pl
from jax.experimental.pallas import tpu as pltpu
from jax.sharding import PartitionSpec as P

N = 256
HALF = 128
TH = 256
TW = 512
PAT = 4
CORES = 2
XS = 4
ZS = 8
YS = 4
GCHUNK = 16
CHUNK = 24
TILE = 8
DIRS = [(-1, 0), (1, 0), (0, -1), (0, 1), (-1, -1), (-1, 1), (1, -1), (1, 1)]
OWN = len(DIRS)
NEAR = (1, 7, 2, 6, 3, 5, 4)
FAR = NEAR[::-1] + (0,)
MESH = pl.DeviceIdType.MESH


def tables(extent):
    indices = np.arange(extent, dtype=np.int32)
    products = indices[:, None] * indices[None, :] % extent
    angles = 2.0 * np.pi / extent * products.astype(np.float64)
    cosine = np.cos(angles) / np.sqrt(float(extent))
    sine_part = np.sin(angles) / np.sqrt(float(extent))
    forward = np.block([[cosine, -sine_part], [sine_part, cosine]])
    inverse = np.block([[cosine, sine_part], [-sine_part, cosine]])
    return (
        forward.astype(np.float32).astype(ml_dtypes.bfloat16),
        inverse.astype(np.float32).astype(ml_dtypes.bfloat16),
    )


def edge(step, size):
    if step == 0:
        return pl.ds(0, size)
    return pl.ds(0 if step < 0 else size - HALF, HALF)


def margin(step, size):
    if step == 0:
        return pl.ds(HALF, size)
    return pl.ds(0 if step < 0 else size + HALF, HALF)


def kernel(
    pos_in,
    cnt_in,
    obj,
    probe_in,
    meas_in,
    fwd_in,
    inv_in,
    obj_new,
    probe_new,
    pos,
    cnt,
    framed,
    probe,
    power,
    ill,
    meas,
    meas_t,
    fwd,
    inv,
    padded,
    canvas,
    rx_v,
    rx_h,
    patches,
    wave,
    exits,
    halves,
    residues,
    backs,
    w1,
    rxw1,
    w2,
    rxw2,
    g1,
    rxg1,
    g2,
    rxg2,
    s3,
    rx3,
    rx4,
    gathered,
    local_sem,
    pos_send,
    pos_recv,
    cnt_send,
    cnt_recv,
    halo_relay,
    grad_relay,
    halo_hop,
    grad_hop,
    halo_send,
    halo_recv,
    grad_send,
    grad_recv,
    red_send,
    red_recv,
):
    row = lax.axis_index("row")
    col = lax.axis_index("col")
    core = lax.rem(col, CORES)
    x_at = (row // YS) * 2 + lax.rem(col // 2, 2)
    z_at = col // 4
    y_at = lax.rem(row, YS)

    def core_peer():
        return (row, col + 1 - 2 * core)

    def x_peer(i):
        return ((i // 2) * YS + y_at, z_at * 4 + lax.rem(i, 2) * 2 + core)

    def z_peer(i):
        return (row, i * 4 + lax.rem(col, 4))

    def y_peer(i):
        return ((row // YS) * YS + i, col)

    def exists(step):
        near_row, near_col = row + step[0], col + step[1]
        conds = []
        if step[0] < 0:
            conds.append(near_row >= 0)
        if step[0] > 0:
            conds.append(near_row < lax.axis_size("row"))
        if step[1] < 0:
            conds.append(near_col >= 0)
        if step[1] > 0:
            conds.append(near_col < lax.axis_size("col"))
        return functools.reduce(jnp.logical_and, conds)

    center = (slice(None), pl.ds(HALF, TH), pl.ds(HALF, TW))
    local = [
        pltpu.make_async_copy(probe_in, probe, local_sem.at[0]),
        pltpu.make_async_copy(meas_in, meas, local_sem.at[1]),
        pltpu.make_async_copy(fwd_in, fwd, local_sem.at[2]),
        pltpu.make_async_copy(inv_in, inv, local_sem.at[3]),
        pltpu.make_async_copy(obj, framed.at[center], local_sem.at[4]),
        pltpu.make_async_copy(pos_in, pos.at[OWN], local_sem.at[5]),
        pltpu.make_async_copy(cnt_in, cnt.at[OWN], local_sem.at[6]),
    ]

    def do_barrier():
        barrier = pltpu.get_barrier_semaphore()
        greeted = jnp.int32(0)
        for step in DIRS:
            there = exists(step)

            @pl.when(there)
            def _():
                pl.semaphore_signal(
                    barrier, inc=1, device_id=(row + step[0], col + step[1]), device_id_type=MESH
                )

            greeted = greeted + there.astype(jnp.int32)
        pl.semaphore_signal(barrier, inc=1, device_id=core_peer(), device_id_type=MESH)
        for d in range(1, XS):
            pl.semaphore_signal(
                barrier, inc=1, device_id=x_peer(lax.rem(x_at + d, XS)), device_id_type=MESH
            )
        for d in range(1, ZS):
            pl.semaphore_signal(
                barrier, inc=1, device_id=z_peer(lax.rem(z_at + d, ZS)), device_id_type=MESH
            )
        for d in range(1, YS):
            pl.semaphore_signal(
                barrier, inc=1, device_id=y_peer(lax.rem(y_at + d, YS)), device_id_type=MESH
            )
        for n in vertical:
            near_end, relay_row, far_end = route(n)

            @pl.when(row == far_end)
            def _():
                pl.semaphore_signal(
                    barrier, inc=1, device_id=across(relay_row), device_id_type=MESH
                )

            greeted = greeted + (row == relay_row).astype(jnp.int32)
        for copy in local[:1] + local[5:]:
            copy.start()
        pl.semaphore_wait(barrier, greeted + (CORES - 1 + XS - 1 + ZS - 1 + YS - 1))

    def near(dr, dc):
        return (row + dr, col + dc)

    def remote(src, dst, send_sem, recv_sem, peer):
        return pltpu.make_async_remote_copy(
            src_ref=src,
            dst_ref=dst,
            send_sem=send_sem,
            recv_sem=recv_sem,
            device_id=peer,
            device_id_type=MESH,
        )

    def opposite(n):
        return DIRS.index((-DIRS[n][0], -DIRS[n][1]))

    def place_copy(n):
        return remote(pos_in, pos.at[opposite(n)], pos_send.at[n], pos_recv.at[n], near(*DIRS[n]))

    def count_copy(n):
        return remote(cnt_in, cnt.at[opposite(n)], cnt_send.at[n], cnt_recv.at[n], near(*DIRS[n]))

    strips = [pl.ds(0, HALF), pl.ds(TW - HALF, HALF), pl.ds(HALF, TW - 2 * HALF)]

    def shifted(cols):
        return pl.ds(cols.start + HALF, cols.size)

    def halo_v(n, part):
        dr = DIRS[n][0]
        sem = n * 3 + part
        return remote(
            obj.at[:, edge(dr, TH), strips[part]],
            framed.at[:, margin(-dr, TH), shifted(strips[part])],
            halo_send.at[sem],
            halo_recv.at[sem],
            near(dr, 0),
        )

    def halo_h(n):
        dc = DIRS[n][1]
        return remote(
            obj.at[:, :, edge(dc, TW)],
            framed.at[:, pl.ds(HALF, TH), margin(-dc, TW)],
            halo_send.at[4 + n],
            halo_recv.at[4 + n],
            near(0, dc),
        )

    def halo_c(n):
        dr, dc = DIRS[n]
        return remote(
            framed.at[:, margin(-dr, TH), shifted(edge(dc, TW))],
            framed.at[:, margin(-dr, TH), margin(-dc, TW)],
            halo_send.at[4 + n],
            halo_recv.at[4 + n],
            near(0, dc),
        )

    def grad_v(n, part):
        dr = DIRS[n][0]
        sem = n * 3 + part
        return remote(
            canvas.at[:, margin(dr, TH), shifted(strips[part])],
            rx_v.at[(dr + 1) // 2, :, :, strips[part]],
            grad_send.at[sem],
            grad_recv.at[sem],
            near(dr, 0),
        )

    def grad_h(n):
        dr, dc = DIRS[n]
        rows = margin(dr, TH)
        return remote(
            canvas.at[:, rows, margin(dc, TW)],
            rx_h.at[(dc + 1) // 2, :, rows],
            grad_send.at[4 + n],
            grad_recv.at[4 + n],
            near(0, dc),
        )

    vertical, level, diagonal = (0, 1), (2, 3), (4, 5, 6, 7)

    def start(make, order, *more):
        for n in order:

            @pl.when(exists(DIRS[n]))
            def _():
                make(n, *more).start()

    def arrive(make, order, *more):
        for n in order:

            @pl.when(exists(DIRS[n]))
            def _():
                make(n, *more).wait_send()

            @pl.when(exists(DIRS[opposite(n)]))
            def _():
                make(n, *more).wait_recv()

    def start_level(n):
        @pl.when(exists((0, DIRS[n][1])))
        def _():
            grad_h(n).start()

    def arrive_level(n):
        @pl.when(exists((0, DIRS[n][1])))
        def _():
            grad_h(n).wait_send()

        @pl.when(exists((0, -DIRS[n][1])))
        def _():
            grad_h(n).wait_recv()

    def do_place_send():
        start(place_copy, range(OWN))
        start(count_copy, range(OWN))

    def route(n):
        return (3, 7, 4) if DIRS[n][0] > 0 else (4, 0, 3)

    def across(i):
        return (i, col + 2 - 4 * lax.rem(col // 2, 2))

    def leg_one(n, p, src, buf, sems):
        return remote(src, buf.at[p], sems.at[p], sems.at[2 + p], across(route(n)[1]))

    def leg_two(n, p, dst, buf, sems):
        return remote(buf.at[p], dst, sems.at[4 + p], sems.at[6 + p], across(route(n)[2]))

    def halo_ends(n, p):
        dr = DIRS[n][0]
        src = obj.at[p, edge(dr, TH), strips[2]]
        return src, framed.at[p, margin(-dr, TH), shifted(strips[2])], halo_relay, halo_hop

    def grad_ends(n, p):
        dr = DIRS[n][0]
        src = canvas.at[p, margin(dr, TH), shifted(strips[2])]
        return src, rx_v.at[(dr + 1) // 2, p, :, strips[2]], grad_relay, grad_hop

    def first_leg(n, p, ends):
        src, dst, buf, sems = ends(n, p)
        return leg_one(n, p, src, buf, sems)

    def second_leg(n, p, ends):
        src, dst, buf, sems = ends(n, p)
        return leg_two(n, p, dst, buf, sems)

    def start_legs(ends):
        for n in vertical:

            @pl.when(row == route(n)[0])
            def _():
                for p in range(2):
                    first_leg(n, p, ends).start()

    def start_middle(direct):
        for n in vertical:

            @pl.when(exists(DIRS[n]) & (row != route(n)[0]))
            def _():
                direct(n, 2).start()

    def relay_middle(p, ends):
        for n in vertical:

            @pl.when(row == route(n)[1])
            def _():
                first_leg(n, p, ends).wait_recv()
                second_leg(n, p, ends).start()

    def arrive_middle(direct, ends):
        for n in vertical:

            @pl.when(row == route(n)[0])
            def _():
                for p in range(2):
                    first_leg(n, p, ends).wait_send()

            @pl.when(exists(DIRS[n]) & (row != route(n)[0]))
            def _():
                direct(n, 2).wait_send()

            @pl.when(row == route(n)[1])
            def _():
                for p in range(2):
                    second_leg(n, p, ends).wait_send()

            @pl.when(row == route(n)[2])
            def _():
                for p in range(2):
                    second_leg(n, p, ends).wait_recv()

            @pl.when(exists(DIRS[opposite(n)]) & (row != route(n)[2]))
            def _():
                direct(n, 2).wait_recv()

    def do_halo_send():
        start(halo_v, vertical, 0)
        start(halo_v, vertical, 1)
        for n in diagonal:

            @pl.when(direct_from(n))
            def _():
                halo_d(n).start()

        start(halo_h, level)

    def do_halo_middle():
        start_legs(halo_ends)
        start_middle(halo_v)

    def halo_d(n):
        dr, dc = DIRS[n]
        return remote(
            obj.at[:, edge(dr, TH), edge(dc, TW)],
            framed.at[:, margin(-dr, TH), margin(-dc, TW)],
            halo_send.at[8 + n],
            halo_recv.at[8 + n],
            near(dr, dc),
        )

    def leaves(dc):
        return core == (1 if dc > 0 else 0)

    def direct_from(n):
        return (row == (2 if DIRS[n][0] > 0 else 5)) & exists((0, DIRS[n][1])) & leaves(DIRS[n][1])

    def direct_to(n):
        dr, dc = DIRS[n]
        return (row == (3 if dr > 0 else 4)) & exists((0, -dc)) & leaves(-dc)

    def handed_from(n):
        dr, dc = DIRS[n]
        apart = (row == (3 if dr > 0 else 4)) & leaves(dc)
        return exists((-dr, dc)) & jnp.logical_not(apart)

    def handed_to(n):
        dr, dc = DIRS[n]
        return exists((-dr, -dc)) & jnp.logical_not(direct_to(n))

    def do_halo_forward():
        arrive(halo_v, vertical, 0)
        arrive(halo_v, vertical, 1)
        for n in diagonal:

            @pl.when(handed_from(n))
            def _():
                halo_c(n).start()

    def do_halo_relay(p):
        relay_middle(p, halo_ends)

    def do_halo_wait():
        arrive(halo_h, level)
        arrive_middle(halo_v, halo_ends)
        for n in diagonal:

            @pl.when(handed_from(n))
            def _():
                halo_c(n).wait_send()

            @pl.when(handed_to(n))
            def _():
                halo_c(n).wait_recv()

            @pl.when(direct_from(n))
            def _():
                halo_d(n).wait_send()

            @pl.when(direct_to(n))
            def _():
                halo_d(n).wait_recv()

    def do_local():
        for copy in local[1:5]:
            copy.start()

    def do_margins():
        for n in range(OWN):
            dr, dc = DIRS[n]

            @pl.when(jnp.logical_not(exists(DIRS[n])))
            def _():
                rows, cols = margin(dr, TH), margin(dc, TW)
                framed[:, rows, cols] = jnp.zeros((2, rows.size, cols.size), jnp.float32)
                cnt[n, 0, 0] = 0
                for k in range(PAT):
                    pos[n, 0, k] = 0
                    pos[n, 1, k] = 0

        for n in vertical:

            @pl.when(jnp.logical_not(exists(DIRS[n])))
            def _():
                rx_v[1 - n] = jnp.zeros((2, HALF, TW), jnp.float32)

        for n in level:

            @pl.when(jnp.logical_not(exists(DIRS[n])))
            def _():
                rx_h[3 - n] = jnp.zeros((2, TH + 2 * HALF, HALF), jnp.float32)

        framed[:, TH + 2 * HALF :, :] = jnp.zeros((2, TILE, TW + 3 * HALF), jnp.float32)
        framed[:, : TH + 2 * HALF, TW + 2 * HALF :] = jnp.zeros(
            (2, TH + 2 * HALF, HALF), jnp.float32
        )

    def clear(i, carry):
        at = pl.ds(pl.multiple_of(i * 32, 32), 32)
        for k in range(PAT):
            for p in range(2):
                padded[k, p, at, :] = jnp.zeros((32, 640), jnp.float32)
        return carry

    def do_clear():
        lax.fori_loop(0, 24, clear, 0)

    def do_probe_in():
        local[0].wait()

    def do_meas_in():
        for copy in local[1:5]:
            copy.wait()

    def do_place_in():
        for copy in local[5:]:
            copy.wait()
        arrive(place_copy, range(OWN))
        arrive(count_copy, range(OWN))

    lives, tops, lefts, downs, overs = [], [], [], [], []

    def do_places():
        for k in range(PAT):
            a = lax.max(lax.min(pos[OWN, 0, k] - (row * TH - HALF), TH), 0)
            b = lax.max(lax.min(pos[OWN, 1, k] - (col * TW - HALF), TW), 0)
            lives.append(jnp.where(k < cnt[OWN, 0, 0], 1.0, 0.0).astype(jnp.float32))
            tops.append(lax.div(a, TILE))
            downs.append(lax.rem(a, TILE))
            lefts.append(lax.div(b, 128))
            overs.append(lax.rem(b, 128))

    def lane_iota(shape):
        return lax.broadcasted_iota(jnp.int32, shape, len(shape) - 1)

    def sub_iota(shape):
        return lax.broadcasted_iota(jnp.int32, shape, len(shape) - 2)

    def window(p, k, first, tiles):
        s, r = downs[k], overs[k]
        rows = pl.ds((tops[k] + first) * TILE, (tiles + 1) * TILE)
        turned = []
        for j in range(3):
            cols = pl.ds((lefts[k] + j) * 128, 128)
            turned.append(pltpu.roll(framed[p, rows, cols], lax.rem(128 - r, 128), 1))
        near = lane_iota(turned[0].shape) < 128 - r
        found = []
        for j in range(2):
            both = jnp.where(near, turned[j], turned[j + 1]).reshape(tiles + 1, TILE, 128)
            both = pltpu.roll(both, lax.rem(TILE - s, TILE), 1)
            upper = sub_iota((tiles, TILE, 128)) < TILE - s
            found.append(
                jnp.where(upper, both[:tiles], both[1:]).reshape(tiles * TILE, 128)
            )
        return found

    def lay(k, p, tiles, s, r):
        moved = []
        for x in tiles:
            x = pltpu.roll(x.reshape(N // TILE, TILE, 128), s, 1)
            none = jnp.zeros((1, TILE, 128), jnp.float32)
            here = jnp.concatenate([x, none], axis=0)
            above = jnp.concatenate([none, x], axis=0)
            y = jnp.where(sub_iota(here.shape) >= s, here, above).reshape(N + TILE, 128)
            moved.append(pltpu.roll(y, r, 1))
        right = lane_iota((N + TILE, 128)) >= r
        rows = pl.ds(N, N + TILE)
        padded[k, p, rows, pl.ds(128, 128)] = jnp.where(right, moved[0], 0.0)
        padded[k, p, rows, pl.ds(256, 128)] = jnp.where(right, moved[1], moved[0])
        padded[k, p, rows, pl.ds(384, 128)] = jnp.where(right, 0.0, moved[1])

    def collect(start, stop, pairs):
        size = 8

        def one(i, carry):
            first = i * size
            rows = pl.ds(pl.multiple_of(first * TILE, size * TILE), size * TILE)
            for q, p in pairs:
                for j in range(6):
                    total = None
                    for k in range(PAT):
                        at = (first - tops[k] + N // TILE) * TILE
                        lane = lax.max(lax.min(j - lefts[k] + 1, 4), 0) * 128
                        part = padded[
                            k, p, pl.ds(at, size * TILE), pl.ds(lane, 128)
                        ]
                        total = part if total is None else total + part
                    canvas[q, rows, pl.ds(j * 128, 128)] = total
            return carry

        lax.fori_loop(start // size, stop // size, one, 0, unroll=True)

    def do_power():
        for j in range(2):
            cols = pl.ds(128 * j, 128)
            power[j] = probe[0, :, cols] * probe[0, :, cols] + probe[1, :, cols] * probe[1, :, cols]
        ill[...] = jnp.zeros((TH, TW), jnp.float32)

    def light(t, carry):
        high, left = [], []
        for k in range(PAT):
            alive = jnp.where(k < cnt[t, 0, 0], 1.0, 0.0).astype(jnp.float32)
            a = lax.max(lax.min(pos[t, 0, k] - row * TH, 384), -384) + 384
            b = lax.max(lax.min(pos[t, 1, k] - col * TW, 896), -640) + 640
            lay(k, 0, [alive * power[j] for j in range(2)], lax.rem(a, TILE), lax.rem(b, 128))
            high.append(lax.div(a, TILE) - 80)
            left.append(lax.div(b, 128) - 5)
        size = 8
        for i in range(0, TH // TILE, size):
            rows = pl.ds(i * TILE, size * TILE)
            for j in range(4):
                total = ill[rows, pl.ds(j * 128, 128)]
                for k in range(PAT):
                    at = lax.max(lax.min(i - high[k], 96 - size), 0) * TILE
                    lane = lax.max(lax.min(j - left[k] + 1, 4), 0) * 128
                    total = total + padded[k, 0, pl.ds(at, size * TILE), pl.ds(lane, 128)]
                ill[rows, pl.ds(j * 128, 128)] = total
        return carry

    def do_light():
        lax.fori_loop(0, len(DIRS) + 1, light, 0)

    def do_peak():
        def largest(i, most):
            rows = pl.ds(pl.multiple_of(i * 32, 32), 32)
            for j in range(4):
                value = ill[rows, pl.ds(128 * j, 128)]
                most = jnp.maximum(most, jnp.max(value.reshape(4, TILE, 128), axis=0))
            return most

        peak = lax.fori_loop(0, TH // 32, largest, jnp.zeros((TILE, 128), jnp.float32))
        for c in range(CORES):
            w1[c, N:, :] = peak

    def do_turn():
        for k in range(PAT):
            meas_t[k] = meas[k].T

    def cut(i, carry):
        tiles = 4
        rows = pl.ds(pl.multiple_of(i * tiles * TILE, tiles * TILE), tiles * TILE)
        weight = [jnp.zeros((tiles * TILE, 128), jnp.float32)] * 2
        for k in range(PAT):
            real = window(0, k, i * tiles, tiles)
            imag = window(1, k, i * tiles, tiles)
            for j in range(2):
                cols = pl.ds(128 * j, 128)
                p_re, p_im = probe[0, rows, cols], probe[1, rows, cols]
                patches[k, 0, rows, cols] = real[j]
                patches[k, 1, rows, cols] = imag[j]
                exits[k, rows, cols] = (p_re * real[j] - p_im * imag[j]).astype(jnp.bfloat16)
                exits[k, rows, pl.ds(N + 128 * j, 128)] = (
                    p_re * imag[j] + p_im * real[j]
                ).astype(jnp.bfloat16)
                weight[j] = weight[j] + lives[k] * (real[j] * real[j] + imag[j] * imag[j])
        for j in range(2):
            w1[j, rows, :] = weight[j]
        return carry

    def do_cut():
        lax.fori_loop(0, 8, cut, 0, unroll=True)

    def dot(a, b):
        return jnp.dot(a, b, preferred_element_type=jnp.float32)

    def do_transforms(first, last):
        these = range(first, last)
        for k in these:
            for h in range(2):
                rows = pl.ds(h * HALF, HALF)
                half = dot(exits[k, rows, :], fwd[...]).astype(jnp.bfloat16)
                halves[k, rows, :] = half[:, :N]
                halves[k, pl.ds(N + h * HALF, HALF), :] = half[:, N:]
        for k in these:
            for h in range(2):
                cols = pl.ds(h * HALF, HALF)
                upper, lower = pl.ds(h * HALF, HALF), pl.ds(N + h * HALF, HALF)
                re = dot(inv[upper, :], halves[k])
                im = dot(inv[lower, :], halves[k])
                factor = lives[k] * (1.0 - meas_t[k, upper, :] * lax.rsqrt(re * re + im * im + 0.25))
                residues[k, upper, :] = (factor * re).astype(jnp.bfloat16)
                residues[k, lower, :] = (factor * im).astype(jnp.bfloat16)
        for k in these:
            for h in range(2):
                upper, lower = pl.ds(h * HALF, HALF), pl.ds(N + h * HALF, HALF)
                backs[k, upper, :N] = dot(fwd[upper, :], residues[k]).astype(jnp.bfloat16)
                backs[k, upper, N:] = dot(fwd[lower, :], residues[k]).astype(jnp.bfloat16)
        for k in these:
            for h in range(2):
                rows = pl.ds(h * HALF, HALF)
                wave[k, rows, :] = dot(backs[k, rows, :], inv[...])

    def do_probe_sum():
        size = 32
        for i in range(N // size):
            rows = pl.ds(i * size, size)
            for j in range(2):
                cols = pl.ds(128 * j, 128)
                real = imag = None
                for k in range(PAT):
                    a, b = patches[k, 0, rows, cols], patches[k, 1, rows, cols]
                    u, v = wave[k, rows, cols], wave[k, rows, pl.ds(N + 128 * j, 128)]
                    one, two = a * u + b * v, a * v - b * u
                    real = one if real is None else real + one
                    imag = two if imag is None else imag + two
                part = pl.ds((i % 2) * size, size)
                g1[j, i // 2, part, :] = real
                g1[j, ZS // 2 + i // 2, part, :] = imag

    def owned(p, rows, at, h, j):
        size = rows.size
        inner = pl.ds(pl.multiple_of(HALF + h * HALF + at, 8), size)
        value = canvas[p, inner, pl.ds(128 * (j + 1), 128)]
        value = value + rx_v[1 - h, p, pl.ds(at, size), pl.ds(128 * j, 128)]
        if j in (0, 3):
            value = value + rx_h[1 if j == 0 else 0, p, inner, :]
        return value

    size = 32

    def send(src, dst, sem, peer):
        return remote(src, dst, red_send.at[sem], red_recv.at[sem], peer)

    def ahead(d):
        return lax.rem(z_at + d, ZS)

    def behind(d):
        return lax.rem(z_at + ZS - d, ZS)

    def w_core():
        return send(w1.at[1 - core], rxw1, 0, core_peer())

    def w_y(e):
        to = lax.rem(y_at + e, YS)
        return send(w2.at[to], rxw2.at[e - 1], e, y_peer(to))

    def g_core(d):
        return send(g1.at[1 - core, ahead(d)], rxg1.at[ahead(d)], 4 + d, core_peer())

    def g_y(d, e):
        to = lax.rem(y_at + e, YS)
        return send(g2.at[ahead(d), to], rxg2.at[e - 1, ahead(d)], 11 + 3 * d + e, y_peer(to))

    def z_copy(d):
        return send(s3.at[ahead(d)], rx3.at[d - 1], 35 + d, z_peer(ahead(d)))

    def x_copy(d):
        to = lax.rem(x_at + d, XS)
        return send(rx4.at[x_at], rx4.at[x_at], 42 + d, x_peer(to))

    def do_w_core_send():
        w_core().start()

    def do_w_core_sum():
        w_core().wait()
        part = N // YS
        crown = jnp.maximum(w1[core, N:, :], rxw1[N:, :])
        total = (w1[core, :N, :] + rxw1[:N, :]).reshape(ZS, YS, TILE, 128)
        for i in range(YS):
            w2[i, :part, :] = total[:, i].reshape(part, 128)
            w2[i, part:, :] = crown

    def do_w_y_send():
        for d in range(1, YS):
            w_y(d).start()

    def do_w_y_sum():
        for d in range(1, YS):
            w_y(d).wait()
        part = N // YS
        crown = w2[y_at, part:, :]
        for d in range(YS - 1):
            crown = jnp.maximum(crown, rxw2[d, part:, :])
        size = CHUNK - GCHUNK
        for i in range(ZS):
            at = pl.ds(i * size, size)
            s3[i, GCHUNK:CHUNK, :] = (w2[y_at, at, :] + rxw2[0, at, :]) + (
                rxw2[1, at, :] + rxw2[2, at, :]
            )
            s3[i, CHUNK:, :] = crown

    def do_core_send():
        for d in FAR:
            g_core(d).start()

    def do_core_sum():
        for d in FAR:
            g_core(d).wait()
            at = ahead(d)
            g2[at] = (g1[core, at] + rxg1[at]).reshape(YS, GCHUNK, 128)
            for e in range(1, YS):
                g_y(d, e).start()

    def do_y_sum():
        for d in FAR:
            for e in range(1, YS):
                g_y(d, e).wait()
            at = ahead(d)
            s3[at, :GCHUNK, :] = (g2[at, y_at] + rxg2[0, at]) + (rxg2[1, at] + rxg2[2, at])
            if d:
                z_copy(d).start()

    def do_z_sum():
        total = s3[z_at, :CHUNK, :]
        crown = s3[z_at, CHUNK:, :]
        for d in NEAR:
            z_copy(d).wait()
            total = total + rx3[d - 1, :CHUNK, :]
            crown = jnp.maximum(crown, rx3[d - 1, CHUNK:, :])
        rx4[x_at, :CHUNK, :] = total
        rx4[x_at, CHUNK:, :] = crown

    def do_x_send():
        for d in range(1, XS):
            x_copy(d).start()

    def do_x_sum():
        for d in range(1, XS):
            x_copy(d).wait()
        gathered[core, z_at, y_at] = (rx4[0, :CHUNK, :] + rx4[1, :CHUNK, :]) + (
            rx4[2, :CHUNK, :] + rx4[3, :CHUNK, :]
        )

    def z_back(d):
        mine = gathered.at[core, z_at, y_at]
        return send(mine, mine, 45 + d, z_peer(ahead(d)))

    def y_back(d, e):
        mine = gathered.at[core, behind(d), y_at]
        return send(mine, mine, 52 + 3 * d + e, y_peer(lax.rem(y_at + e, YS)))

    def core_back(d):
        mine = gathered.at[core, behind(d)]
        return send(mine, mine, 77 + d, core_peer())

    def do_z_back():
        for d in NEAR[::-1]:
            z_back(d).start()
        for e in range(1, YS):
            y_back(0, e).start()

    def do_y_back():
        for d in NEAR:
            z_back(d).wait()
            for e in range(1, YS):
                y_back(d, e).start()

    def do_core_back():
        for d in (0,) + NEAR:
            for e in range(1, YS):
                y_back(d, e).wait()
            core_back(d).start()

    def do_core_wait():
        for d in (0,) + NEAR:
            core_back(d).wait()

    def do_lay():
        for k in range(PAT):
            parts = ([], [])
            for j in range(2):
                cols = pl.ds(128 * j, 128)
                u, v = wave[k, :, cols], wave[k, :, pl.ds(N + 128 * j, 128)]
                p_re, p_im = probe[0, :, cols], probe[1, :, cols]
                parts[0].append(p_re * u + p_im * v)
                parts[1].append(p_re * v - p_im * u)
            for p in range(2):
                lay(k, p, parts[p], downs[k], overs[k])

    def do_collect(first, last):
        collect(first, last, [(0, 0), (1, 1)])

    def do_grad_corner():
        for n in diagonal:
            start_level(n)

    def do_grad_middle():
        start_middle(grad_v)

    def do_grad_legs():
        start_legs(grad_ends)

    def do_grad_relay(p):
        relay_middle(p, grad_ends)

    def do_grad_level():
        for n in level:
            start_level(n)

    def do_grad_forward():
        for n in diagonal:
            arrive_level(n)
        for dr in (-1, 1):
            rows = margin(dr, TH)
            for dc in (-1, 1):
                cols = shifted(edge(dc, TW))
                canvas[:, rows, cols] = canvas[:, rows, cols] + rx_h[(1 - dc) // 2, :, rows, :]
        start(grad_v, vertical, 0)
        start(grad_v, vertical, 1)

    def do_grad_wait():
        for n in level:
            arrive_level(n)
        for part in range(2):
            arrive(grad_v, vertical, part)
        arrive_middle(grad_v, grad_ends)

    def do_object():
        crown = jnp.maximum(
            jnp.maximum(rx4[0, CHUNK:, :], rx4[1, CHUNK:, :]),
            jnp.maximum(rx4[2, CHUNK:, :], rx4[3, CHUNK:, :]),
        )
        top = jnp.max(crown)
        for h in range(2):

            def renew(i, carry, h=h):
                at = pl.multiple_of(i * size, size)
                rows = pl.ds(pl.multiple_of(h * HALF + at, size), size)
                inner = pl.ds(pl.multiple_of(HALF + h * HALF + at, 8), size)
                for j in range(4):
                    cols = pl.ds(128 * (j + 1), 128)
                    share = 1.0 / (0.75 * ill[rows, pl.ds(128 * j, 128)] + 0.25 * top)
                    for p in range(2):
                        obj_new[p, rows, pl.ds(128 * j, 128)] = (
                            framed[p, inner, cols] - owned(p, rows, at, h, j) * share
                        )
                return carry

            lax.fori_loop(0, HALF // size, renew, 0, unroll=True)

    def do_probe():
        weight = [gathered[j, :, :, GCHUNK:, :].reshape(N, 128) for j in range(2)]
        heavy = jnp.maximum(jnp.max(weight[0]), jnp.max(weight[1]))
        for j in range(2):
            cols = pl.ds(128 * j, 128)
            share = 1.0 / (0.75 * weight[j] + 0.25 * heavy)
            for p in range(2):
                half = ZS // 2
                total = gathered[j, half * p : half * (p + 1), :, :GCHUNK, :].reshape(N, 128)
                probe_new[p, :, cols] = probe[p, :, cols] - total * share

    do_barrier()
    do_place_send()
    do_halo_send()
    do_halo_middle()
    do_local()
    do_margins()
    do_clear()
    do_probe_in()
    do_power()
    do_place_in()
    do_places()
    do_light()
    do_halo_forward()
    do_peak()
    do_meas_in()
    do_turn()
    do_halo_relay(0)
    do_halo_relay(1)
    do_halo_wait()
    do_cut()
    do_w_core_send()
    do_transforms(0, 2)
    do_w_core_sum()
    do_w_y_send()
    do_transforms(2, 4)
    do_probe_sum()
    do_core_send()
    do_lay()
    do_w_y_sum()
    do_core_sum()
    do_collect(0, 64)
    do_grad_legs()
    do_grad_middle()
    do_grad_corner()
    do_y_sum()
    do_grad_relay(0)
    do_z_sum()
    do_x_send()
    do_grad_relay(1)
    do_grad_forward()
    do_x_sum()
    do_z_back()
    do_grad_level()
    do_y_back()
    do_core_back()
    do_grad_wait()
    do_object()
    do_core_wait()
    do_probe()


def body(object_field, probe, measured, positions, counts):
    forward, inverse = tables(N)
    any_space = pl.BlockSpec(memory_space=pl.ANY)
    vmem = pl.BlockSpec(memory_space=pltpu.VMEM)
    f32 = jnp.float32
    bf16 = jnp.bfloat16
    red = 85
    dma = pltpu.SemaphoreType.DMA
    return pl.pallas_call(
        kernel,
        out_shape=(pltpu.VMEM((2, TH, TW), f32), pltpu.VMEM((2, N, N), f32)),
        in_specs=[any_space] * 7,
        out_specs=(vmem, vmem),
        scratch_shapes=[
            pltpu.SMEM((OWN + 1, 2, PAT), jnp.int32),
            pltpu.SMEM((OWN + 1, 1, 1), jnp.int32),
            pltpu.VMEM((2, TH + 2 * HALF + TILE, TW + 3 * HALF), f32),
            pltpu.VMEM((2, N, N), f32),
            pltpu.VMEM((2, N, 128), f32),
            pltpu.VMEM((TH, TW), f32),
            pltpu.VMEM((PAT, N, N), f32),
            pltpu.VMEM((PAT, N, N), f32),
            pltpu.VMEM((2 * N, 2 * N), bf16),
            pltpu.VMEM((2 * N, 2 * N), bf16),
            pltpu.VMEM((PAT, 2, 3 * N, 640), f32),
            pltpu.VMEM((2, TH + 2 * HALF, TW + 2 * HALF), f32),
            pltpu.VMEM((2, 2, HALF, TW), f32),
            pltpu.VMEM((2, 2, TH + 2 * HALF, HALF), f32),
            pltpu.VMEM((PAT, 2, N, N), f32),
            pltpu.VMEM((PAT, N, 2 * N), f32),
            pltpu.VMEM((PAT, N, 2 * N), bf16),
            pltpu.VMEM((PAT, 2 * N, N), bf16),
            pltpu.VMEM((PAT, 2 * N, N), bf16),
            pltpu.VMEM((PAT, N, 2 * N), bf16),
            pltpu.VMEM((CORES, N + TILE, 128), f32),
            pltpu.VMEM((N + TILE, 128), f32),
            pltpu.VMEM((XS, N // XS + TILE, 128), f32),
            pltpu.VMEM((XS - 1, N // XS + TILE, 128), f32),
            pltpu.VMEM((CORES, ZS, 2 * N // ZS, 128), f32),
            pltpu.VMEM((ZS, 2 * N // ZS, 128), f32),
            pltpu.VMEM((ZS, XS, GCHUNK, 128), f32),
            pltpu.VMEM((XS - 1, ZS, GCHUNK, 128), f32),
            pltpu.VMEM((ZS, CHUNK + TILE, 128), f32),
            pltpu.VMEM((ZS - 1, CHUNK + TILE, 128), f32),
            pltpu.VMEM((YS, CHUNK + TILE, 128), f32),
            pltpu.VMEM((CORES, ZS, XS, CHUNK, 128), f32),
            dma((7,)),
            dma((OWN,)),
            dma((OWN,)),
            dma((OWN,)),
            dma((OWN,)),
            pltpu.VMEM((2, HALF, TW - 2 * HALF), f32),
            pltpu.VMEM((2, HALF, TW - 2 * HALF), f32),
            dma((8,)),
            dma((8,)),
            dma((16,)),
            dma((16,)),
            dma((12,)),
            dma((12,)),
            dma((red,)),
            dma((red,)),
        ],
        compiler_params=pltpu.CompilerParams(
            collective_id=0, has_side_effects=True, vmem_limit_bytes=56 * 1024 * 1024
        ),
    )(
        positions.reshape(PAT, 2).T,
        counts,
        object_field,
        probe,
        measured.reshape(PAT, N, N),
        jnp.asarray(forward),
        jnp.asarray(inverse),
    )


def solution(mesh):
    in_specs = (
        P(None, "row", "col"),
        P(),
        P("row", "col", None, None, None),
        P("row", "col", None, None),
        P("row", "col"),
    )
    out_specs = (P(None, "row", "col"), P())
    return jax.shard_map(body, mesh=mesh, in_specs=in_specs, out_specs=out_specs, check_vma=False)
```

```python
import functools

import jax
import jax.numpy as jnp
import ml_dtypes
import numpy as np
from jax import lax
from jax.experimental import pallas as pl
from jax.experimental.pallas import tpu as pltpu
from jax.sharding import PartitionSpec as P

N = 256
HALF = 128
TH = 256
TW = 512
PAT = 4
CORES = 2
XS = 4
ZS = 8
YS = 4
GCHUNK = 16
CHUNK = 24
TILE = 8
DIRS = [(-1, 0), (1, 0), (0, -1), (0, 1), (-1, -1), (-1, 1), (1, -1), (1, 1)]
OWN = len(DIRS)
NEAR = (1, 7, 2, 6, 3, 5, 4)
FAR = NEAR[::-1] + (0,)
MESH = pl.DeviceIdType.MESH


def tables(extent):
    indices = np.arange(extent, dtype=np.int32)
    products = indices[:, None] * indices[None, :] % extent
    angles = 2.0 * np.pi / extent * products.astype(np.float64)
    cosine = np.cos(angles) / np.sqrt(float(extent))
    sine_part = np.sin(angles) / np.sqrt(float(extent))
    forward = np.block([[cosine, -sine_part], [sine_part, cosine]])
    inverse = np.block([[cosine, sine_part], [-sine_part, cosine]])
    return (
        forward.astype(np.float32).astype(ml_dtypes.bfloat16),
        inverse.astype(np.float32).astype(ml_dtypes.bfloat16),
    )


def edge(step, size):
    if step == 0:
        return pl.ds(0, size)
    return pl.ds(0 if step < 0 else size - HALF, HALF)


def margin(step, size):
    if step == 0:
        return pl.ds(HALF, size)
    return pl.ds(0 if step < 0 else size + HALF, HALF)


def kernel(
    pos_in,
    cnt_in,
    obj,
    probe_in,
    meas_in,
    fwd_in,
    inv_in,
    obj_new,
    probe_new,
    pos,
    cnt,
    framed,
    probe,
    power,
    ill,
    meas,
    meas_t,
    fwd,
    inv,
    padded,
    canvas,
    rx_v,
    rx_h,
    patches,
    wave,
    exits,
    halves,
    residues,
    backs,
    w1,
    rxw1,
    w2,
    rxw2,
    g1,
    rxg1,
    g2,
    rxg2,
    s3,
    rx3,
    rx4,
    gathered,
    local_sem,
    pos_send,
    pos_recv,
    cnt_send,
    cnt_recv,
    halo_relay,
    grad_relay,
    halo_hop,
    grad_hop,
    halo_send,
    halo_recv,
    grad_send,
    grad_recv,
    red_send,
    red_recv,
):
    row = lax.axis_index("row")
    col = lax.axis_index("col")
    core = lax.rem(col, CORES)
    x_at = (row // YS) * 2 + lax.rem(col // 2, 2)
    z_at = col // 4
    y_at = lax.rem(row, YS)

    def core_peer():
        return (row, col + 1 - 2 * core)

    def x_peer(i):
        return ((i // 2) * YS + y_at, z_at * 4 + lax.rem(i, 2) * 2 + core)

    def z_peer(i):
        return (row, i * 4 + lax.rem(col, 4))

    def y_peer(i):
        return ((row // YS) * YS + i, col)

    def exists(step):
        near_row, near_col = row + step[0], col + step[1]
        conds = []
        if step[0] < 0:
            conds.append(near_row >= 0)
        if step[0] > 0:
            conds.append(near_row < lax.axis_size("row"))
        if step[1] < 0:
            conds.append(near_col >= 0)
        if step[1] > 0:
            conds.append(near_col < lax.axis_size("col"))
        return functools.reduce(jnp.logical_and, conds)

    center = (slice(None), pl.ds(HALF, TH), pl.ds(HALF, TW))
    local = [
        pltpu.make_async_copy(probe_in, probe, local_sem.at[0]),
        pltpu.make_async_copy(meas_in, meas, local_sem.at[1]),
        pltpu.make_async_copy(fwd_in, fwd, local_sem.at[2]),
        pltpu.make_async_copy(inv_in, inv, local_sem.at[3]),
        pltpu.make_async_copy(obj, framed.at[center], local_sem.at[4]),
        pltpu.make_async_copy(pos_in, pos.at[OWN], local_sem.at[5]),
        pltpu.make_async_copy(cnt_in, cnt.at[OWN], local_sem.at[6]),
    ]

    def do_barrier():
        barrier = pltpu.get_barrier_semaphore()
        greeted = jnp.int32(0)
        for step in DIRS:
            there = exists(step)

            @pl.when(there)
            def _():
                pl.semaphore_signal(
                    barrier, inc=1, device_id=(row + step[0], col + step[1]), device_id_type=MESH
                )

            greeted = greeted + there.astype(jnp.int32)
        pl.semaphore_signal(barrier, inc=1, device_id=core_peer(), device_id_type=MESH)
        for d in range(1, XS):
            pl.semaphore_signal(
                barrier, inc=1, device_id=x_peer(lax.rem(x_at + d, XS)), device_id_type=MESH
            )
        for d in range(1, ZS):
            pl.semaphore_signal(
                barrier, inc=1, device_id=z_peer(lax.rem(z_at + d, ZS)), device_id_type=MESH
            )
        for d in range(1, YS):
            pl.semaphore_signal(
                barrier, inc=1, device_id=y_peer(lax.rem(y_at + d, YS)), device_id_type=MESH
            )
        for n in vertical:
            near_end, relay_row, far_end = route(n)

            @pl.when(row == far_end)
            def _():
                pl.semaphore_signal(
                    barrier, inc=1, device_id=across(relay_row), device_id_type=MESH
                )

            greeted = greeted + (row == relay_row).astype(jnp.int32)
        for copy in local[:1] + local[5:]:
            copy.start()
        pl.semaphore_wait(barrier, greeted + (CORES - 1 + XS - 1 + ZS - 1 + YS - 1))

    def near(dr, dc):
        return (row + dr, col + dc)

    def remote(src, dst, send_sem, recv_sem, peer):
        return pltpu.make_async_remote_copy(
            src_ref=src,
            dst_ref=dst,
            send_sem=send_sem,
            recv_sem=recv_sem,
            device_id=peer,
            device_id_type=MESH,
        )

    def opposite(n):
        return DIRS.index((-DIRS[n][0], -DIRS[n][1]))

    def place_copy(n):
        return remote(pos_in, pos.at[opposite(n)], pos_send.at[n], pos_recv.at[n], near(*DIRS[n]))

    def count_copy(n):
        return remote(cnt_in, cnt.at[opposite(n)], cnt_send.at[n], cnt_recv.at[n], near(*DIRS[n]))

    strips = [pl.ds(0, HALF), pl.ds(TW - HALF, HALF), pl.ds(HALF, TW - 2 * HALF)]

    def shifted(cols):
        return pl.ds(cols.start + HALF, cols.size)

    def halo_v(n, part):
        dr = DIRS[n][0]
        sem = n * 3 + part
        return remote(
            obj.at[:, edge(dr, TH), strips[part]],
            framed.at[:, margin(-dr, TH), shifted(strips[part])],
            halo_send.at[sem],
            halo_recv.at[sem],
            near(dr, 0),
        )

    def halo_h(n):
        dc = DIRS[n][1]
        return remote(
            obj.at[:, :, edge(dc, TW)],
            framed.at[:, pl.ds(HALF, TH), margin(-dc, TW)],
            halo_send.at[4 + n],
            halo_recv.at[4 + n],
            near(0, dc),
        )

    def halo_c(n):
        dr, dc = DIRS[n]
        return remote(
            framed.at[:, margin(-dr, TH), shifted(edge(dc, TW))],
            framed.at[:, margin(-dr, TH), margin(-dc, TW)],
            halo_send.at[4 + n],
            halo_recv.at[4 + n],
            near(0, dc),
        )

    def grad_v(n, part):
        dr = DIRS[n][0]
        sem = n * 3 + part
        return remote(
            canvas.at[:, margin(dr, TH), shifted(strips[part])],
            rx_v.at[(dr + 1) // 2, :, :, strips[part]],
            grad_send.at[sem],
            grad_recv.at[sem],
            near(dr, 0),
        )

    def grad_h(n):
        dr, dc = DIRS[n]
        rows = margin(dr, TH)
        return remote(
            canvas.at[:, rows, margin(dc, TW)],
            rx_h.at[(dc + 1) // 2, :, rows],
            grad_send.at[4 + n],
            grad_recv.at[4 + n],
            near(0, dc),
        )

    vertical, level, diagonal = (0, 1), (2, 3), (4, 5, 6, 7)

    def start(make, order, *more):
        for n in order:

            @pl.when(exists(DIRS[n]))
            def _():
                make(n, *more).start()

    def arrive(make, order, *more):
        for n in order:

            @pl.when(exists(DIRS[n]))
            def _():
                make(n, *more).wait_send()

            @pl.when(exists(DIRS[opposite(n)]))
            def _():
                make(n, *more).wait_recv()

    def start_level(n):
        @pl.when(exists((0, DIRS[n][1])))
        def _():
            grad_h(n).start()

    def arrive_level(n):
        @pl.when(exists((0, DIRS[n][1])))
        def _():
            grad_h(n).wait_send()

        @pl.when(exists((0, -DIRS[n][1])))
        def _():
            grad_h(n).wait_recv()

    def do_place_send():
        start(place_copy, range(OWN))
        start(count_copy, range(OWN))

    def route(n):
        return (3, 7, 4) if DIRS[n][0] > 0 else (4, 0, 3)

    def across(i):
        return (i, col + 2 - 4 * lax.rem(col // 2, 2))

    def leg_one(n, p, src, buf, sems):
        return remote(src, buf.at[p], sems.at[p], sems.at[2 + p], across(route(n)[1]))

    def leg_two(n, p, dst, buf, sems):
        return remote(buf.at[p], dst, sems.at[4 + p], sems.at[6 + p], across(route(n)[2]))

    def halo_ends(n, p):
        dr = DIRS[n][0]
        src = obj.at[p, edge(dr, TH), strips[2]]
        return src, framed.at[p, margin(-dr, TH), shifted(strips[2])], halo_relay, halo_hop

    def grad_ends(n, p):
        dr = DIRS[n][0]
        src = canvas.at[p, margin(dr, TH), shifted(strips[2])]
        return src, rx_v.at[(dr + 1) // 2, p, :, strips[2]], grad_relay, grad_hop

    def first_leg(n, p, ends):
        src, dst, buf, sems = ends(n, p)
        return leg_one(n, p, src, buf, sems)

    def second_leg(n, p, ends):
        src, dst, buf, sems = ends(n, p)
        return leg_two(n, p, dst, buf, sems)

    def whole(n, ends):
        src, dst, buf, sems = ends(n, 1)
        return remote(src, dst, sems.at[1], sems.at[3], near(DIRS[n][0], 0))

    def start_legs(ends):
        for n in vertical:

            @pl.when(row == route(n)[0])
            def _():
                first_leg(n, 0, ends).start()
                whole(n, ends).start()

    def start_middle(direct):
        for n in vertical:

            @pl.when(exists(DIRS[n]) & (row != route(n)[0]))
            def _():
                direct(n, 2).start()

    def relay_middle(p, ends):
        for n in vertical:

            @pl.when(row == route(n)[1])
            def _():
                first_leg(n, p, ends).wait_recv()
                second_leg(n, p, ends).start()

    def arrive_middle(direct, ends):
        for n in vertical:

            @pl.when(row == route(n)[0])
            def _():
                first_leg(n, 0, ends).wait_send()
                whole(n, ends).wait_send()

            @pl.when(exists(DIRS[n]) & (row != route(n)[0]))
            def _():
                direct(n, 2).wait_send()

            @pl.when(row == route(n)[1])
            def _():
                second_leg(n, 0, ends).wait_send()

            @pl.when(row == route(n)[2])
            def _():
                second_leg(n, 0, ends).wait_recv()
                whole(n, ends).wait_recv()

            @pl.when(exists(DIRS[opposite(n)]) & (row != route(n)[2]))
            def _():
                direct(n, 2).wait_recv()

    def do_halo_send():
        start(halo_v, vertical, 0)
        start(halo_v, vertical, 1)
        for n in diagonal:

            @pl.when(direct_from(n))
            def _():
                halo_d(n).start()

        start(halo_h, level)

    def do_halo_middle():
        start_legs(halo_ends)
        start_middle(halo_v)

    def halo_d(n):
        dr, dc = DIRS[n]
        return remote(
            obj.at[:, edge(dr, TH), edge(dc, TW)],
            framed.at[:, margin(-dr, TH), margin(-dc, TW)],
            halo_send.at[8 + n],
            halo_recv.at[8 + n],
            near(dr, dc),
        )

    def leaves(dc):
        return core == (1 if dc > 0 else 0)

    def direct_from(n):
        return (row == (2 if DIRS[n][0] > 0 else 5)) & exists((0, DIRS[n][1])) & leaves(DIRS[n][1])

    def direct_to(n):
        dr, dc = DIRS[n]
        return (row == (3 if dr > 0 else 4)) & exists((0, -dc)) & leaves(-dc)

    def handed_from(n):
        dr, dc = DIRS[n]
        apart = (row == (3 if dr > 0 else 4)) & leaves(dc)
        return exists((-dr, dc)) & jnp.logical_not(apart)

    def handed_to(n):
        dr, dc = DIRS[n]
        return exists((-dr, -dc)) & jnp.logical_not(direct_to(n))

    def do_halo_forward():
        arrive(halo_v, vertical, 0)
        arrive(halo_v, vertical, 1)
        for n in diagonal:

            @pl.when(handed_from(n))
            def _():
                halo_c(n).start()

    def do_halo_relay(p):
        relay_middle(p, halo_ends)

    def do_halo_wait():
        arrive(halo_h, level)
        arrive_middle(halo_v, halo_ends)
        for n in diagonal:

            @pl.when(handed_from(n))
            def _():
                halo_c(n).wait_send()

            @pl.when(handed_to(n))
            def _():
                halo_c(n).wait_recv()

            @pl.when(direct_from(n))
            def _():
                halo_d(n).wait_send()

            @pl.when(direct_to(n))
            def _():
                halo_d(n).wait_recv()

    def do_local():
        for copy in local[1:5]:
            copy.start()

    def do_margins():
        for n in range(OWN):
            dr, dc = DIRS[n]

            @pl.when(jnp.logical_not(exists(DIRS[n])))
            def _():
                rows, cols = margin(dr, TH), margin(dc, TW)
                framed[:, rows, cols] = jnp.zeros((2, rows.size, cols.size), jnp.float32)
                cnt[n, 0, 0] = 0
                for k in range(PAT):
                    pos[n, 0, k] = 0
                    pos[n, 1, k] = 0

        for n in vertical:

            @pl.when(jnp.logical_not(exists(DIRS[n])))
            def _():
                rx_v[1 - n] = jnp.zeros((2, HALF, TW), jnp.float32)

        for n in level:

            @pl.when(jnp.logical_not(exists(DIRS[n])))
            def _():
                rx_h[3 - n] = jnp.zeros((2, TH + 2 * HALF, HALF), jnp.float32)

        framed[:, TH + 2 * HALF :, :] = jnp.zeros((2, TILE, TW + 3 * HALF), jnp.float32)
        framed[:, : TH + 2 * HALF, TW + 2 * HALF :] = jnp.zeros(
            (2, TH + 2 * HALF, HALF), jnp.float32
        )

    def clear(i, carry):
        at = pl.ds(pl.multiple_of(i * 32, 32), 32)
        for k in range(PAT):
            for p in range(2):
                padded[k, p, at, :] = jnp.zeros((32, 640), jnp.float32)
        return carry

    def do_clear():
        lax.fori_loop(0, 24, clear, 0)

    def do_probe_in():
        local[0].wait()

    def do_meas_in():
        for copy in local[1:5]:
            copy.wait()

    def do_place_in():
        for copy in local[5:]:
            copy.wait()
        arrive(place_copy, range(OWN))
        arrive(count_copy, range(OWN))

    lives, tops, lefts, downs, overs = [], [], [], [], []

    def do_places():
        for k in range(PAT):
            a = lax.max(lax.min(pos[OWN, 0, k] - (row * TH - HALF), TH), 0)
            b = lax.max(lax.min(pos[OWN, 1, k] - (col * TW - HALF), TW), 0)
            lives.append(jnp.where(k < cnt[OWN, 0, 0], 1.0, 0.0).astype(jnp.float32))
            tops.append(lax.div(a, TILE))
            downs.append(lax.rem(a, TILE))
            lefts.append(lax.div(b, 128))
            overs.append(lax.rem(b, 128))

    def lane_iota(shape):
        return lax.broadcasted_iota(jnp.int32, shape, len(shape) - 1)

    def sub_iota(shape):
        return lax.broadcasted_iota(jnp.int32, shape, len(shape) - 2)

    def window(p, k, first, tiles):
        s, r = downs[k], overs[k]
        rows = pl.ds((tops[k] + first) * TILE, (tiles + 1) * TILE)
        turned = []
        for j in range(3):
            cols = pl.ds((lefts[k] + j) * 128, 128)
            turned.append(pltpu.roll(framed[p, rows, cols], lax.rem(128 - r, 128), 1))
        near = lane_iota(turned[0].shape) < 128 - r
        found = []
        for j in range(2):
            both = jnp.where(near, turned[j], turned[j + 1]).reshape(tiles + 1, TILE, 128)
            both = pltpu.roll(both, lax.rem(TILE - s, TILE), 1)
            upper = sub_iota((tiles, TILE, 128)) < TILE - s
            found.append(
                jnp.where(upper, both[:tiles], both[1:]).reshape(tiles * TILE, 128)
            )
        return found

    def lay(k, p, tiles, s, r):
        moved = []
        for x in tiles:
            x = pltpu.roll(x.reshape(N // TILE, TILE, 128), s, 1)
            none = jnp.zeros((1, TILE, 128), jnp.float32)
            here = jnp.concatenate([x, none], axis=0)
            above = jnp.concatenate([none, x], axis=0)
            y = jnp.where(sub_iota(here.shape) >= s, here, above).reshape(N + TILE, 128)
            moved.append(pltpu.roll(y, r, 1))
        right = lane_iota((N + TILE, 128)) >= r
        rows = pl.ds(N, N + TILE)
        padded[k, p, rows, pl.ds(128, 128)] = jnp.where(right, moved[0], 0.0)
        padded[k, p, rows, pl.ds(256, 128)] = jnp.where(right, moved[1], moved[0])
        padded[k, p, rows, pl.ds(384, 128)] = jnp.where(right, 0.0, moved[1])

    def collect(start, stop, pairs):
        size = 8

        def one(i, carry):
            first = i * size
            rows = pl.ds(pl.multiple_of(first * TILE, size * TILE), size * TILE)
            for q, p in pairs:
                for j in range(6):
                    total = None
                    for k in range(PAT):
                        at = (first - tops[k] + N // TILE) * TILE
                        lane = lax.max(lax.min(j - lefts[k] + 1, 4), 0) * 128
                        part = padded[
                            k, p, pl.ds(at, size * TILE), pl.ds(lane, 128)
                        ]
                        total = part if total is None else total + part
                    canvas[q, rows, pl.ds(j * 128, 128)] = total
            return carry

        lax.fori_loop(start // size, stop // size, one, 0, unroll=True)

    def do_power():
        for j in range(2):
            cols = pl.ds(128 * j, 128)
            power[j] = probe[0, :, cols] * probe[0, :, cols] + probe[1, :, cols] * probe[1, :, cols]
        ill[...] = jnp.zeros((TH, TW), jnp.float32)

    def light(t, carry):
        high, left = [], []
        for k in range(PAT):
            alive = jnp.where(k < cnt[t, 0, 0], 1.0, 0.0).astype(jnp.float32)
            a = lax.max(lax.min(pos[t, 0, k] - row * TH, 384), -384) + 384
            b = lax.max(lax.min(pos[t, 1, k] - col * TW, 896), -640) + 640
            lay(k, 0, [alive * power[j] for j in range(2)], lax.rem(a, TILE), lax.rem(b, 128))
            high.append(lax.div(a, TILE) - 80)
            left.append(lax.div(b, 128) - 5)
        size = 8
        for i in range(0, TH // TILE, size):
            rows = pl.ds(i * TILE, size * TILE)
            for j in range(4):
                total = ill[rows, pl.ds(j * 128, 128)]
                for k in range(PAT):
                    at = lax.max(lax.min(i - high[k], 96 - size), 0) * TILE
                    lane = lax.max(lax.min(j - left[k] + 1, 4), 0) * 128
                    total = total + padded[k, 0, pl.ds(at, size * TILE), pl.ds(lane, 128)]
                ill[rows, pl.ds(j * 128, 128)] = total
        return carry

    def do_light():
        lax.fori_loop(0, len(DIRS) + 1, light, 0)

    def do_peak():
        def largest(i, most):
            rows = pl.ds(pl.multiple_of(i * 32, 32), 32)
            for j in range(4):
                value = ill[rows, pl.ds(128 * j, 128)]
                most = jnp.maximum(most, jnp.max(value.reshape(4, TILE, 128), axis=0))
            return most

        peak = lax.fori_loop(0, TH // 32, largest, jnp.zeros((TILE, 128), jnp.float32))
        for c in range(CORES):
            w1[c, N:, :] = peak

    def do_turn():
        for k in range(PAT):
            meas_t[k] = meas[k].T

    def cut(i, carry):
        tiles = 4
        rows = pl.ds(pl.multiple_of(i * tiles * TILE, tiles * TILE), tiles * TILE)
        weight = [jnp.zeros((tiles * TILE, 128), jnp.float32)] * 2
        for k in range(PAT):
            real = window(0, k, i * tiles, tiles)
            imag = window(1, k, i * tiles, tiles)
            for j in range(2):
                cols = pl.ds(128 * j, 128)
                p_re, p_im = probe[0, rows, cols], probe[1, rows, cols]
                patches[k, 0, rows, cols] = real[j]
                patches[k, 1, rows, cols] = imag[j]
                exits[k, rows, cols] = (p_re * real[j] - p_im * imag[j]).astype(jnp.bfloat16)
                exits[k, rows, pl.ds(N + 128 * j, 128)] = (
                    p_re * imag[j] + p_im * real[j]
                ).astype(jnp.bfloat16)
                weight[j] = weight[j] + lives[k] * (real[j] * real[j] + imag[j] * imag[j])
        for j in range(2):
            w1[j, rows, :] = weight[j]
        return carry

    def do_cut():
        lax.fori_loop(0, 8, cut, 0, unroll=True)

    def dot(a, b):
        return jnp.dot(a, b, preferred_element_type=jnp.float32)

    def do_transforms(first, last):
        these = range(first, last)
        for k in these:
            for h in range(2):
                rows = pl.ds(h * HALF, HALF)
                half = dot(exits[k, rows, :], fwd[...]).astype(jnp.bfloat16)
                halves[k, rows, :] = half[:, :N]
                halves[k, pl.ds(N + h * HALF, HALF), :] = half[:, N:]
        for k in these:
            for h in range(2):
                cols = pl.ds(h * HALF, HALF)
                upper, lower = pl.ds(h * HALF, HALF), pl.ds(N + h * HALF, HALF)
                re = dot(inv[upper, :], halves[k])
                im = dot(inv[lower, :], halves[k])
                factor = lives[k] * (1.0 - meas_t[k, upper, :] * lax.rsqrt(re * re + im * im + 0.25))
                residues[k, upper, :] = (factor * re).astype(jnp.bfloat16)
                residues[k, lower, :] = (factor * im).astype(jnp.bfloat16)
        for k in these:
            for h in range(2):
                upper, lower = pl.ds(h * HALF, HALF), pl.ds(N + h * HALF, HALF)
                backs[k, upper, :N] = dot(fwd[upper, :], residues[k]).astype(jnp.bfloat16)
                backs[k, upper, N:] = dot(fwd[lower, :], residues[k]).astype(jnp.bfloat16)
        for k in these:
            for h in range(2):
                rows = pl.ds(h * HALF, HALF)
                wave[k, rows, :] = dot(backs[k, rows, :], inv[...])

    def do_probe_sum():
        size = 32
        for i in range(N // size):
            rows = pl.ds(i * size, size)
            for j in range(2):
                cols = pl.ds(128 * j, 128)
                real = imag = None
                for k in range(PAT):
                    a, b = patches[k, 0, rows, cols], patches[k, 1, rows, cols]
                    u, v = wave[k, rows, cols], wave[k, rows, pl.ds(N + 128 * j, 128)]
                    one, two = a * u + b * v, a * v - b * u
                    real = one if real is None else real + one
                    imag = two if imag is None else imag + two
                part = pl.ds((i % 2) * size, size)
                g1[j, i // 2, part, :] = real
                g1[j, ZS // 2 + i // 2, part, :] = imag

    def owned(p, rows, at, h, j):
        size = rows.size
        inner = pl.ds(pl.multiple_of(HALF + h * HALF + at, 8), size)
        value = canvas[p, inner, pl.ds(128 * (j + 1), 128)]
        value = value + rx_v[1 - h, p, pl.ds(at, size), pl.ds(128 * j, 128)]
        if j in (0, 3):
            value = value + rx_h[1 if j == 0 else 0, p, inner, :]
        return value

    size = 32

    def send(src, dst, sem, peer):
        return remote(src, dst, red_send.at[sem], red_recv.at[sem], peer)

    def ahead(d):
        return lax.rem(z_at + d, ZS)

    def behind(d):
        return lax.rem(z_at + ZS - d, ZS)

    def w_core():
        return send(w1.at[1 - core], rxw1, 0, core_peer())

    def w_y(e):
        to = lax.rem(y_at + e, YS)
        return send(w2.at[to], rxw2.at[e - 1], e, y_peer(to))

    def g_core(d):
        return send(g1.at[1 - core, ahead(d)], rxg1.at[ahead(d)], 4 + d, core_peer())

    def g_y(d, e):
        to = lax.rem(y_at + e, YS)
        return send(g2.at[ahead(d), to], rxg2.at[e - 1, ahead(d)], 11 + 3 * d + e, y_peer(to))

    def z_copy(d):
        return send(s3.at[ahead(d)], rx3.at[d - 1], 35 + d, z_peer(ahead(d)))

    def x_copy(d):
        to = lax.rem(x_at + d, XS)
        return send(rx4.at[x_at], rx4.at[x_at], 42 + d, x_peer(to))

    def do_w_core_send():
        w_core().start()

    def do_w_core_sum():
        w_core().wait()
        part = N // YS
        crown = jnp.maximum(w1[core, N:, :], rxw1[N:, :])
        total = (w1[core, :N, :] + rxw1[:N, :]).reshape(ZS, YS, TILE, 128)
        for i in range(YS):
            w2[i, :part, :] = total[:, i].reshape(part, 128)
            w2[i, part:, :] = crown

    def do_w_y_send():
        for d in range(1, YS):
            w_y(d).start()

    def do_w_y_sum():
        for d in range(1, YS):
            w_y(d).wait()
        part = N // YS
        crown = w2[y_at, part:, :]
        for d in range(YS - 1):
            crown = jnp.maximum(crown, rxw2[d, part:, :])
        size = CHUNK - GCHUNK
        for i in range(ZS):
            at = pl.ds(i * size, size)
            s3[i, GCHUNK:CHUNK, :] = (w2[y_at, at, :] + rxw2[0, at, :]) + (
                rxw2[1, at, :] + rxw2[2, at, :]
            )
            s3[i, CHUNK:, :] = crown

    def do_core_send():
        for d in FAR:
            g_core(d).start()

    def do_core_sum():
        for d in FAR:
            g_core(d).wait()
            at = ahead(d)
            g2[at] = (g1[core, at] + rxg1[at]).reshape(YS, GCHUNK, 128)
            for e in range(1, YS):
                g_y(d, e).start()

    def do_y_sum():
        for d in FAR:
            for e in range(1, YS):
                g_y(d, e).wait()
            at = ahead(d)
            s3[at, :GCHUNK, :] = (g2[at, y_at] + rxg2[0, at]) + (rxg2[1, at] + rxg2[2, at])
            if d:
                z_copy(d).start()

    def do_z_sum():
        total = s3[z_at, :CHUNK, :]
        crown = s3[z_at, CHUNK:, :]
        for d in NEAR:
            z_copy(d).wait()
            total = total + rx3[d - 1, :CHUNK, :]
            crown = jnp.maximum(crown, rx3[d - 1, CHUNK:, :])
        rx4[x_at, :CHUNK, :] = total
        rx4[x_at, CHUNK:, :] = crown

    def do_x_send():
        for d in range(1, XS):
            x_copy(d).start()

    def do_x_sum():
        for d in range(1, XS):
            x_copy(d).wait()
        gathered[core, z_at, y_at] = (rx4[0, :CHUNK, :] + rx4[1, :CHUNK, :]) + (
            rx4[2, :CHUNK, :] + rx4[3, :CHUNK, :]
        )

    def z_back(d):
        mine = gathered.at[core, z_at, y_at]
        return send(mine, mine, 45 + d, z_peer(ahead(d)))

    def y_back(d, e):
        mine = gathered.at[core, behind(d), y_at]
        return send(mine, mine, 52 + 3 * d + e, y_peer(lax.rem(y_at + e, YS)))

    def core_back(d):
        mine = gathered.at[core, behind(d)]
        return send(mine, mine, 77 + d, core_peer())

    def do_z_back():
        for d in NEAR[::-1]:
            z_back(d).start()
        for e in range(1, YS):
            y_back(0, e).start()

    def do_y_back():
        for d in NEAR:
            z_back(d).wait()
            for e in range(1, YS):
                y_back(d, e).start()

    def do_core_back():
        for d in (0,) + NEAR:
            for e in range(1, YS):
                y_back(d, e).wait()
            core_back(d).start()

    def do_core_wait():
        for d in (0,) + NEAR:
            core_back(d).wait()

    def do_lay():
        for k in range(PAT):
            parts = ([], [])
            for j in range(2):
                cols = pl.ds(128 * j, 128)
                u, v = wave[k, :, cols], wave[k, :, pl.ds(N + 128 * j, 128)]
                p_re, p_im = probe[0, :, cols], probe[1, :, cols]
                parts[0].append(p_re * u + p_im * v)
                parts[1].append(p_re * v - p_im * u)
            for p in range(2):
                lay(k, p, parts[p], downs[k], overs[k])

    def do_collect(first, last):
        collect(first, last, [(0, 0), (1, 1)])

    def do_grad_corner():
        for n in diagonal:
            start_level(n)

    def do_grad_middle():
        start_middle(grad_v)

    def do_grad_legs():
        start_legs(grad_ends)

    def do_grad_relay(p):
        relay_middle(p, grad_ends)

    def do_grad_level():
        for n in level:
            start_level(n)

    def do_grad_forward():
        for n in diagonal:
            arrive_level(n)
        for dr in (-1, 1):
            rows = margin(dr, TH)
            for dc in (-1, 1):
                cols = shifted(edge(dc, TW))
                canvas[:, rows, cols] = canvas[:, rows, cols] + rx_h[(1 - dc) // 2, :, rows, :]
        start(grad_v, vertical, 0)
        start(grad_v, vertical, 1)

    def do_grad_wait():
        for n in level:
            arrive_level(n)
        for part in range(2):
            arrive(grad_v, vertical, part)
        arrive_middle(grad_v, grad_ends)

    def do_object():
        crown = jnp.maximum(
            jnp.maximum(rx4[0, CHUNK:, :], rx4[1, CHUNK:, :]),
            jnp.maximum(rx4[2, CHUNK:, :], rx4[3, CHUNK:, :]),
        )
        top = jnp.max(crown)
        for h in range(2):

            def renew(i, carry, h=h):
                at = pl.multiple_of(i * size, size)
                rows = pl.ds(pl.multiple_of(h * HALF + at, size), size)
                inner = pl.ds(pl.multiple_of(HALF + h * HALF + at, 8), size)
                for j in range(4):
                    cols = pl.ds(128 * (j + 1), 128)
                    share = 1.0 / (0.75 * ill[rows, pl.ds(128 * j, 128)] + 0.25 * top)
                    for p in range(2):
                        obj_new[p, rows, pl.ds(128 * j, 128)] = (
                            framed[p, inner, cols] - owned(p, rows, at, h, j) * share
                        )
                return carry

            lax.fori_loop(0, HALF // size, renew, 0, unroll=True)

    def do_probe():
        weight = [gathered[j, :, :, GCHUNK:, :].reshape(N, 128) for j in range(2)]
        heavy = jnp.maximum(jnp.max(weight[0]), jnp.max(weight[1]))
        for j in range(2):
            cols = pl.ds(128 * j, 128)
            share = 1.0 / (0.75 * weight[j] + 0.25 * heavy)
            for p in range(2):
                half = ZS // 2
                total = gathered[j, half * p : half * (p + 1), :, :GCHUNK, :].reshape(N, 128)
                probe_new[p, :, cols] = probe[p, :, cols] - total * share

    do_barrier()
    do_place_send()
    do_halo_send()
    do_halo_middle()
    do_local()
    do_margins()
    do_clear()
    do_probe_in()
    do_power()
    do_place_in()
    do_places()
    do_light()
    do_halo_forward()
    do_halo_relay(0)
    do_peak()
    do_meas_in()
    do_turn()
    do_halo_wait()
    do_cut()
    do_w_core_send()
    do_transforms(0, 2)
    do_w_core_sum()
    do_w_y_send()
    do_transforms(2, 4)
    do_probe_sum()
    do_core_send()
    do_lay()
    do_w_y_sum()
    do_core_sum()
    do_collect(0, 64)
    do_grad_legs()
    do_grad_middle()
    do_grad_corner()
    do_y_sum()
    do_grad_relay(0)
    do_z_sum()
    do_x_send()
    do_grad_forward()
    do_x_sum()
    do_z_back()
    do_grad_level()
    do_y_back()
    do_core_back()
    do_grad_wait()
    do_object()
    do_core_wait()
    do_probe()


def body(object_field, probe, measured, positions, counts):
    forward, inverse = tables(N)
    any_space = pl.BlockSpec(memory_space=pl.ANY)
    vmem = pl.BlockSpec(memory_space=pltpu.VMEM)
    f32 = jnp.float32
    bf16 = jnp.bfloat16
    red = 85
    dma = pltpu.SemaphoreType.DMA
    return pl.pallas_call(
        kernel,
        out_shape=(pltpu.VMEM((2, TH, TW), f32), pltpu.VMEM((2, N, N), f32)),
        in_specs=[any_space] * 7,
        out_specs=(vmem, vmem),
        scratch_shapes=[
            pltpu.SMEM((OWN + 1, 2, PAT), jnp.int32),
            pltpu.SMEM((OWN + 1, 1, 1), jnp.int32),
            pltpu.VMEM((2, TH + 2 * HALF + TILE, TW + 3 * HALF), f32),
            pltpu.VMEM((2, N, N), f32),
            pltpu.VMEM((2, N, 128), f32),
            pltpu.VMEM((TH, TW), f32),
            pltpu.VMEM((PAT, N, N), f32),
            pltpu.VMEM((PAT, N, N), f32),
            pltpu.VMEM((2 * N, 2 * N), bf16),
            pltpu.VMEM((2 * N, 2 * N), bf16),
            pltpu.VMEM((PAT, 2, 3 * N, 640), f32),
            pltpu.VMEM((2, TH + 2 * HALF, TW + 2 * HALF), f32),
            pltpu.VMEM((2, 2, HALF, TW), f32),
            pltpu.VMEM((2, 2, TH + 2 * HALF, HALF), f32),
            pltpu.VMEM((PAT, 2, N, N), f32),
            pltpu.VMEM((PAT, N, 2 * N), f32),
            pltpu.VMEM((PAT, N, 2 * N), bf16),
            pltpu.VMEM((PAT, 2 * N, N), bf16),
            pltpu.VMEM((PAT, 2 * N, N), bf16),
            pltpu.VMEM((PAT, N, 2 * N), bf16),
            pltpu.VMEM((CORES, N + TILE, 128), f32),
            pltpu.VMEM((N + TILE, 128), f32),
            pltpu.VMEM((XS, N // XS + TILE, 128), f32),
            pltpu.VMEM((XS - 1, N // XS + TILE, 128), f32),
            pltpu.VMEM((CORES, ZS, 2 * N // ZS, 128), f32),
            pltpu.VMEM((ZS, 2 * N // ZS, 128), f32),
            pltpu.VMEM((ZS, XS, GCHUNK, 128), f32),
            pltpu.VMEM((XS - 1, ZS, GCHUNK, 128), f32),
            pltpu.VMEM((ZS, CHUNK + TILE, 128), f32),
            pltpu.VMEM((ZS - 1, CHUNK + TILE, 128), f32),
            pltpu.VMEM((YS, CHUNK + TILE, 128), f32),
            pltpu.VMEM((CORES, ZS, XS, CHUNK, 128), f32),
            dma((7,)),
            dma((OWN,)),
            dma((OWN,)),
            dma((OWN,)),
            dma((OWN,)),
            pltpu.VMEM((2, HALF, TW - 2 * HALF), f32),
            pltpu.VMEM((2, HALF, TW - 2 * HALF), f32),
            dma((8,)),
            dma((8,)),
            dma((16,)),
            dma((16,)),
            dma((12,)),
            dma((12,)),
            dma((red,)),
            dma((red,)),
        ],
        compiler_params=pltpu.CompilerParams(
            collective_id=0, has_side_effects=True, vmem_limit_bytes=56 * 1024 * 1024
        ),
    )(
        positions.reshape(PAT, 2).T,
        counts,
        object_field,
        probe,
        measured.reshape(PAT, N, N),
        jnp.asarray(forward),
        jnp.asarray(inverse),
    )


def solution(mesh):
    in_specs = (
        P(None, "row", "col"),
        P(),
        P("row", "col", None, None, None),
        P("row", "col", None, None),
        P("row", "col"),
    )
    out_specs = (P(None, "row", "col"), P())
    return jax.shard_map(body, mesh=mesh, in_specs=in_specs, out_specs=out_specs, check_vma=False)
```
